32 devices in a mesh: groups: 2 (over y), space: 8 (over z, x), dp: 2 (over core).
Axes of the slice: x: 2, y: 2, z: 4, core: 2. Of those that a mesh axis runs over, the one named last changes fastest.
Arguments:
- features: bfloat16 [4, 16, 8, 8, 512], P(('groups', 'dp'), 'space'), parts along dimension 0, may hold values from -6 to 6
- cotangent: bfloat16 [4, 16, 8, 8, 512], P(('groups', 'dp'), 'space'), parts along dimension 0, may hold values from -6 to 6
- kernel: bfloat16 [3, 3, 3, 64, 64], replicated, may hold values from -0.15625 to 0.15625
- neighbours: int32 [4, 16, 6], P(('groups', 'dp'), 'space'), parts along dimension 0, may hold values from -1 to 15, as said below
Outputs:
- response: bfloat16 [4, 16, 8, 8, 512], P(('groups', 'dp'), 'space'), parts along dimension 0
- feature_grad: bfloat16 [4, 16, 8, 8, 512], P(('groups', 'dp'), 'space'), parts along dimension 0
- kernel_grad: float32 [6, 3, 3, 64, 64], P('groups'), parts along dimension 0
The draws below stay inside these ranges and needn't reach their ends.
There are 2 independent parts, one for each index of `groups`. The reference program is written for one: setup_inputs(seed, part) draws one part's arguments, and reference() takes and returns one part's arrays. A program takes and returns all parts, laid end to end along the dimension named above; an argument that names none is the same for every part. Nothing has to cross between parts.
Inputs may be any that keep to these rules, and one draw needn't show every extreme that they name: `neighbours`: the active bricks lie on a lattice of 3 by 8 by 4 bricks. Tile t sits at position p = t + 2: it covers lattice row p // 4 of the first dimension, rows 2 * (p % 4) to 2 * (p % 4) + 1 of the second and all rows of the third; it holds exactly 2 active bricks, in slots 2 * t to 2 * t + 1, listed by second then third lattice coordinate. In each realization one third-dimension row z is drawn, and every tile holds the bricks at z in its first and in its last second-dimension row; its other bricks are drawn at random. Directions are first dimension down, up, second down, up, third down, up; the relation is symmetric (if brick u is the up neighbour of s, s is the down neighbour of u), and -1 marks a neighbour that is inactive or outside the lattice.
All inputs are finite; a program needn't handle non-finite values.
Results may differ from the reference program's by a relative error of at most 0.0045.
Values may be sent and summed in bfloat16 or wider, within the bound.
A program may use at most 64 MiB of HBM per device.

```python
import math
import jax
import jax.numpy as jnp
from jax import lax

CHANNELS = 64
BRICK = 8
DEPTH_BRICKS = 4
TILES_Y = 4
BRICKS_DEV = 2
BRICKS = 16
REALIZATIONS = 2


def draw_neighbours(key, part):
    tile_count = BRICKS // BRICKS_DEV
    lattice_x = tile_count // TILES_Y + 1
    lattice_y = TILES_Y * BRICKS_DEV
    places = DEPTH_BRICKS * BRICKS_DEV
    keys_all = jax.random.split(key, REALIZATIONS * tile_count)
    spine_depth = jax.random.randint(jax.random.fold_in(key, 7), (REALIZATIONS,), 0, DEPTH_BRICKS).astype(jnp.int32)
    spine_all = jnp.repeat(spine_depth, tile_count)
    place_ids = jnp.arange(places, dtype=jnp.int32)

    def choose(sub_key, spine_z):
        priority = jax.random.permutation(sub_key, places).astype(jnp.int32)
        first_spine = spine_z
        last_spine = (BRICKS_DEV - 1) * DEPTH_BRICKS + spine_z
        forced = (place_ids == first_spine) | (place_ids == last_spine)
        priority = jnp.where(forced, -1, priority)
        order = jnp.argsort(priority, stable=True).astype(jnp.int32)
        return jnp.sort(order[:BRICKS_DEV])
    chosen = jax.vmap(choose)(keys_all, spine_all).reshape(REALIZATIONS, tile_count, BRICKS_DEV).astype(jnp.int32)
    tile_ids = jnp.arange(tile_count, dtype=jnp.int32)
    placed = tile_ids + TILES_Y // 2
    coord_x = jnp.broadcast_to((placed // TILES_Y)[None, :, None], chosen.shape)
    coord_y = (placed % TILES_Y * BRICKS_DEV)[None, :, None] + chosen // DEPTH_BRICKS
    coord_z = chosen % DEPTH_BRICKS
    slot_grid = jnp.broadcast_to(jnp.arange(BRICKS, dtype=jnp.int32).reshape(1, tile_count, BRICKS_DEV), chosen.shape)
    cells_total = lattice_x * lattice_y * DEPTH_BRICKS

    def linear(along_x, along_y, along_z):
        return (along_x * lattice_y + along_y) * DEPTH_BRICKS + along_z

    def per_realization(first_c, second_c, third_c, slot_part):
        table = jnp.full((cells_total,), -1, jnp.int32).at[linear(first_c, second_c, third_c).ravel()].set(slot_part.ravel())
        columns = []
        for step_x, step_y, step_z in ((-1, 0, 0), (1, 0, 0), (0, -1, 0), (0, 1, 0), (0, 0, -1), (0, 0, 1)):
            near_x = first_c + step_x
            near_y = second_c + step_y
            near_z = third_c + step_z
            inside = (near_x >= 0) & (near_x < lattice_x) & (near_y >= 0) & (near_y < lattice_y) & (near_z >= 0) & (near_z < DEPTH_BRICKS)
            found = table[jnp.where(inside, linear(near_x, near_y, near_z), 0)]
            columns.append(jnp.where(inside, found, -1).ravel())
        return jnp.stack(columns, axis=-1)
    return jax.vmap(per_realization)(coord_x, coord_y, coord_z, slot_grid).astype(jnp.int32)


def level_of(key, extent, cuts, smallest, top_value):
    factor_of, own = 1.0, jax.random.fold_in(key, 6)
    for position, parts in cuts:
        draws = jnp.exp(jax.random.uniform(jax.random.fold_in(own, position), (parts,), jnp.float32, smallest / len(cuts), top_value / len(cuts)))
        factor_of = factor_of * jnp.repeat(draws, extent[position] // parts).reshape([-1 if axis == position else 1 for axis in range(len(extent))])
    return factor_of


def gaussian(own_key, shape, width, most, pieces=(), kind=jnp.bfloat16):
    entries = width * jax.random.normal(own_key, shape, jnp.float32)
    if pieces:
        entries = entries * level_of(own_key, shape, pieces, -0.22, 0.18)
    return jnp.clip(entries, -most, most).astype(kind)


def setup_inputs(seed: int = 0, part: int = 0) -> dict:
    arg_keys = jax.random.split(jax.random.key(seed), 5)
    part_keys = jax.random.split(jax.random.fold_in(arg_keys[4], part), 5)
    return {
        "features": gaussian(part_keys[0], (REALIZATIONS, BRICKS, BRICK, BRICK, BRICK * CHANNELS), 1.0, 6.0, ((0, 2), (1, 8))),
        "cotangent": gaussian(part_keys[1], (REALIZATIONS, BRICKS, BRICK, BRICK, BRICK * CHANNELS), 1.0, 6.0, ((0, 2), (1, 8))),
        "kernel": gaussian(arg_keys[2], (3, 3, 3, CHANNELS, CHANNELS), (27 * CHANNELS) ** -0.5, 0.15625),
        "neighbours": draw_neighbours(jax.random.fold_in(jax.random.fold_in(arg_keys[4], part), 71), part),
    }


def pick_rows(values, slots):
    present = slots >= 0
    picked = jnp.take(values, jnp.where(present, slots, 0).astype(jnp.int32), axis=0)
    shape_tail = (1,) * (values.ndim - 1)
    return jnp.where(present.reshape((-1,) + shape_tail), picked, jnp.zeros_like(picked))

def extend(volume, slots):
    for axis_dim, columns in zip((1, 2, 3), ((0, 1), (2, 3), (4, 5))):
        length = volume.shape[axis_dim]
        upper_face = lax.slice_in_dim(volume, length - 1, length, axis=axis_dim)
        lower_face = lax.slice_in_dim(volume, 0, 1, axis=axis_dim)
        below = pick_rows(upper_face, slots[:, columns[0]])
        above = pick_rows(lower_face, slots[:, columns[1]])
        volume = jnp.concatenate([below, volume, above], axis=axis_dim)
    return volume

def reference(features, cotangent, kernel, neighbours):
    kernel_wide = kernel.astype(jnp.float32)

    def single(inputs):
        volume_in, cotangent_in, slots = inputs
        volume_wide = volume_in.reshape(BRICKS, BRICK, BRICK, BRICK, CHANNELS).astype(jnp.float32)
        seed_grad = cotangent_in.reshape(BRICKS, BRICK, BRICK, BRICK, CHANNELS).astype(jnp.float32)

        def forward(volume, weights):
            return lax.conv_general_dilated(extend(volume, slots), weights, (1, 1, 1), 'VALID', dimension_numbers=('NDHWC', 'DHWIO', 'NDHWC'), precision=lax.Precision.HIGHEST)
        output, pullback = jax.vjp(forward, volume_wide, kernel_wide)
        volume_grad, weight_grad = pullback(seed_grad)
        shaped = (BRICKS, BRICK, BRICK, BRICK * CHANNELS)
        return (output.astype(jnp.bfloat16).reshape(shaped), volume_grad.astype(jnp.bfloat16).reshape(shaped), weight_grad)
    response, feature_grad, weight_parts = lax.map(single, (features, cotangent, neighbours))
    scale_factor = 1.0 / math.sqrt(REALIZATIONS * BRICKS * BRICK ** 3)
    kernel_grad = lax.optimization_barrier(jnp.sum(weight_parts, axis=0)) * scale_factor
    return (response, feature_grad, kernel_grad)
```

```python
import functools
import math

import jax
import jax.numpy as jnp
from jax import lax
from jax.experimental import pallas as pl
from jax.experimental.pallas import tpu as pltpu
from jax.sharding import PartitionSpec as P

TILES_Y = 4
EDGE = 8
CH = 64
PAIR = 2 * CH
PAIRS = EDGE // 2
ROWS = EDGE * CH
WIDE = ROWS + PAIR
TILES = 14
OWNED = TILES // 2
MESH = pl.DeviceIdType.MESH
DIAGONALS = [(side, dx) for side in range(2) for dx in range(3)]


def low_lanes(shape):
    return lax.broadcasted_iota(jnp.int32, shape, len(shape) - 1) < CH


def in_range(tile, count):
    return (tile >= 0) & (tile < count)


def receives(tile, dx, dy, count, first_x):
    column = (tile + TILES_Y // 2) % TILES_Y + dy
    there = in_range(tile + TILES_Y * dx + dy, count) & (column >= 0) & (column < TILES_Y)
    between = tile + TILES_Y * dx if first_x else tile + dy
    return in_range(tile, count) & in_range(between, count) & there


def place_windows(store, center, edge):
    low = low_lanes((center.shape[0], PAIR))
    pairs = [center[:, PAIR * k : PAIR * (k + 1)] for k in range(PAIRS)]
    for k in range(PAIRS):
        after = pairs[k + 1] if k + 1 < PAIRS else edge
        before = pairs[k - 1] if k > 0 else edge
        store(k, jnp.where(low, after, before), pairs[k])


def build_windows(out_ref, center, edge, halo_low, halo_high, edge_low, edge_high):
    planes = center.shape[0]

    def flat(values):
        return values.reshape(planes * EDGE, values.shape[-1])

    def shifted(values, low_row, high_row, tap):
        if tap == 0:
            return jnp.concatenate([low_row, values[:, : EDGE - 1]], axis=1)
        if tap == 2:
            return jnp.concatenate([values[:, 1:], high_row], axis=1)
        return values

    for tap in range(3):
        moved = flat(shifted(center, halo_low, halo_high, tap))
        moved_edge = flat(shifted(edge, edge_low, edge_high, tap))

        def store(k, around, pair):
            rows = pl.ds(k * planes * EDGE, planes * EDGE)
            base = tap * 2 * PAIR
            out_ref[rows, base : base + PAIR] = around.astype(jnp.bfloat16)
            out_ref[rows, base + PAIR : base + 2 * PAIR] = pair.astype(jnp.bfloat16)

        place_windows(store, moved, moved_edge)


def outer_rows(center, y_ref, width):
    low, high = [], []
    for side in range(2):
        below = y_ref[side, 0].astype(jnp.float32)[EDGE - 1 :, None, :width]
        level = y_ref[side, 1].astype(jnp.float32)[:, None, :width]
        above = y_ref[side, 2].astype(jnp.float32)[:1, None, :width]
        (low if side == 0 else high).extend([below, level, above])
    planes = EDGE + 2
    low.append(center[:planes, EDGE - 1 :])
    high = [center[planes:, :1]] + high
    return jnp.concatenate(low, axis=0), jnp.concatenate(high, axis=0)


def sum_taps(result, planes, store):
    for k in range(PAIRS):
        for brick in range(2):
            base = k * planes * EDGE + brick * (planes // 2) * EDGE
            total = result[base : base + EDGE * EDGE, :PAIR]
            for a in range(1, 3):
                start = base + a * EDGE
                total = total + result[start : start + EDGE * EDGE, a * PAIR : (a + 1) * PAIR]
            store(brick, k, total.reshape(EDGE, EDGE, PAIR).astype(jnp.bfloat16))


def kernel_body(
    count, dp_count, scale, reduce_here,
    nb_ref, f_ref, c_ref, w_ref,
    resp_ref, fg_ref, kg_ref,
    fx, fy, cx, cy, fys, cys, cz, xw, cw, wf, wg, part, core_in, sbuf, rbuf, fin,
    halo_send, halo_recv, core_sem, rs_send, rs_recv, ag_send, ag_recv, fw_send, fw_recv,
):
    me = lax.axis_index("space")
    core = lax.axis_index("dp")
    planes = 2 * (EDGE + 2)

    fx[...] = jnp.zeros_like(fx)
    fy[...] = jnp.zeros_like(fy)
    cx[...] = jnp.zeros_like(cx)
    cy[...] = jnp.zeros_like(cy)

    barrier = pltpu.get_barrier_semaphore()
    if reduce_here:
        for step in range(1, count):
            pl.semaphore_signal(
                barrier, inc=1, device_id={"space": (me + step) % count}, device_id_type=MESH
            )
        pl.semaphore_signal(barrier, inc=1, device_id={"dp": 1 - core}, device_id_type=MESH)
    else:
        for step in (1, 3, 4, 5):
            for other in (me + step, me - step):

                @pl.when(in_range(other, count))
                def _():
                    pl.semaphore_signal(
                        barrier, inc=1, device_id={"space": other}, device_id_type=MESH
                    )

    for brick in range(2):
        other = 1 - brick
        before = jnp.where(nb_ref[0, brick, 4] >= 0, 1.0, 0.0)
        after = jnp.where(nb_ref[0, brick, 5] >= 0, 1.0, 0.0)
        cz[brick, :, :, :ROWS] = c_ref[0, brick]
        low = low_lanes((EDGE, EDGE, PAIR))
        edge = jnp.where(
            low,
            c_ref[0, other, :, :, :PAIR].astype(jnp.float32) * after,
            c_ref[0, other, :, :, ROWS - PAIR :].astype(jnp.float32) * before,
        )
        cz[brick, :, :, ROWS:] = edge.astype(jnp.bfloat16)
    fys[0] = f_ref[0, 1].astype(jnp.float32)[:, EDGE - 1].astype(jnp.bfloat16)
    fys[1] = f_ref[0, 0].astype(jnp.float32)[:, 0].astype(jnp.bfloat16)
    cys[0] = cz[1].astype(jnp.float32)[:, EDGE - 1].astype(jnp.bfloat16)
    cys[1] = cz[0].astype(jnp.float32)[:, 0].astype(jnp.bfloat16)

    if reduce_here:
        pl.semaphore_wait(barrier, count)
    else:
        for step in (1, 3, 4, 5):
            for other in (me + step, me - step):

                @pl.when(in_range(other, count))
                def _():
                    pl.semaphore_wait(barrier, 1)

    def halo(kind):
        x_ref, y_ref, ys_ref = ((fx, fy, fys), (cx, cy, cys))[kind]
        entries = []
        for side in range(2):
            dx = 2 * side - 1
            target = me - TILES_Y * dx
            face = EDGE - 1 if side == 0 else 0
            source = f_ref.at[0, :, face] if kind == 0 else cz.at[:, face]
            entries.append((
                receives(target, dx, 0, count, True),
                receives(me, dx, 0, count, True),
                source, x_ref.at[side], target,
            ))
        for side, column in DIAGONALS:
            dx, dy = column - 1, 2 * side - 1
            target = me - TILES_Y * dx - dy
            entries.append((
                receives(target, dx, dy, count, kind == 1),
                receives(me, dx, dy, count, kind == 1),
                ys_ref.at[side], y_ref.at[side, column], target,
            ))
        out = []
        for number, (sent, arrives, source, target_ref, target) in enumerate(entries):
            out.append((sent, arrives, pltpu.make_async_remote_copy(
                src_ref=source, dst_ref=target_ref,
                send_sem=halo_send.at[kind * 8 + number],
                recv_sem=halo_recv.at[kind * 8 + number],
                device_id={"space": target}, device_id_type=MESH,
            )))
        return out

    def start_halo(copies):
        for sent, _, copy in copies:
            pl.when(sent)(copy.start)

    def wait_halo(copies):
        for _, arrives, copy in copies:
            pl.when(arrives)(copy.wait_recv)

    f_copies, c_copies = halo(0), halo(1)
    start_halo(f_copies)
    start_halo(c_copies)

    order = (3, 0, 1, 2)
    blank = jnp.zeros((CH, CH), jnp.bfloat16)
    for a in range(3):
        for b in range(3):
            taps = [w_ref[a, b, d] for d in range(3)]
            for slot, w in enumerate(order):
                left = taps[w] if w < 3 else blank
                right = taps[w - 1] if w > 0 else blank
                row = b * 4 * CH + slot * CH
                wf[row : row + CH, a * PAIR : (a + 1) * PAIR] = jnp.concatenate([left, right], axis=1)
            flip_a, flip_b = 2 - a, 2 - b
            for cell in range(2):
                row = flip_a * PAIR + cell * CH
                for half in range(2):
                    pieces = []
                    for w in order[2 * half : 2 * half + 2]:
                        d = w - cell
                        pieces.append(taps[2 - d] if 0 <= d <= 2 else blank)
                    lane = flip_b * 4 * CH + half * PAIR
                    wg[row : row + CH, lane : lane + PAIR] = jnp.concatenate(pieces, axis=1)

    wait_halo(f_copies)

    def stack(values, x_ref, width):
        parts = []
        for brick in range(2):
            parts.append(x_ref[0, brick].astype(jnp.float32)[None, :, :width])
            parts.append(values[brick])
            parts.append(x_ref[1, brick].astype(jnp.float32)[None, :, :width])
        return jnp.concatenate(parts, axis=0)

    center = stack([f_ref[0, b].astype(jnp.float32) for b in range(2)], fx, ROWS)
    row_low, row_high = outer_rows(center, fy, ROWS)

    def third_edge(values):
        pieces = []
        half = planes // 2
        for brick in range(2):
            other = values[(1 - brick) * half : (2 - brick) * half]
            before = jnp.where(nb_ref[0, brick, 4] >= 0, 1.0, 0.0)
            after = jnp.where(nb_ref[0, brick, 5] >= 0, 1.0, 0.0)
            low = low_lanes((half, values.shape[1], PAIR))
            pieces.append(
                jnp.where(low, other[..., :PAIR] * after, other[..., ROWS - PAIR :] * before)
            )
        return jnp.concatenate(pieces, axis=0)

    build_windows(
        xw, center, third_edge(center), row_low, row_high, third_edge(row_low), third_edge(row_high)
    )

    cot_rows = []
    zero_plane = jnp.zeros((EDGE, PAIR), jnp.float32)
    for k in range(PAIRS):
        per_tap = []
        blocks = [
            c_ref[0, brick, :, :, k * PAIR : (k + 1) * PAIR].astype(jnp.float32).reshape(EDGE * EDGE, PAIR)
            for brick in range(2)
        ]
        for a in range(3):
            pieces = []
            for brick in range(2):
                pieces += [zero_plane] * a + [blocks[brick]] + [zero_plane] * (2 - a)
            per_tap.append(jnp.concatenate(pieces, axis=0))
        cot_rows.append(jnp.concatenate(per_tap, axis=1).astype(jnp.bfloat16))
    cot_all = jnp.concatenate(cot_rows, axis=0)
    grad = lax.dot_general(
        cot_all, xw[...], (((0,), (0,)), ((), ())), preferred_element_type=jnp.float32
    )
    low = low_lanes((CH, PAIR))
    first_taps = []
    for a in range(3):
        for b in range(3):
            cell0 = grad[a * PAIR : a * PAIR + CH, b * 4 * CH : (b + 1) * 4 * CH]
            cell1 = grad[a * PAIR + CH : (a + 1) * PAIR, b * 4 * CH : (b + 1) * 4 * CH]
            turned0 = pltpu.roll(cell1[:, :PAIR], CH, 1)
            turned1 = pltpu.roll(cell1[:, PAIR:], CH, 1)
            part[a * 3 + b] = cell0[:, PAIR:] + jnp.where(low, turned1, turned0)
            first_taps.append(cell0[:, :PAIR] + turned1)
    for m in range(5):
        high = first_taps[2 * m + 1] if 2 * m + 1 < 9 else jnp.zeros((CH, PAIR), jnp.float32)
        part[9 + m] = jnp.where(low, pltpu.roll(first_taps[2 * m], CH, 1), high)

    if reduce_here:
        core_copy = pltpu.make_async_remote_copy(
            src_ref=part.at[pl.ds((1 - core) * OWNED, OWNED)], dst_ref=core_in,
            send_sem=core_sem.at[0], recv_sem=core_sem.at[1],
            device_id={"dp": 1 - core}, device_id_type=MESH,
        )
        core_copy.start()

    result = jnp.dot(xw[...], wf[...], preferred_element_type=jnp.float32)

    def put_response(brick, k, value):
        resp_ref[0, brick, :, :, k * PAIR : (k + 1) * PAIR] = value

    sum_taps(result, planes, put_response)

    if reduce_here:
        core_copy.wait()
        rs_copies = []
        for tile in range(OWNED):
            sbuf[tile] = (part[core * OWNED + tile] + core_in[tile]).astype(jnp.bfloat16)
            copy = pltpu.make_async_remote_copy(
                src_ref=sbuf.at[tile], dst_ref=rbuf.at[me],
                send_sem=rs_send.at[tile], recv_sem=rs_recv.at[me],
                device_id={"space": tile}, device_id_type=MESH,
            )
            rs_copies.append(copy)

            @pl.when(me != tile)
            def _():
                copy.start()

            @pl.when(me == tile)
            def _():
                rbuf[tile] = sbuf[tile]

    wait_halo(c_copies)
    wide = stack([cz[b].astype(jnp.float32) for b in range(2)], cx, WIDE)
    wide_low, wide_high = outer_rows(wide, cy, WIDE)
    build_windows(
        cw, wide[..., :ROWS], wide[..., ROWS:], wide_low[..., :ROWS], wide_high[..., :ROWS],
        wide_low[..., ROWS:], wide_high[..., ROWS:],
    )
    result = lax.dot_general(
        cw[...], wg[...], (((1,), (1,)), ((), ())), preferred_element_type=jnp.float32
    )

    def put_gradient(brick, k, value):
        fg_ref[0, brick, :, :, k * PAIR : (k + 1) * PAIR] = value

    sum_taps(result, planes, put_gradient)

    def finish(tile, value):
        turned = (value * scale).T
        if tile < 9:
            kg_ref[tile // 3, tile % 3, 1] = turned[:CH]
            kg_ref[tile // 3, tile % 3, 2] = turned[CH:]
        else:
            for half in range(2):
                tap = 2 * (tile - 9) + half
                if tap < 9:
                    kg_ref[tap // 3, tap % 3, 0] = turned[half * CH : (half + 1) * CH]

    if reduce_here:
        for tile in range(OWNED):
            pl.when(me != tile)(rs_copies[tile].wait_send)

        def gather_copy(step):
            target = (me + step) % count
            return pltpu.make_async_remote_copy(
                src_ref=fin.at[core * OWNED + me], dst_ref=fin.at[core * OWNED + me],
                send_sem=ag_send.at[step], recv_sem=ag_recv.at[me],
                device_id={"space": target}, device_id_type=MESH,
            )

        def forward_copy(tile):
            spot = fin.at[core * OWNED + tile]
            return pltpu.make_async_remote_copy(
                src_ref=spot, dst_ref=spot,
                send_sem=fw_send.at[tile], recv_sem=fw_recv.at[tile],
                device_id={"dp": 1 - core}, device_id_type=MESH,
            )

        @pl.when(me < OWNED)
        def _():
            total = jnp.zeros((CH, PAIR), jnp.float32)
            for source in range(count):

                @pl.when(me != source)
                def _():
                    pltpu.make_async_remote_copy(
                        src_ref=sbuf.at[0], dst_ref=rbuf.at[source],
                        send_sem=rs_send.at[0], recv_sem=rs_recv.at[source],
                        device_id={"space": source}, device_id_type=MESH,
                    ).wait_recv()

                total = total + rbuf[source].astype(jnp.float32)
            fin[core * OWNED + me] = total.astype(jnp.bfloat16)
            for step in range(1, count):
                gather_copy(step).start()

        for tile in range(OWNED):

            @pl.when(me != tile)
            def _():
                spot = fin.at[core * OWNED + tile]
                pltpu.make_async_remote_copy(
                    src_ref=spot, dst_ref=spot,
                    send_sem=ag_send.at[0], recv_sem=ag_recv.at[tile],
                    device_id={"space": tile}, device_id_type=MESH,
                ).wait_recv()

            forward_copy(tile).start()

        for tile in range(OWNED):
            spot = fin.at[(1 - core) * OWNED + tile]
            pltpu.make_async_remote_copy(
                src_ref=spot, dst_ref=spot,
                send_sem=fw_send.at[tile], recv_sem=fw_recv.at[tile],
                device_id={"dp": 1 - core}, device_id_type=MESH,
            ).wait_recv()
        for tile in range(TILES):
            finish(tile, fin[tile].astype(jnp.float32))
        for tile in range(OWNED):
            forward_copy(tile).wait_send()

        @pl.when(me < OWNED)
        def _():
            for step in range(1, count):
                gather_copy(step).wait_send()
    else:
        for tile in range(TILES):
            finish(tile, part[tile])
    for sent, _, copy in f_copies + c_copies:
        pl.when(sent)(copy.wait_send)


def body(features, cotangent, kernel, neighbours):
    count = lax.axis_size("space")
    dp_count = lax.axis_size("dp")
    reduce_here = count == 8 and dp_count == 2
    cells = features.shape[0] * features.shape[1] * dp_count * count * EDGE**3
    scale = 1.0 / math.sqrt(cells)
    bf16, f32 = jnp.bfloat16, jnp.float32
    planes = 2 * (EDGE + 2)
    rows = PAIRS * planes * EDGE
    dma = pltpu.SemaphoreType.DMA
    vmem = pl.BlockSpec(memory_space=pltpu.VMEM)
    response, feature_grad, kernel_grad = pl.pallas_call(
        functools.partial(kernel_body, count, dp_count, scale, reduce_here),
        out_shape=(
            jax.ShapeDtypeStruct(features.shape, bf16),
            jax.ShapeDtypeStruct(features.shape, bf16),
            jax.ShapeDtypeStruct(kernel.shape, f32),
        ),
        in_specs=[pl.BlockSpec(memory_space=pltpu.SMEM), vmem, vmem, vmem],
        out_specs=(vmem, vmem, vmem),
        scratch_shapes=[
            pltpu.VMEM((2, 2, EDGE, ROWS), bf16),
            pltpu.VMEM((2, 3, EDGE, ROWS), bf16),
            pltpu.VMEM((2, 2, EDGE, WIDE), bf16),
            pltpu.VMEM((2, 3, EDGE, WIDE), bf16),
            pltpu.VMEM((2, EDGE, ROWS), bf16),
            pltpu.VMEM((2, EDGE, WIDE), bf16),
            pltpu.VMEM((2, EDGE, EDGE, WIDE), bf16),
            pltpu.VMEM((rows, 12 * CH), bf16),
            pltpu.VMEM((rows, 12 * CH), bf16),
            pltpu.VMEM((12 * CH, 6 * CH), bf16),
            pltpu.VMEM((6 * CH, 12 * CH), bf16),
            pltpu.VMEM((TILES, CH, PAIR), f32),
            pltpu.VMEM((OWNED, CH, PAIR), f32),
            pltpu.VMEM((OWNED, CH, PAIR), bf16),
            pltpu.VMEM((8, CH, PAIR), bf16),
            pltpu.VMEM((TILES, CH, PAIR), bf16),
            dma((16,)), dma((16,)), dma((2,)), dma((8,)), dma((8,)),
            dma((8,)), dma((8,)), dma((8,)), dma((8,)),
        ],
        compiler_params=pltpu.CompilerParams(
            collective_id=0, has_side_effects=True, vmem_limit_bytes=40 * 1024 * 1024
        ),
        cost_estimate=pl.CostEstimate(flops=10**9, bytes_accessed=2 * 10**6, transcendentals=0),
    )(neighbours, features, cotangent, kernel)
    if not reduce_here:
        kernel_grad = lax.psum(kernel_grad, ("space", "dp"))
    return (response, feature_grad, kernel_grad)


def solution(mesh):
    in_specs = (
        P(("groups", "dp"), "space", None, None, None),
        P(("groups", "dp"), "space", None, None, None),
        P(),
        P(("groups", "dp"), "space", None),
    )
    out_specs = (
        P(("groups", "dp"), "space", None, None, None),
        P(("groups", "dp"), "space", None, None, None),
        P("groups", None, None, None, None),
    )
    return jax.shard_map(body, mesh=mesh, in_specs=in_specs, out_specs=out_specs, check_vma=False)
```

```python
import functools
import math

import jax
import jax.numpy as jnp
from jax import lax
from jax.experimental import pallas as pl
from jax.experimental.pallas import tpu as pltpu
from jax.sharding import PartitionSpec as P

TILES_Y = 4
EDGE = 8
CH = 64
PAIR = 2 * CH
PAIRS = EDGE // 2
ROWS = EDGE * CH
WIDE = ROWS + PAIR
TILES = 14
OWNED = TILES // 2
MESH = pl.DeviceIdType.MESH
DIAGONALS = [(side, dx) for side in range(2) for dx in range(3)]


def low_lanes(shape):
    return lax.broadcasted_iota(jnp.int32, shape, len(shape) - 1) < CH


def in_range(tile, count):
    return (tile >= 0) & (tile < count)


def receives(tile, dx, dy, count, first_x):
    column = (tile + TILES_Y // 2) % TILES_Y + dy
    there = in_range(tile + TILES_Y * dx + dy, count) & (column >= 0) & (column < TILES_Y)
    between = tile + TILES_Y * dx if first_x else tile + dy
    return in_range(tile, count) & in_range(between, count) & there


def place_windows(store, center, edge):
    low = low_lanes((center.shape[0], PAIR))
    pairs = [center[:, PAIR * k : PAIR * (k + 1)] for k in range(PAIRS)]
    for k in range(PAIRS):
        after = pairs[k + 1] if k + 1 < PAIRS else edge
        before = pairs[k - 1] if k > 0 else edge
        store(k, jnp.where(low, after, before), pairs[k])


def window_builder(out_ref, center, edge, halo_low, halo_high, edge_low, edge_high):
    planes = center.shape[0]

    def flat(values):
        return values.reshape(planes * EDGE, values.shape[-1])

    def shifted(values, low_row, high_row, tap):
        if tap == 0:
            return jnp.concatenate([low_row, values[:, : EDGE - 1]], axis=1)
        if tap == 2:
            return jnp.concatenate([values[:, 1:], high_row], axis=1)
        return values

    def build(tap):
        moved = flat(shifted(center, halo_low, halo_high, tap))
        moved_edge = flat(shifted(edge, edge_low, edge_high, tap))

        def store(k, around, pair):
            rows = pl.ds(k * planes * EDGE, planes * EDGE)
            base = tap * 2 * PAIR
            out_ref[rows, base : base + PAIR] = around.astype(jnp.bfloat16)
            out_ref[rows, base + PAIR : base + 2 * PAIR] = pair.astype(jnp.bfloat16)

        place_windows(store, moved, moved_edge)

    return build


def outer_rows(center, y_ref, width):
    low, high = [], []
    for side in range(2):
        below = y_ref[side, 0].astype(jnp.float32)[EDGE - 1 :, None, :width]
        level = y_ref[side, 1].astype(jnp.float32)[:, None, :width]
        above = y_ref[side, 2].astype(jnp.float32)[:1, None, :width]
        (low if side == 0 else high).extend([below, level, above])
    planes = EDGE + 2
    low.append(center[:planes, EDGE - 1 :])
    high = [center[planes:, :1]] + high
    return jnp.concatenate(low, axis=0), jnp.concatenate(high, axis=0)


def sum_taps(result, planes, store):
    for k in range(PAIRS):
        for brick in range(2):
            base = k * planes * EDGE + brick * (planes // 2) * EDGE
            total = result[base : base + EDGE * EDGE, :PAIR]
            for a in range(1, 3):
                start = base + a * EDGE
                total = total + result[start : start + EDGE * EDGE, a * PAIR : (a + 1) * PAIR]
            store(brick, k, total.reshape(EDGE, EDGE, PAIR).astype(jnp.bfloat16))


def kernel_body(
    count, reduce_here,
    nb_hbm, f_hbm, c_hbm, w_hbm,
    resp_ref, fg_ref, tiles_ref,
    nb_ref, f_ref, c_ref, w_ref,
    fx, fy, cx, cy, fys, cys, cz, xw, cw, ct, wf, wg, part, core_in, sbuf, rbuf,
    load_sem, halo_send, halo_recv, core_sem, rs_send, rs_recv, ag_send, ag_recv, fw_send, fw_recv,
):
    me = lax.axis_index("space")
    core = lax.axis_index("dp")
    planes = 2 * (EDGE + 2)

    if reduce_here:
        fin = tiles_ref
    else:
        part = tiles_ref
    loads = [
        pltpu.make_async_copy(src, dst, load_sem.at[number])
        for number, (src, dst) in enumerate(
            [(f_hbm, f_ref), (c_hbm, c_ref), (nb_hbm, nb_ref), (w_hbm, w_ref)]
        )
    ]
    for load in loads:
        load.start()

    fx[...] = jnp.zeros_like(fx)
    fy[...] = jnp.zeros_like(fy)
    cx[...] = jnp.zeros_like(cx)
    cy[...] = jnp.zeros_like(cy)

    barrier = pltpu.get_barrier_semaphore()
    if reduce_here:
        for step in range(1, count):
            pl.semaphore_signal(
                barrier, inc=1, device_id={"space": (me + step) % count}, device_id_type=MESH
            )
        pl.semaphore_signal(barrier, inc=1, device_id={"dp": 1 - core}, device_id_type=MESH)
    else:
        for step in (1, 3, 4, 5):
            for other in (me + step, me - step):

                @pl.when(in_range(other, count))
                def _():
                    pl.semaphore_signal(
                        barrier, inc=1, device_id={"space": other}, device_id_type=MESH
                    )

    def halo(kind):
        x_ref, y_ref, ys_ref = ((fx, fy, fys), (cx, cy, cys))[kind]
        entries = []
        for side in range(2):
            dx = 2 * side - 1
            target = me - TILES_Y * dx
            face = EDGE - 1 if side == 0 else 0
            source = f_ref.at[0, :, face] if kind == 0 else cz.at[:, face]
            entries.append((
                receives(target, dx, 0, count, True),
                receives(me, dx, 0, count, True),
                source, x_ref.at[side], target,
            ))
        for side, column in DIAGONALS:
            dx, dy = column - 1, 2 * side - 1
            target = me - TILES_Y * dx - dy
            entries.append((
                receives(target, dx, dy, count, kind == 1),
                receives(me, dx, dy, count, kind == 1),
                ys_ref.at[side], y_ref.at[side, column], target,
            ))
        out = []
        for number, (sent, arrives, source, target_ref, target) in enumerate(entries):
            out.append((sent, arrives, pltpu.make_async_remote_copy(
                src_ref=source, dst_ref=target_ref,
                send_sem=halo_send.at[kind * 8 + number],
                recv_sem=halo_recv.at[kind * 8 + number],
                device_id={"space": target}, device_id_type=MESH,
            )))
        return out

    def start_halo(copies):
        for sent, _, copy in copies:
            pl.when(sent)(copy.start)

    def wait_halo(copies):
        for _, arrives, copy in copies:
            pl.when(arrives)(copy.wait_recv)

    loads[0].wait()
    fys[0] = f_ref[0, 1].astype(jnp.float32)[:, EDGE - 1].astype(jnp.bfloat16)
    fys[1] = f_ref[0, 0].astype(jnp.float32)[:, 0].astype(jnp.bfloat16)

    if reduce_here:
        pl.semaphore_wait(barrier, count)
    else:
        for step in (1, 3, 4, 5):
            for other in (me + step, me - step):

                @pl.when(in_range(other, count))
                def _():
                    pl.semaphore_wait(barrier, 1)

    f_copies, c_copies = halo(0), halo(1)
    start_halo(f_copies)

    loads[1].wait()
    loads[2].wait()
    for brick in range(2):
        other = 1 - brick
        before = jnp.where(nb_ref[0, brick, 4] >= 0, 1.0, 0.0)
        after = jnp.where(nb_ref[0, brick, 5] >= 0, 1.0, 0.0)
        cz[brick, :, :, :ROWS] = c_ref[0, brick]
        low = low_lanes((EDGE, EDGE, PAIR))
        edge = jnp.where(
            low,
            c_ref[0, other, :, :, :PAIR].astype(jnp.float32) * after,
            c_ref[0, other, :, :, ROWS - PAIR :].astype(jnp.float32) * before,
        )
        cz[brick, :, :, ROWS:] = edge.astype(jnp.bfloat16)
    cys[0] = cz[1].astype(jnp.float32)[:, EDGE - 1].astype(jnp.bfloat16)
    cys[1] = cz[0].astype(jnp.float32)[:, 0].astype(jnp.bfloat16)
    start_halo(c_copies)

    cot_rows = []
    zero_plane = jnp.zeros((EDGE, PAIR), jnp.float32)
    for k in range(PAIRS):
        per_tap = []
        blocks = [
            c_ref[0, brick, :, :, k * PAIR : (k + 1) * PAIR].astype(jnp.float32).reshape(EDGE * EDGE, PAIR)
            for brick in range(2)
        ]
        for a in range(3):
            pieces = []
            for brick in range(2):
                pieces += [zero_plane] * a + [blocks[brick]] + [zero_plane] * (2 - a)
            per_tap.append(jnp.concatenate(pieces, axis=0))
        cot_rows.append(jnp.concatenate(per_tap, axis=1))
    ct[...] = jnp.concatenate(cot_rows, axis=0).T.astype(jnp.bfloat16)

    loads[3].wait()
    order = (3, 0, 1, 2)
    blank = jnp.zeros((CH, CH), jnp.bfloat16)
    for a in range(3):
        for b in range(3):
            taps = [w_ref[a, b, d] for d in range(3)]
            for slot, w in enumerate(order):
                left = taps[w] if w < 3 else blank
                right = taps[w - 1] if w > 0 else blank
                row = b * 4 * CH + slot * CH
                wf[row : row + CH, a * PAIR : (a + 1) * PAIR] = jnp.concatenate([left, right], axis=1)
            flip_a, flip_b = 2 - a, 2 - b
            for cell in range(2):
                row = flip_a * PAIR + cell * CH
                for half in range(2):
                    pieces = []
                    for w in order[2 * half : 2 * half + 2]:
                        d = w - cell
                        pieces.append(taps[2 - d] if 0 <= d <= 2 else blank)
                    lane = flip_b * 4 * CH + half * PAIR
                    wg[row : row + CH, lane : lane + PAIR] = jnp.concatenate(pieces, axis=1)

    wait_halo(f_copies)

    def stack(values, x_ref, width):
        parts = []
        for brick in range(2):
            parts.append(x_ref[0, brick].astype(jnp.float32)[None, :, :width])
            parts.append(values[brick])
            parts.append(x_ref[1, brick].astype(jnp.float32)[None, :, :width])
        return jnp.concatenate(parts, axis=0)

    center = stack([f_ref[0, b].astype(jnp.float32) for b in range(2)], fx, ROWS)
    row_low, row_high = outer_rows(center, fy, ROWS)

    def third_edge(values):
        pieces = []
        half = planes // 2
        for brick in range(2):
            other = values[(1 - brick) * half : (2 - brick) * half]
            before = jnp.where(nb_ref[0, brick, 4] >= 0, 1.0, 0.0)
            after = jnp.where(nb_ref[0, brick, 5] >= 0, 1.0, 0.0)
            low = low_lanes((half, values.shape[1], PAIR))
            pieces.append(
                jnp.where(low, other[..., :PAIR] * after, other[..., ROWS - PAIR :] * before)
            )
        return jnp.concatenate(pieces, axis=0)

    build_features = window_builder(
        xw, center, third_edge(center), row_low, row_high, third_edge(row_low), third_edge(row_high)
    )

    low = low_lanes((CH, PAIR))
    first_taps = []
    for b in range(3):
        build_features(b)
        grad = jnp.dot(
            ct[...], xw[:, b * 4 * CH : (b + 1) * 4 * CH], preferred_element_type=jnp.float32
        )
        for a in range(3):
            cell0 = grad[a * PAIR : a * PAIR + CH]
            cell1 = grad[a * PAIR + CH : (a + 1) * PAIR]
            turned0 = pltpu.roll(cell1[:, :PAIR], CH, 1)
            turned1 = pltpu.roll(cell1[:, PAIR:], CH, 1)
            part[b * 3 + a] = cell0[:, PAIR:] + jnp.where(low, turned1, turned0)
            first_taps.append(cell0[:, :PAIR] + turned1)
    for m in range(5):
        high = first_taps[2 * m + 1] if 2 * m + 1 < 9 else jnp.zeros((CH, PAIR), jnp.float32)
        part[9 + m] = jnp.where(low, pltpu.roll(first_taps[2 * m], CH, 1), high)

    if reduce_here:
        core_copy = pltpu.make_async_remote_copy(
            src_ref=part.at[pl.ds((1 - core) * OWNED, OWNED)], dst_ref=core_in,
            send_sem=core_sem.at[0], recv_sem=core_sem.at[1],
            device_id={"dp": 1 - core}, device_id_type=MESH,
        )
        core_copy.start()

    wait_halo(c_copies)
    wide = stack([cz[b].astype(jnp.float32) for b in range(2)], cx, WIDE)
    wide_low, wide_high = outer_rows(wide, cy, WIDE)
    build_cotangent = window_builder(
        cw, wide[..., :ROWS], wide[..., ROWS:], wide_low[..., :ROWS], wide_high[..., :ROWS],
        wide_low[..., ROWS:], wide_high[..., ROWS:],
    )
    for tap in range(3):
        build_cotangent(tap)

    if reduce_here:
        core_copy.wait()
        rs_copies = []
        for tile in range(OWNED):
            sbuf[tile] = (part[core * OWNED + tile] + core_in[tile]).astype(jnp.bfloat16)
            copy = pltpu.make_async_remote_copy(
                src_ref=sbuf.at[tile], dst_ref=rbuf.at[me],
                send_sem=rs_send.at[tile], recv_sem=rs_recv.at[me],
                device_id={"space": tile}, device_id_type=MESH,
            )
            rs_copies.append(copy)

            @pl.when(me != tile)
            def _():
                copy.start()

            @pl.when(me == tile)
            def _():
                rbuf[tile] = sbuf[tile]

    result = jnp.dot(xw[...], wf[...], preferred_element_type=jnp.float32)

    def put_response(brick, k, value):
        resp_ref[0, brick, :, :, k * PAIR : (k + 1) * PAIR] = value

    sum_taps(result, planes, put_response)

    result = lax.dot_general(
        cw[...], wg[...], (((1,), (1,)), ((), ())), preferred_element_type=jnp.float32
    )

    def put_gradient(brick, k, value):
        fg_ref[0, brick, :, :, k * PAIR : (k + 1) * PAIR] = value

    sum_taps(result, planes, put_gradient)

    if reduce_here:
        for tile in range(OWNED):
            pl.when(me != tile)(rs_copies[tile].wait_send)

        def gather_copy(step):
            target = (me + step) % count
            return pltpu.make_async_remote_copy(
                src_ref=fin.at[core * OWNED + me], dst_ref=fin.at[core * OWNED + me],
                send_sem=ag_send.at[step], recv_sem=ag_recv.at[me],
                device_id={"space": target}, device_id_type=MESH,
            )

        def forward_copy(tile):
            spot = fin.at[core * OWNED + tile]
            return pltpu.make_async_remote_copy(
                src_ref=spot, dst_ref=spot,
                send_sem=fw_send.at[tile], recv_sem=fw_recv.at[tile],
                device_id={"dp": 1 - core}, device_id_type=MESH,
            )

        @pl.when(me < OWNED)
        def _():
            total = jnp.zeros((CH, PAIR), jnp.float32)
            for source in range(count):

                @pl.when(me != source)
                def _():
                    pltpu.make_async_remote_copy(
                        src_ref=sbuf.at[0], dst_ref=rbuf.at[source],
                        send_sem=rs_send.at[0], recv_sem=rs_recv.at[source],
                        device_id={"space": source}, device_id_type=MESH,
                    ).wait_recv()

                total = total + rbuf[source].astype(jnp.float32)
            fin[core * OWNED + me] = total.astype(jnp.bfloat16)
            for step in range(1, count):
                gather_copy(step).start()

        for tile in range(OWNED):

            @pl.when(me != tile)
            def _():
                spot = fin.at[core * OWNED + tile]
                pltpu.make_async_remote_copy(
                    src_ref=spot, dst_ref=spot,
                    send_sem=ag_send.at[0], recv_sem=ag_recv.at[tile],
                    device_id={"space": tile}, device_id_type=MESH,
                ).wait_recv()

            forward_copy(tile).start()

        for tile in range(OWNED):
            spot = fin.at[(1 - core) * OWNED + tile]
            pltpu.make_async_remote_copy(
                src_ref=spot, dst_ref=spot,
                send_sem=fw_send.at[tile], recv_sem=fw_recv.at[tile],
                device_id={"dp": 1 - core}, device_id_type=MESH,
            ).wait_recv()
        for tile in range(OWNED):
            forward_copy(tile).wait_send()

        @pl.when(me < OWNED)
        def _():
            for step in range(1, count):
                gather_copy(step).wait_send()
    for sent, _, copy in f_copies + c_copies:
        pl.when(sent)(copy.wait_send)


def finish_body(scale, resp_ref, fg_ref, tiles_ref, resp_hbm, fg_hbm, kg_hbm, kg, sems):
    copies = [
        pltpu.make_async_copy(resp_ref, resp_hbm, sems.at[0]),
        pltpu.make_async_copy(fg_ref, fg_hbm, sems.at[1]),
    ]
    for copy in copies:
        copy.start()
    for tile in range(TILES):
        turned = (tiles_ref[tile].astype(jnp.float32) * scale).T
        for half in range(2):
            block = turned[half * CH : (half + 1) * CH]
            if tile < 9:
                kg[tile % 3, tile // 3, half + 1] = block
            else:
                tap = 2 * (tile - 9) + half
                if tap < 9:
                    kg[tap % 3, tap // 3, 0] = block
    last = pltpu.make_async_copy(kg, kg_hbm, sems.at[2])
    last.start()
    for copy in copies:
        copy.wait()
    last.wait()


def body(features, cotangent, kernel, neighbours):
    count = lax.axis_size("space")
    dp_count = lax.axis_size("dp")
    reduce_here = count == 8 and dp_count == 2
    cells = features.shape[0] * features.shape[1] * dp_count * count * EDGE**3
    scale = 1.0 / math.sqrt(cells)
    bf16, f32 = jnp.bfloat16, jnp.float32
    planes = 2 * (EDGE + 2)
    rows = PAIRS * planes * EDGE
    dma = pltpu.SemaphoreType.DMA
    vmem = pl.BlockSpec(memory_space=pltpu.VMEM)
    hbm = pl.BlockSpec(memory_space=pltpu.HBM)
    part_shape = (TILES, CH, PAIR)
    response, feature_grad, tiles = pl.pallas_call(
        functools.partial(kernel_body, count, reduce_here),
        out_shape=(
            jax.ShapeDtypeStruct(features.shape, bf16),
            jax.ShapeDtypeStruct(features.shape, bf16),
            jax.ShapeDtypeStruct(part_shape, bf16 if reduce_here else f32),
        ),
        in_specs=[hbm] * 4,
        out_specs=(vmem, vmem, vmem),
        scratch_shapes=[
            pltpu.SMEM(neighbours.shape, jnp.int32),
            pltpu.VMEM(features.shape, bf16),
            pltpu.VMEM(features.shape, bf16),
            pltpu.VMEM(kernel.shape, bf16),
            pltpu.VMEM((2, 2, EDGE, ROWS), bf16),
            pltpu.VMEM((2, 3, EDGE, ROWS), bf16),
            pltpu.VMEM((2, 2, EDGE, WIDE), bf16),
            pltpu.VMEM((2, 3, EDGE, WIDE), bf16),
            pltpu.VMEM((2, EDGE, ROWS), bf16),
            pltpu.VMEM((2, EDGE, WIDE), bf16),
            pltpu.VMEM((2, EDGE, EDGE, WIDE), bf16),
            pltpu.VMEM((rows, 12 * CH), bf16),
            pltpu.VMEM((rows, 12 * CH), bf16),
            pltpu.VMEM((6 * CH, rows), bf16),
            pltpu.VMEM((12 * CH, 6 * CH), bf16),
            pltpu.VMEM((6 * CH, 12 * CH), bf16),
            pltpu.VMEM(part_shape, f32),
            pltpu.VMEM((OWNED, CH, PAIR), f32),
            pltpu.VMEM((OWNED, CH, PAIR), bf16),
            pltpu.VMEM((8, CH, PAIR), bf16),
            dma((4,)), dma((16,)), dma((16,)), dma((2,)), dma((8,)), dma((8,)),
            dma((8,)), dma((8,)), dma((8,)), dma((8,)),
        ],
        compiler_params=pltpu.CompilerParams(
            collective_id=0, has_side_effects=True, vmem_limit_bytes=40 * 1024 * 1024
        ),
        cost_estimate=pl.CostEstimate(flops=10**9, bytes_accessed=2 * 10**6, transcendentals=0),
    )(*(
        pltpu.with_memory_space_constraint(x, pltpu.HBM)
        for x in (neighbours, features, cotangent, kernel)
    ))
    if not reduce_here:
        tiles = lax.psum(tiles, ("space", "dp"))
    return pl.pallas_call(
        functools.partial(finish_body, scale),
        out_shape=(
            jax.ShapeDtypeStruct(features.shape, bf16),
            jax.ShapeDtypeStruct(features.shape, bf16),
            jax.ShapeDtypeStruct(kernel.shape, f32),
        ),
        in_specs=[vmem] * 3,
        out_specs=(hbm,) * 3,
        scratch_shapes=[pltpu.VMEM(kernel.shape, f32), dma((3,))],
        cost_estimate=pl.CostEstimate(flops=10**6, bytes_accessed=10**6, transcendentals=0),
    )(response, feature_grad, tiles)


def solution(mesh):
    in_specs = (
        P(("groups", "dp"), "space", None, None, None),
        P(("groups", "dp"), "space", None, None, None),
        P(),
        P(("groups", "dp"), "space", None),
    )
    out_specs = (
        P(("groups", "dp"), "space", None, None, None),
        P(("groups", "dp"), "space", None, None, None),
        P("groups", None, None, None, None),
    )
    return jax.shard_map(body, mesh=mesh, in_specs=in_specs, out_specs=out_specs, check_vma=False)
```

```python
import functools
import math

import jax
import jax.numpy as jnp
from jax import lax
from jax.experimental import pallas as pl
from jax.experimental.pallas import tpu as pltpu
from jax.sharding import PartitionSpec as P

TILES_Y = 4
EDGE = 8
CH = 64
PAIR = 2 * CH
PAIRS = EDGE // 2
ROWS = EDGE * CH
WIDE = ROWS + PAIR
TILES = 14
OWNED = TILES // 2
MESH = pl.DeviceIdType.MESH
DIAGONALS = [(side, dx) for side in range(2) for dx in range(3)]


def low_lanes(shape):
    return lax.broadcasted_iota(jnp.int32, shape, len(shape) - 1) < CH


def in_range(tile, count):
    return (tile >= 0) & (tile < count)


def receives(tile, dx, dy, count, first_x):
    column = (tile + TILES_Y // 2) % TILES_Y + dy
    there = in_range(tile + TILES_Y * dx + dy, count) & (column >= 0) & (column < TILES_Y)
    between = tile + TILES_Y * dx if first_x else tile + dy
    return in_range(tile, count) & in_range(between, count) & there


def place_windows(store, center, edge):
    low = low_lanes((center.shape[0], PAIR))
    pairs = [center[:, PAIR * k : PAIR * (k + 1)] for k in range(PAIRS)]
    for k in range(PAIRS):
        after = pairs[k + 1] if k + 1 < PAIRS else edge
        before = pairs[k - 1] if k > 0 else edge
        store(k, jnp.where(low, after, before), pairs[k])


def window_builder(out_ref, center, edge, halo_low, halo_high, edge_low, edge_high):
    planes = center.shape[0]

    def flat(values):
        return values.reshape(planes * EDGE, values.shape[-1])

    def shifted(values, low_row, high_row, tap):
        if tap == 0:
            return jnp.concatenate([low_row, values[:, : EDGE - 1]], axis=1)
        if tap == 2:
            return jnp.concatenate([values[:, 1:], high_row], axis=1)
        return values

    def build(tap):
        moved = flat(shifted(center, halo_low, halo_high, tap))
        moved_edge = flat(shifted(edge, edge_low, edge_high, tap))

        def store(k, around, pair):
            rows = pl.ds(k * planes * EDGE, planes * EDGE)
            base = tap * 2 * PAIR
            out_ref[rows, base : base + PAIR] = around.astype(jnp.bfloat16)
            out_ref[rows, base + PAIR : base + 2 * PAIR] = pair.astype(jnp.bfloat16)

        place_windows(store, moved, moved_edge)

    return build


def outer_rows(center, y_ref, width):
    low, high = [], []
    for side in range(2):
        below = y_ref[side, 0].astype(jnp.float32)[EDGE - 1 :, None, :width]
        level = y_ref[side, 1].astype(jnp.float32)[:, None, :width]
        above = y_ref[side, 2].astype(jnp.float32)[:1, None, :width]
        (low if side == 0 else high).extend([below, level, above])
    planes = EDGE + 2
    low.append(center[:planes, EDGE - 1 :])
    high = [center[planes:, :1]] + high
    return jnp.concatenate(low, axis=0), jnp.concatenate(high, axis=0)


def sum_taps(result, planes, store):
    for k in range(PAIRS):
        for brick in range(2):
            base = k * planes * EDGE + brick * (planes // 2) * EDGE
            total = result[base : base + EDGE * EDGE, :PAIR]
            for a in range(1, 3):
                start = base + a * EDGE
                total = total + result[start : start + EDGE * EDGE, a * PAIR : (a + 1) * PAIR]
            store(brick, k, total.reshape(EDGE, EDGE, PAIR).astype(jnp.bfloat16))


def turn(tile):
    turned = tile.T
    return jnp.concatenate([turned[:CH], turned[CH:]], axis=1)


def kernel_body(
    count, reduce_here,
    nb_hbm, f_hbm, c_hbm, w_hbm,
    resp_ref, fg_ref, tiles_ref,
    nb_ref, f_ref, c_ref, w_ref,
    fx, fy, cx, cy, fys, cys, cz, xw, cw, ct, wf, wg, part, core_in, sbuf, rbuf,
    load_sem, halo_send, halo_recv, core_sem, rs_send, rs_recv, ag_send, ag_recv, fw_send, fw_recv,
):
    me = lax.axis_index("space")
    core = lax.axis_index("dp")
    planes = 2 * (EDGE + 2)

    if reduce_here:
        fin = tiles_ref
    else:
        part = tiles_ref
    loads = [
        pltpu.make_async_copy(src, dst, load_sem.at[number])
        for number, (src, dst) in enumerate(
            [(f_hbm, f_ref), (c_hbm, c_ref), (nb_hbm, nb_ref), (w_hbm, w_ref)]
        )
    ]
    for load in loads:
        load.start()

    fx[...] = jnp.zeros_like(fx)
    fy[...] = jnp.zeros_like(fy)
    cx[...] = jnp.zeros_like(cx)
    cy[...] = jnp.zeros_like(cy)

    barrier = pltpu.get_barrier_semaphore()
    if reduce_here:
        for step in range(1, count):
            pl.semaphore_signal(
                barrier, inc=1, device_id={"space": (me + step) % count}, device_id_type=MESH
            )
        pl.semaphore_signal(barrier, inc=1, device_id={"dp": 1 - core}, device_id_type=MESH)
    else:
        for step in (1, 3, 4, 5):
            for other in (me + step, me - step):

                @pl.when(in_range(other, count))
                def _():
                    pl.semaphore_signal(
                        barrier, inc=1, device_id={"space": other}, device_id_type=MESH
                    )

    def halo(kind):
        x_ref, y_ref, ys_ref = ((fx, fy, fys), (cx, cy, cys))[kind]
        entries = []
        for side in range(2):
            dx = 2 * side - 1
            target = me - TILES_Y * dx
            face = EDGE - 1 if side == 0 else 0
            source = f_ref.at[0, :, face] if kind == 0 else cz.at[:, face]
            entries.append((
                receives(target, dx, 0, count, True),
                receives(me, dx, 0, count, True),
                source, x_ref.at[side], target,
            ))
        for side, column in DIAGONALS:
            dx, dy = column - 1, 2 * side - 1
            target = me - TILES_Y * dx - dy
            entries.append((
                receives(target, dx, dy, count, kind == 1),
                receives(me, dx, dy, count, kind == 1),
                ys_ref.at[side], y_ref.at[side, column], target,
            ))
        out = []
        for number, (sent, arrives, source, target_ref, target) in enumerate(entries):
            out.append((sent, arrives, pltpu.make_async_remote_copy(
                src_ref=source, dst_ref=target_ref,
                send_sem=halo_send.at[kind * 8 + number],
                recv_sem=halo_recv.at[kind * 8 + number],
                device_id={"space": target}, device_id_type=MESH,
            )))
        return out

    def start_halo(copies):
        for sent, _, copy in copies:
            pl.when(sent)(copy.start)

    def wait_halo(copies):
        for _, arrives, copy in copies:
            pl.when(arrives)(copy.wait_recv)

    loads[0].wait()
    fys[0] = f_ref[0, 1].astype(jnp.float32)[:, EDGE - 1].astype(jnp.bfloat16)
    fys[1] = f_ref[0, 0].astype(jnp.float32)[:, 0].astype(jnp.bfloat16)

    if reduce_here:
        pl.semaphore_wait(barrier, count)
    else:
        for step in (1, 3, 4, 5):
            for other in (me + step, me - step):

                @pl.when(in_range(other, count))
                def _():
                    pl.semaphore_wait(barrier, 1)

    f_copies, c_copies = halo(0), halo(1)
    start_halo(f_copies)

    loads[1].wait()
    loads[2].wait()
    for brick in range(2):
        other = 1 - brick
        before = jnp.where(nb_ref[0, brick, 4] >= 0, 1.0, 0.0)
        after = jnp.where(nb_ref[0, brick, 5] >= 0, 1.0, 0.0)
        cz[brick, :, :, :ROWS] = c_ref[0, brick]
        low = low_lanes((EDGE, EDGE, PAIR))
        edge = jnp.where(
            low,
            c_ref[0, other, :, :, :PAIR].astype(jnp.float32) * after,
            c_ref[0, other, :, :, ROWS - PAIR :].astype(jnp.float32) * before,
        )
        cz[brick, :, :, ROWS:] = edge.astype(jnp.bfloat16)
    cys[0] = cz[1].astype(jnp.float32)[:, EDGE - 1].astype(jnp.bfloat16)
    cys[1] = cz[0].astype(jnp.float32)[:, 0].astype(jnp.bfloat16)
    start_halo(c_copies)

    cot_rows = []
    zero_plane = jnp.zeros((EDGE, PAIR), jnp.float32)
    for k in range(PAIRS):
        per_tap = []
        blocks = [
            c_ref[0, brick, :, :, k * PAIR : (k + 1) * PAIR].astype(jnp.float32).reshape(EDGE * EDGE, PAIR)
            for brick in range(2)
        ]
        for a in range(3):
            pieces = []
            for brick in range(2):
                pieces += [zero_plane] * a + [blocks[brick]] + [zero_plane] * (2 - a)
            per_tap.append(jnp.concatenate(pieces, axis=0))
        cot_rows.append(jnp.concatenate(per_tap, axis=1))
    ct[...] = jnp.concatenate(cot_rows, axis=0).T.astype(jnp.bfloat16)

    wait_halo(f_copies)

    def stack(values, x_ref, width):
        parts = []
        for brick in range(2):
            parts.append(x_ref[0, brick].astype(jnp.float32)[None, :, :width])
            parts.append(values[brick])
            parts.append(x_ref[1, brick].astype(jnp.float32)[None, :, :width])
        return jnp.concatenate(parts, axis=0)

    center = stack([f_ref[0, b].astype(jnp.float32) for b in range(2)], fx, ROWS)
    row_low, row_high = outer_rows(center, fy, ROWS)

    def third_edge(values):
        pieces = []
        half = planes // 2
        for brick in range(2):
            other = values[(1 - brick) * half : (2 - brick) * half]
            before = jnp.where(nb_ref[0, brick, 4] >= 0, 1.0, 0.0)
            after = jnp.where(nb_ref[0, brick, 5] >= 0, 1.0, 0.0)
            low = low_lanes((half, values.shape[1], PAIR))
            pieces.append(
                jnp.where(low, other[..., :PAIR] * after, other[..., ROWS - PAIR :] * before)
            )
        return jnp.concatenate(pieces, axis=0)

    build_features = window_builder(
        xw, center, third_edge(center), row_low, row_high, third_edge(row_low), third_edge(row_high)
    )

    low = low_lanes((CH, PAIR))
    first_taps = []
    for b in range(3):
        build_features(b)
        grad = jnp.dot(
            ct[...], xw[:, b * 4 * CH : (b + 1) * 4 * CH], preferred_element_type=jnp.float32
        )
        for a in range(3):
            cell0 = grad[a * PAIR : a * PAIR + CH]
            cell1 = grad[a * PAIR + CH : (a + 1) * PAIR]
            turned0 = pltpu.roll(cell1[:, :PAIR], CH, 1)
            turned1 = pltpu.roll(cell1[:, PAIR:], CH, 1)
            part[b * 3 + a] = cell0[:, PAIR:] + jnp.where(low, turned1, turned0)
            first_taps.append(cell0[:, :PAIR] + turned1)
    for m in range(5):
        high = first_taps[2 * m + 1] if 2 * m + 1 < 9 else jnp.zeros((CH, PAIR), jnp.float32)
        part[9 + m] = jnp.where(low, pltpu.roll(first_taps[2 * m], CH, 1), high)

    if reduce_here:
        core_copy = pltpu.make_async_remote_copy(
            src_ref=part.at[pl.ds((1 - core) * OWNED, OWNED)], dst_ref=core_in,
            send_sem=core_sem.at[0], recv_sem=core_sem.at[1],
            device_id={"dp": 1 - core}, device_id_type=MESH,
        )
        core_copy.start()

    loads[3].wait()
    order = (3, 0, 1, 2)
    blank = jnp.zeros((CH, CH), jnp.bfloat16)
    for a in range(3):
        for b in range(3):
            taps = [w_ref[a, b, d] for d in range(3)]
            for slot, w in enumerate(order):
                left = taps[w] if w < 3 else blank
                right = taps[w - 1] if w > 0 else blank
                row = b * 4 * CH + slot * CH
                wf[row : row + CH, a * PAIR : (a + 1) * PAIR] = jnp.concatenate([left, right], axis=1)
            flip_a, flip_b = 2 - a, 2 - b
            for cell in range(2):
                row = flip_a * PAIR + cell * CH
                for half in range(2):
                    pieces = []
                    for w in order[2 * half : 2 * half + 2]:
                        d = w - cell
                        pieces.append(taps[2 - d] if 0 <= d <= 2 else blank)
                    lane = flip_b * 4 * CH + half * PAIR
                    wg[row : row + CH, lane : lane + PAIR] = jnp.concatenate(pieces, axis=1)

    if reduce_here:
        core_copy.wait()
        for tile in range(OWNED):
            sbuf[tile] = (part[core * OWNED + tile] + core_in[tile]).astype(jnp.bfloat16)

        def scatter_copy(step):
            target = (me + step) % count
            return target, pltpu.make_async_remote_copy(
                src_ref=sbuf.at[target], dst_ref=rbuf.at[me],
                send_sem=rs_send.at[step], recv_sem=rs_recv.at[me],
                device_id={"space": target}, device_id_type=MESH,
            )

        for step in range(1, count):
            target, copy = scatter_copy(step)
            pl.when(target < OWNED)(copy.start)

        @pl.when(me < OWNED)
        def _():
            rbuf[me] = sbuf[me]

    result = jnp.dot(xw[...], wf[...], preferred_element_type=jnp.float32)

    def put_response(brick, k, value):
        resp_ref[0, brick, :, :, k * PAIR : (k + 1) * PAIR] = value

    sum_taps(result, planes, put_response)

    wait_halo(c_copies)
    wide = stack([cz[b].astype(jnp.float32) for b in range(2)], cx, WIDE)
    wide_low, wide_high = outer_rows(wide, cy, WIDE)
    build_cotangent = window_builder(
        cw, wide[..., :ROWS], wide[..., ROWS:], wide_low[..., :ROWS], wide_high[..., :ROWS],
        wide_low[..., ROWS:], wide_high[..., ROWS:],
    )
    for tap in range(3):
        build_cotangent(tap)

    if reduce_here:
        for step in range(1, count):
            target, copy = scatter_copy(step)
            pl.when(target < OWNED)(copy.wait_send)

        def gather_copy(step):
            target = (me + step) % count
            return pltpu.make_async_remote_copy(
                src_ref=fin.at[core * OWNED + me], dst_ref=fin.at[core * OWNED + me],
                send_sem=ag_send.at[step], recv_sem=ag_recv.at[me],
                device_id={"space": target}, device_id_type=MESH,
            )

        def forward_copy(tile):
            spot = fin.at[core * OWNED + tile]
            return pltpu.make_async_remote_copy(
                src_ref=spot, dst_ref=spot,
                send_sem=fw_send.at[tile], recv_sem=fw_recv.at[tile],
                device_id={"dp": 1 - core}, device_id_type=MESH,
            )

        @pl.when(me < OWNED)
        def _():
            total = jnp.zeros((CH, PAIR), jnp.float32)
            for source in range(count):

                @pl.when(me != source)
                def _():
                    pltpu.make_async_remote_copy(
                        src_ref=sbuf.at[0], dst_ref=rbuf.at[source],
                        send_sem=rs_send.at[0], recv_sem=rs_recv.at[source],
                        device_id={"space": source}, device_id_type=MESH,
                    ).wait_recv()

                total = total + rbuf[source].astype(jnp.float32)
            fin[core * OWNED + me] = turn(total).astype(jnp.bfloat16)
            for step in range(1, count):
                gather_copy(step).start()

    result = lax.dot_general(
        cw[...], wg[...], (((1,), (1,)), ((), ())), preferred_element_type=jnp.float32
    )

    def put_gradient(brick, k, value):
        fg_ref[0, brick, :, :, k * PAIR : (k + 1) * PAIR] = value

    sum_taps(result, planes, put_gradient)

    if reduce_here:
        for tile in range(OWNED):

            @pl.when(me != tile)
            def _():
                spot = fin.at[core * OWNED + tile]
                pltpu.make_async_remote_copy(
                    src_ref=spot, dst_ref=spot,
                    send_sem=ag_send.at[0], recv_sem=ag_recv.at[tile],
                    device_id={"space": tile}, device_id_type=MESH,
                ).wait_recv()

            forward_copy(tile).start()

        for tile in range(OWNED):
            spot = fin.at[(1 - core) * OWNED + tile]
            pltpu.make_async_remote_copy(
                src_ref=spot, dst_ref=spot,
                send_sem=fw_send.at[tile], recv_sem=fw_recv.at[tile],
                device_id={"dp": 1 - core}, device_id_type=MESH,
            ).wait_recv()
        for tile in range(OWNED):
            forward_copy(tile).wait_send()

        @pl.when(me < OWNED)
        def _():
            for step in range(1, count):
                gather_copy(step).wait_send()
    else:
        for tile in range(TILES):
            part[tile] = turn(part[tile])
    for sent, _, copy in f_copies + c_copies:
        pl.when(sent)(copy.wait_send)


def finish_body(scale, resp_ref, fg_ref, tiles_ref, resp_hbm, fg_hbm, kg_hbm, kg, sems):
    copies = [
        pltpu.make_async_copy(resp_ref, resp_hbm, sems.at[0]),
        pltpu.make_async_copy(fg_ref, fg_hbm, sems.at[1]),
    ]
    for copy in copies:
        copy.start()
    for a in range(3):
        for b in range(3):
            tap = b * 3 + a
            later = tiles_ref[tap].astype(jnp.float32) * scale
            first = tiles_ref[9 + tap // 2].astype(jnp.float32) * scale
            kg[a, b, 0] = first[:, tap % 2 * CH : (tap % 2 + 1) * CH]
            kg[a, b, 1] = later[:, :CH]
            kg[a, b, 2] = later[:, CH:]
        copies.append(pltpu.make_async_copy(kg.at[a], kg_hbm.at[a], sems.at[2 + a]))
        copies[-1].start()
    for copy in copies:
        copy.wait()


def body(features, cotangent, kernel, neighbours):
    count = lax.axis_size("space")
    dp_count = lax.axis_size("dp")
    reduce_here = count == 8 and dp_count == 2
    cells = features.shape[0] * features.shape[1] * dp_count * count * EDGE**3
    scale = 1.0 / math.sqrt(cells)
    bf16, f32 = jnp.bfloat16, jnp.float32
    planes = 2 * (EDGE + 2)
    rows = PAIRS * planes * EDGE
    dma = pltpu.SemaphoreType.DMA
    vmem = pl.BlockSpec(memory_space=pltpu.VMEM)
    hbm = pl.BlockSpec(memory_space=pltpu.HBM)
    part_shape = (TILES, CH, PAIR)
    response, feature_grad, tiles = pl.pallas_call(
        functools.partial(kernel_body, count, reduce_here),
        out_shape=(
            pltpu.VMEM(features.shape, bf16),
            pltpu.VMEM(features.shape, bf16),
            pltpu.VMEM(part_shape, bf16 if reduce_here else f32),
        ),
        in_specs=[hbm] * 4,
        out_specs=(vmem, vmem, vmem),
        scratch_shapes=[
            pltpu.SMEM(neighbours.shape, jnp.int32),
            pltpu.VMEM(features.shape, bf16),
            pltpu.VMEM(features.shape, bf16),
            pltpu.VMEM(kernel.shape, bf16),
            pltpu.VMEM((2, 2, EDGE, ROWS), bf16),
            pltpu.VMEM((2, 3, EDGE, ROWS), bf16),
            pltpu.VMEM((2, 2, EDGE, WIDE), bf16),
            pltpu.VMEM((2, 3, EDGE, WIDE), bf16),
            pltpu.VMEM((2, EDGE, ROWS), bf16),
            pltpu.VMEM((2, EDGE, WIDE), bf16),
            pltpu.VMEM((2, EDGE, EDGE, WIDE), bf16),
            pltpu.VMEM((rows, 12 * CH), bf16),
            pltpu.VMEM((rows, 12 * CH), bf16),
            pltpu.VMEM((6 * CH, rows), bf16),
            pltpu.VMEM((12 * CH, 6 * CH), bf16),
            pltpu.VMEM((6 * CH, 12 * CH), bf16),
            pltpu.VMEM(part_shape, f32),
            pltpu.VMEM((OWNED, CH, PAIR), f32),
            pltpu.VMEM((8, CH, PAIR), bf16),
            pltpu.VMEM((8, CH, PAIR), bf16),
            dma((4,)), dma((16,)), dma((16,)), dma((2,)), dma((8,)), dma((8,)),
            dma((8,)), dma((8,)), dma((8,)), dma((8,)),
        ],
        compiler_params=pltpu.CompilerParams(
            collective_id=0, has_side_effects=True, vmem_limit_bytes=40 * 1024 * 1024
        ),
        cost_estimate=pl.CostEstimate(flops=10**9, bytes_accessed=2 * 10**6, transcendentals=0),
    )(*(
        pltpu.with_memory_space_constraint(x, pltpu.HBM)
        for x in (neighbours, features, cotangent, kernel)
    ))
    if not reduce_here:
        tiles = lax.psum(tiles, ("space", "dp"))
    return pl.pallas_call(
        functools.partial(finish_body, scale),
        out_shape=(
            jax.ShapeDtypeStruct(features.shape, bf16),
            jax.ShapeDtypeStruct(features.shape, bf16),
            jax.ShapeDtypeStruct(kernel.shape, f32),
        ),
        in_specs=[vmem] * 3,
        out_specs=(hbm,) * 3,
        scratch_shapes=[pltpu.VMEM(kernel.shape, f32), dma((5,))],
        cost_estimate=pl.CostEstimate(flops=10**6, bytes_accessed=10**6, transcendentals=0),
    )(*(
        pltpu.with_memory_space_constraint(x, pltpu.VMEM)
        for x in (response, feature_grad, tiles)
    ))


def solution(mesh):
    in_specs = (
        P(("groups", "dp"), "space", None, None, None),
        P(("groups", "dp"), "space", None, None, None),
        P(),
        P(("groups", "dp"), "space", None),
    )
    out_specs = (
        P(("groups", "dp"), "space", None, None, None),
        P(("groups", "dp"), "space", None, None, None),
        P("groups", None, None, None, None),
    )
    return jax.shard_map(body, mesh=mesh, in_specs=in_specs, out_specs=out_specs, check_vma=False)
```

```python
import functools
import math

import jax
import jax.numpy as jnp
from jax import lax
from jax.experimental import pallas as pl
from jax.experimental.pallas import tpu as pltpu
from jax.sharding import PartitionSpec as P

TILES_Y = 4
EDGE = 8
CH = 64
PAIR = 2 * CH
PAIRS = EDGE // 2
ROWS = EDGE * CH
WIDE = ROWS + PAIR
TILES = 14
OWNED = TILES // 2
MESH = pl.DeviceIdType.MESH
BATCHES = ((0, 2), (2, 4), (4, 7))
READY = (
    [("late", 0), ("late", 1), ("late", 2), ("early", 0)]
    + [("late", 3), ("late", 4), ("late", 5), ("early", 1)]
    + [("early", 2), ("late", 6), ("late", 7), ("late", 8), ("early", 3), ("early", 4)]
)
SPOT = {name: number % 2 * OWNED + number // 2 for number, name in enumerate(READY)}
DIAGONALS = [(side, dx) for side in range(2) for dx in range(3)]


def low_lanes(shape):
    return lax.broadcasted_iota(jnp.int32, shape, len(shape) - 1) < CH


def in_range(tile, count):
    return (tile >= 0) & (tile < count)


def receives(tile, dx, dy, count, first_x):
    column = (tile + TILES_Y // 2) % TILES_Y + dy
    there = in_range(tile + TILES_Y * dx + dy, count) & (column >= 0) & (column < TILES_Y)
    between = tile + TILES_Y * dx if first_x else tile + dy
    return in_range(tile, count) & in_range(between, count) & there


def place_windows(store, center, edge):
    low = low_lanes((center.shape[0], PAIR))
    pairs = [center[:, PAIR * k : PAIR * (k + 1)] for k in range(PAIRS)]
    for k in range(PAIRS):
        after = pairs[k + 1] if k + 1 < PAIRS else edge
        before = pairs[k - 1] if k > 0 else edge
        store(k, jnp.where(low, after, before), pairs[k])


def window_builder(out_ref, center, edge, halo_low, halo_high, edge_low, edge_high):
    planes = center.shape[0]

    def flat(values):
        return values.reshape(planes * EDGE, values.shape[-1])

    def shifted(values, low_row, high_row, tap):
        if tap == 0:
            return jnp.concatenate([low_row, values[:, : EDGE - 1]], axis=1)
        if tap == 2:
            return jnp.concatenate([values[:, 1:], high_row], axis=1)
        return values

    def build(tap):
        moved = flat(shifted(center, halo_low, halo_high, tap))
        moved_edge = flat(shifted(edge, edge_low, edge_high, tap))

        def store(k, around, pair):
            rows = pl.ds(k * planes * EDGE, planes * EDGE)
            base = tap * 2 * PAIR
            out_ref[rows, base : base + PAIR] = around.astype(jnp.bfloat16)
            out_ref[rows, base + PAIR : base + 2 * PAIR] = pair.astype(jnp.bfloat16)

        place_windows(store, moved, moved_edge)

    return build


def outer_rows(center, y_ref, width):
    low, high = [], []
    for side in range(2):
        below = y_ref[side, 0].astype(jnp.float32)[EDGE - 1 :, None, :width]
        level = y_ref[side, 1].astype(jnp.float32)[:, None, :width]
        above = y_ref[side, 2].astype(jnp.float32)[:1, None, :width]
        (low if side == 0 else high).extend([below, level, above])
    planes = EDGE + 2
    low.append(center[:planes, EDGE - 1 :])
    high = [center[planes:, :1]] + high
    return jnp.concatenate(low, axis=0), jnp.concatenate(high, axis=0)


def sum_taps(result, planes, store):
    for k in range(PAIRS):
        for brick in range(2):
            base = k * planes * EDGE + brick * (planes // 2) * EDGE
            total = result[base : base + EDGE * EDGE, :PAIR]
            for a in range(1, 3):
                start = base + a * EDGE
                total = total + result[start : start + EDGE * EDGE, a * PAIR : (a + 1) * PAIR]
            store(brick, k, total.reshape(EDGE, EDGE, PAIR).astype(jnp.bfloat16))


def turn(tile):
    turned = tile.T
    return jnp.concatenate([turned[:CH], turned[CH:]], axis=1)


def kernel_body(
    count, reduce_here,
    nb_hbm, f_hbm, c_hbm, w_hbm,
    resp_ref, fg_ref, tiles_ref,
    nb_ref, f_ref, c_ref, w_ref,
    fx, fy, cx, cy, fys, cys, cz, xw, cw, ct, wf, wg, part, core_in, sbuf, rbuf,
    load_sem, halo_send, halo_recv, core_send, core_recv, rs_send, rs_recv, ag_send, ag_recv, fw_send, fw_recv,
):
    me = lax.axis_index("space")
    core = lax.axis_index("dp")
    planes = 2 * (EDGE + 2)

    if reduce_here:
        fin = tiles_ref
    else:
        part = tiles_ref
    loads = [
        pltpu.make_async_copy(src, dst, load_sem.at[number])
        for number, (src, dst) in enumerate(
            [(f_hbm, f_ref), (c_hbm, c_ref), (nb_hbm, nb_ref), (w_hbm, w_ref)]
        )
    ]
    for load in loads:
        load.start()

    fx[...] = jnp.zeros_like(fx)
    fy[...] = jnp.zeros_like(fy)
    cx[...] = jnp.zeros_like(cx)
    cy[...] = jnp.zeros_like(cy)

    barrier = pltpu.get_barrier_semaphore()
    if reduce_here:
        for step in range(1, count):
            pl.semaphore_signal(
                barrier, inc=1, device_id={"space": (me + step) % count}, device_id_type=MESH
            )
        pl.semaphore_signal(barrier, inc=1, device_id={"dp": 1 - core}, device_id_type=MESH)
    else:
        for step in (1, 3, 4, 5):
            for other in (me + step, me - step):

                @pl.when(in_range(other, count))
                def _():
                    pl.semaphore_signal(
                        barrier, inc=1, device_id={"space": other}, device_id_type=MESH
                    )

    def halo(kind):
        x_ref, y_ref, ys_ref = ((fx, fy, fys), (cx, cy, cys))[kind]
        entries = []
        for side in range(2):
            dx = 2 * side - 1
            target = me - TILES_Y * dx
            face = EDGE - 1 if side == 0 else 0
            source = f_ref.at[0, :, face] if kind == 0 else cz.at[:, face]
            entries.append((
                receives(target, dx, 0, count, True),
                receives(me, dx, 0, count, True),
                source, x_ref.at[side], target,
            ))
        for side, column in DIAGONALS:
            dx, dy = column - 1, 2 * side - 1
            target = me - TILES_Y * dx - dy
            entries.append((
                receives(target, dx, dy, count, kind == 1),
                receives(me, dx, dy, count, kind == 1),
                ys_ref.at[side], y_ref.at[side, column], target,
            ))
        out = []
        for number, (sent, arrives, source, target_ref, target) in enumerate(entries):
            out.append((sent, arrives, pltpu.make_async_remote_copy(
                src_ref=source, dst_ref=target_ref,
                send_sem=halo_send.at[kind * 8 + number],
                recv_sem=halo_recv.at[kind * 8 + number],
                device_id={"space": target}, device_id_type=MESH,
            )))
        return out

    def start_halo(copies):
        for sent, _, copy in copies:
            pl.when(sent)(copy.start)

    def wait_halo(copies):
        for _, arrives, copy in copies:
            pl.when(arrives)(copy.wait_recv)

    loads[0].wait()
    fys[0] = f_ref[0, 1].astype(jnp.float32)[:, EDGE - 1].astype(jnp.bfloat16)
    fys[1] = f_ref[0, 0].astype(jnp.float32)[:, 0].astype(jnp.bfloat16)

    if reduce_here:
        pl.semaphore_wait(barrier, count)
    else:
        for step in (1, 3, 4, 5):
            for other in (me + step, me - step):

                @pl.when(in_range(other, count))
                def _():
                    pl.semaphore_wait(barrier, 1)

    f_copies, c_copies = halo(0), halo(1)
    start_halo(f_copies)

    loads[1].wait()
    loads[2].wait()
    for brick in range(2):
        other = 1 - brick
        before = jnp.where(nb_ref[0, brick, 4] >= 0, 1.0, 0.0)
        after = jnp.where(nb_ref[0, brick, 5] >= 0, 1.0, 0.0)
        cz[brick, :, :, :ROWS] = c_ref[0, brick]
        low = low_lanes((EDGE, EDGE, PAIR))
        edge = jnp.where(
            low,
            c_ref[0, other, :, :, :PAIR].astype(jnp.float32) * after,
            c_ref[0, other, :, :, ROWS - PAIR :].astype(jnp.float32) * before,
        )
        cz[brick, :, :, ROWS:] = edge.astype(jnp.bfloat16)
    cys[0] = cz[1].astype(jnp.float32)[:, EDGE - 1].astype(jnp.bfloat16)
    cys[1] = cz[0].astype(jnp.float32)[:, 0].astype(jnp.bfloat16)
    start_halo(c_copies)

    cot_rows = []
    zero_plane = jnp.zeros((EDGE, PAIR), jnp.float32)
    for k in range(PAIRS):
        per_tap = []
        blocks = [
            c_ref[0, brick, :, :, k * PAIR : (k + 1) * PAIR].astype(jnp.float32).reshape(EDGE * EDGE, PAIR)
            for brick in range(2)
        ]
        for a in range(3):
            pieces = []
            for brick in range(2):
                pieces += [zero_plane] * a + [blocks[brick]] + [zero_plane] * (2 - a)
            per_tap.append(jnp.concatenate(pieces, axis=0))
        cot_rows.append(jnp.concatenate(per_tap, axis=1))
    ct[...] = jnp.concatenate(cot_rows, axis=0).T.astype(jnp.bfloat16)

    wait_halo(f_copies)

    def stack(values, x_ref, width):
        parts = []
        for brick in range(2):
            parts.append(x_ref[0, brick].astype(jnp.float32)[None, :, :width])
            parts.append(values[brick])
            parts.append(x_ref[1, brick].astype(jnp.float32)[None, :, :width])
        return jnp.concatenate(parts, axis=0)

    center = stack([f_ref[0, b].astype(jnp.float32) for b in range(2)], fx, ROWS)
    row_low, row_high = outer_rows(center, fy, ROWS)

    def third_edge(values):
        pieces = []
        half = planes // 2
        for brick in range(2):
            other = values[(1 - brick) * half : (2 - brick) * half]
            before = jnp.where(nb_ref[0, brick, 4] >= 0, 1.0, 0.0)
            after = jnp.where(nb_ref[0, brick, 5] >= 0, 1.0, 0.0)
            low = low_lanes((half, values.shape[1], PAIR))
            pieces.append(
                jnp.where(low, other[..., :PAIR] * after, other[..., ROWS - PAIR :] * before)
            )
        return jnp.concatenate(pieces, axis=0)

    build_features = window_builder(
        xw, center, third_edge(center), row_low, row_high, third_edge(row_low), third_edge(row_high)
    )

    low = low_lanes((CH, PAIR))
    core_copies = [
        pltpu.make_async_remote_copy(
            src_ref=part.at[pl.ds((1 - core) * OWNED + first, last - first)],
            dst_ref=core_in.at[pl.ds(first, last - first)],
            send_sem=core_send.at[batch], recv_sem=core_recv.at[batch],
            device_id={"dp": 1 - core}, device_id_type=MESH,
        )
        for batch, (first, last) in enumerate(BATCHES)
    ] if reduce_here else []

    def scatter_copy(tile):
        return pltpu.make_async_remote_copy(
            src_ref=sbuf.at[tile], dst_ref=rbuf.at[me],
            send_sem=rs_send.at[tile], recv_sem=rs_recv.at[me],
            device_id={"space": tile}, device_id_type=MESH,
        )

    def scatter(batch):
        core_copies[batch].wait_recv()
        for tile in range(*BATCHES[batch]):
            total = part[core * OWNED + tile] + core_in[tile]
            sbuf[tile] = total.astype(jnp.bfloat16)
            pl.when(me != tile)(scatter_copy(tile).start)

    first_taps = []
    for b in range(3):
        build_features(b)
        grad = jnp.dot(
            ct[...], xw[:, b * 4 * CH : (b + 1) * 4 * CH], preferred_element_type=jnp.float32
        )
        for a in range(3):
            cell0 = grad[a * PAIR : a * PAIR + CH]
            cell1 = grad[a * PAIR + CH : (a + 1) * PAIR]
            turned0 = pltpu.roll(cell1[:, :PAIR], CH, 1)
            turned1 = pltpu.roll(cell1[:, PAIR:], CH, 1)
            tap = b * 3 + a
            part[SPOT["late", tap]] = cell0[:, PAIR:] + jnp.where(low, turned1, turned0)
            first_taps.append(cell0[:, :PAIR] + turned1)
            if tap % 2 == 1 or tap == 8:
                pair = first_taps[tap - tap % 2 :] + [jnp.zeros((CH, PAIR), jnp.float32)]
                part[SPOT["early", tap // 2]] = jnp.where(low, pltpu.roll(pair[0], CH, 1), pair[1])
        if reduce_here:
            core_copies[b].start()
            if b > 0:
                scatter(b - 1)

    loads[3].wait()
    order = (3, 0, 1, 2)
    blank = jnp.zeros((CH, CH), jnp.bfloat16)
    for a in range(3):
        for b in range(3):
            taps = [w_ref[a, b, d] for d in range(3)]
            for slot, w in enumerate(order):
                left = taps[w] if w < 3 else blank
                right = taps[w - 1] if w > 0 else blank
                row = b * 4 * CH + slot * CH
                wf[row : row + CH, a * PAIR : (a + 1) * PAIR] = jnp.concatenate([left, right], axis=1)
            flip_a, flip_b = 2 - a, 2 - b
            for cell in range(2):
                row = flip_a * PAIR + cell * CH
                for half in range(2):
                    pieces = []
                    for w in order[2 * half : 2 * half + 2]:
                        d = w - cell
                        pieces.append(taps[2 - d] if 0 <= d <= 2 else blank)
                    lane = flip_b * 4 * CH + half * PAIR
                    wg[row : row + CH, lane : lane + PAIR] = jnp.concatenate(pieces, axis=1)

    if reduce_here:
        scatter(2)

        @pl.when(me < OWNED)
        def _():
            rbuf[me] = sbuf[me]

    result = jnp.dot(xw[...], wf[...], preferred_element_type=jnp.float32)

    def put_response(brick, k, value):
        resp_ref[0, brick, :, :, k * PAIR : (k + 1) * PAIR] = value

    sum_taps(result, planes, put_response)

    wait_halo(c_copies)
    wide = stack([cz[b].astype(jnp.float32) for b in range(2)], cx, WIDE)
    wide_low, wide_high = outer_rows(wide, cy, WIDE)
    build_cotangent = window_builder(
        cw, wide[..., :ROWS], wide[..., ROWS:], wide_low[..., :ROWS], wide_high[..., :ROWS],
        wide_low[..., ROWS:], wide_high[..., ROWS:],
    )
    for tap in range(3):
        build_cotangent(tap)

    if reduce_here:
        def gather_copy(step):
            target = (me + step) % count
            return pltpu.make_async_remote_copy(
                src_ref=fin.at[core * OWNED + me], dst_ref=fin.at[core * OWNED + me],
                send_sem=ag_send.at[step], recv_sem=ag_recv.at[me],
                device_id={"space": target}, device_id_type=MESH,
            )

        def forward_copy(tile):
            spot = fin.at[core * OWNED + tile]
            return pltpu.make_async_remote_copy(
                src_ref=spot, dst_ref=spot,
                send_sem=fw_send.at[tile], recv_sem=fw_recv.at[tile],
                device_id={"dp": 1 - core}, device_id_type=MESH,
            )

        @pl.when(me < OWNED)
        def _():
            total = jnp.zeros((CH, PAIR), jnp.float32)
            for source in range(count):

                @pl.when(me != source)
                def _():
                    pltpu.make_async_remote_copy(
                        src_ref=sbuf.at[0], dst_ref=rbuf.at[source],
                        send_sem=rs_send.at[0], recv_sem=rs_recv.at[source],
                        device_id={"space": source}, device_id_type=MESH,
                    ).wait_recv()

                total = total + rbuf[source].astype(jnp.float32)
            fin[core * OWNED + me] = turn(total).astype(jnp.bfloat16)
            for step in range(1, count):
                gather_copy(step).start()

    result = lax.dot_general(
        cw[...], wg[...], (((1,), (1,)), ((), ())), preferred_element_type=jnp.float32
    )

    def put_gradient(brick, k, value):
        fg_ref[0, brick, :, :, k * PAIR : (k + 1) * PAIR] = value

    sum_taps(result, planes, put_gradient)

    if reduce_here:
        for tile in range(OWNED):

            @pl.when(me != tile)
            def _():
                spot = fin.at[core * OWNED + tile]
                pltpu.make_async_remote_copy(
                    src_ref=spot, dst_ref=spot,
                    send_sem=ag_send.at[0], recv_sem=ag_recv.at[tile],
                    device_id={"space": tile}, device_id_type=MESH,
                ).wait_recv()

            forward_copy(tile).start()

        for tile in range(OWNED):
            spot = fin.at[(1 - core) * OWNED + tile]
            pltpu.make_async_remote_copy(
                src_ref=spot, dst_ref=spot,
                send_sem=fw_send.at[tile], recv_sem=fw_recv.at[tile],
                device_id={"dp": 1 - core}, device_id_type=MESH,
            ).wait_recv()
        for tile in range(OWNED):
            forward_copy(tile).wait_send()

        @pl.when(me < OWNED)
        def _():
            for step in range(1, count):
                gather_copy(step).wait_send()
    else:
        for tile in range(TILES):
            part[tile] = turn(part[tile])
    if reduce_here:
        for copy in core_copies:
            copy.wait_send()
        for tile in range(OWNED):
            pl.when(me != tile)(scatter_copy(tile).wait_send)
    for sent, _, copy in f_copies + c_copies:
        pl.when(sent)(copy.wait_send)


def finish_body(scale, resp_ref, fg_ref, tiles_ref, resp_hbm, fg_hbm, kg_hbm, kg, sems):
    copies = [
        pltpu.make_async_copy(resp_ref, resp_hbm, sems.at[0]),
        pltpu.make_async_copy(fg_ref, fg_hbm, sems.at[1]),
    ]
    for copy in copies:
        copy.start()
    for a in range(3):
        for b in range(3):
            tap = b * 3 + a
            later = tiles_ref[SPOT["late", tap]].astype(jnp.float32) * scale
            first = tiles_ref[SPOT["early", tap // 2]].astype(jnp.float32) * scale
            kg[a, b, 0] = first[:, tap % 2 * CH : (tap % 2 + 1) * CH]
            kg[a, b, 1] = later[:, :CH]
            kg[a, b, 2] = later[:, CH:]
        copies.append(pltpu.make_async_copy(kg.at[a], kg_hbm.at[a], sems.at[2 + a]))
        copies[-1].start()
    for copy in copies:
        copy.wait()


def body(features, cotangent, kernel, neighbours):
    count = lax.axis_size("space")
    dp_count = lax.axis_size("dp")
    reduce_here = count == 8 and dp_count == 2
    cells = features.shape[0] * features.shape[1] * dp_count * count * EDGE**3
    scale = 1.0 / math.sqrt(cells)
    bf16, f32 = jnp.bfloat16, jnp.float32
    planes = 2 * (EDGE + 2)
    rows = PAIRS * planes * EDGE
    dma = pltpu.SemaphoreType.DMA
    vmem = pl.BlockSpec(memory_space=pltpu.VMEM)
    hbm = pl.BlockSpec(memory_space=pltpu.HBM)
    part_shape = (TILES, CH, PAIR)
    response, feature_grad, tiles = pl.pallas_call(
        functools.partial(kernel_body, count, reduce_here),
        out_shape=(
            pltpu.VMEM(features.shape, bf16),
            pltpu.VMEM(features.shape, bf16),
            pltpu.VMEM(part_shape, bf16 if reduce_here else f32),
        ),
        in_specs=[hbm] * 4,
        out_specs=(vmem, vmem, vmem),
        scratch_shapes=[
            pltpu.SMEM(neighbours.shape, jnp.int32),
            pltpu.VMEM(features.shape, bf16),
            pltpu.VMEM(features.shape, bf16),
            pltpu.VMEM(kernel.shape, bf16),
            pltpu.VMEM((2, 2, EDGE, ROWS), bf16),
            pltpu.VMEM((2, 3, EDGE, ROWS), bf16),
            pltpu.VMEM((2, 2, EDGE, WIDE), bf16),
            pltpu.VMEM((2, 3, EDGE, WIDE), bf16),
            pltpu.VMEM((2, EDGE, ROWS), bf16),
            pltpu.VMEM((2, EDGE, WIDE), bf16),
            pltpu.VMEM((2, EDGE, EDGE, WIDE), bf16),
            pltpu.VMEM((rows, 12 * CH), bf16),
            pltpu.VMEM((rows, 12 * CH), bf16),
            pltpu.VMEM((6 * CH, rows), bf16),
            pltpu.VMEM((12 * CH, 6 * CH), bf16),
            pltpu.VMEM((6 * CH, 12 * CH), bf16),
            pltpu.VMEM(part_shape, f32),
            pltpu.VMEM((OWNED, CH, PAIR), f32),
            pltpu.VMEM((8, CH, PAIR), bf16),
            pltpu.VMEM((8, CH, PAIR), bf16),
            dma((4,)), dma((16,)), dma((16,)), dma((3,)), dma((3,)), dma((8,)), dma((8,)),
            dma((8,)), dma((8,)), dma((8,)), dma((8,)),
        ],
        compiler_params=pltpu.CompilerParams(
            collective_id=0, has_side_effects=True, vmem_limit_bytes=40 * 1024 * 1024
        ),
        cost_estimate=pl.CostEstimate(flops=10**9, bytes_accessed=2 * 10**6, transcendentals=0),
    )(*(
        pltpu.with_memory_space_constraint(x, pltpu.HBM)
        for x in (neighbours, features, cotangent, kernel)
    ))
    if not reduce_here:
        tiles = lax.psum(tiles, ("space", "dp"))
    return pl.pallas_call(
        functools.partial(finish_body, scale),
        out_shape=(
            jax.ShapeDtypeStruct(features.shape, bf16),
            jax.ShapeDtypeStruct(features.shape, bf16),
            jax.ShapeDtypeStruct(kernel.shape, f32),
        ),
        in_specs=[vmem] * 3,
        out_specs=(hbm,) * 3,
        scratch_shapes=[pltpu.VMEM(kernel.shape, f32), dma((5,))],
        cost_estimate=pl.CostEstimate(flops=10**6, bytes_accessed=10**6, transcendentals=0),
    )(*(
        pltpu.with_memory_space_constraint(x, pltpu.VMEM)
        for x in (response, feature_grad, tiles)
    ))


def solution(mesh):
    in_specs = (
        P(("groups", "dp"), "space", None, None, None),
        P(("groups", "dp"), "space", None, None, None),
        P(),
        P(("groups", "dp"), "space", None),
    )
    out_specs = (
        P(("groups", "dp"), "space", None, None, None),
        P(("groups", "dp"), "space", None, None, None),
        P("groups", None, None, None, None),
    )
    return jax.shard_map(body, mesh=mesh, in_specs=in_specs, out_specs=out_specs, check_vma=False)
```

```python
import functools
import math

import jax
import jax.numpy as jnp
from jax import lax
from jax.experimental import pallas as pl
from jax.experimental.pallas import tpu as pltpu
from jax.sharding import PartitionSpec as P

TILES_Y = 4
EDGE = 8
CH = 64
PAIR = 2 * CH
PAIRS = EDGE // 2
ROWS = EDGE * CH
WIDE = ROWS + PAIR
TILES = 14
OWNED = TILES // 2
MESH = pl.DeviceIdType.MESH
BATCHES = ((0, 2), (2, 4), (4, 7))
READY = (
    [("late", 0), ("late", 1), ("late", 2), ("early", 0)]
    + [("late", 3), ("late", 4), ("late", 5), ("early", 1)]
    + [("early", 2), ("late", 6), ("late", 7), ("late", 8), ("early", 3), ("early", 4)]
)
SPOT = {name: number % 2 * OWNED + number // 2 for number, name in enumerate(READY)}
DIAGONALS = [(side, dx) for side in range(2) for dx in range(3)]


def low_lanes(shape):
    return lax.broadcasted_iota(jnp.int32, shape, len(shape) - 1) < CH


def in_range(tile, count):
    return (tile >= 0) & (tile < count)


def receives(tile, dx, dy, count, first_x):
    column = (tile + TILES_Y // 2) % TILES_Y + dy
    there = in_range(tile + TILES_Y * dx + dy, count) & (column >= 0) & (column < TILES_Y)
    between = tile + TILES_Y * dx if first_x else tile + dy
    return in_range(tile, count) & in_range(between, count) & there


def window_builder(out_ref, center, edge, halo_low, halo_high, edge_low, edge_high):
    def shifted(values, low_row, high_row, tap):
        if tap == 0:
            return jnp.concatenate([low_row, values[:, :, : EDGE - 1]], axis=2)
        if tap == 2:
            return jnp.concatenate([values[:, :, 1:], high_row], axis=2)
        return values

    def build(tap):
        moved = shifted(center, halo_low, halo_high, tap)
        outer = shifted(edge, edge_low, edge_high, tap)
        low = low_lanes(outer.shape)
        pairs = [moved[..., PAIR * k : PAIR * (k + 1)] for k in range(PAIRS)]
        around = []
        for k in range(PAIRS):
            after = pairs[k + 1] if k + 1 < PAIRS else outer
            before = pairs[k - 1] if k > 0 else outer
            around.append(jnp.where(low, after, before))
        for half, pieces in enumerate((around, pairs)):
            rows = jnp.stack(pieces, axis=2).reshape(-1, PAIR).astype(jnp.bfloat16)
            base = (2 * tap + half) * PAIR
            out_ref[:, base : base + PAIR] = rows

    return build


def outer_rows(center, y_ref, width):
    sides = []
    for side in range(2):
        below = y_ref[side, 0].astype(jnp.float32)[EDGE - 1 :, None, :width]
        level = y_ref[side, 1].astype(jnp.float32)[:, None, :width]
        above = y_ref[side, 2].astype(jnp.float32)[:1, None, :width]
        sides.append(jnp.concatenate([below, level, above], axis=0))
    low = jnp.stack([sides[0], center[:, 0, EDGE - 1 :]], axis=1)
    high = jnp.stack([center[:, 1, :1], sides[1]], axis=1)
    return low, high


def sum_taps(result, store):
    step = 2 * PAIRS * EDGE
    count = EDGE * step
    total = result[:count, :PAIR]
    for a in range(1, 3):
        total = total + result[a * step : a * step + count, a * PAIR : (a + 1) * PAIR]
    total = total.reshape(EDGE, 2, PAIRS, EDGE, PAIR).astype(jnp.bfloat16)
    for brick in range(2):
        for k in range(PAIRS):
            store(brick, k, total[:, brick, k])


def turn(tile):
    turned = tile.T
    return jnp.concatenate([turned[:CH], turned[CH:]], axis=1)


def kernel_body(
    count, reduce_here,
    nb_hbm, f_hbm, c_hbm, w_hbm,
    resp_ref, fg_ref, tiles_ref,
    nb_ref, f_ref, c_ref, w_ref,
    fx, fy, cx, cy, fys, cys, cz, xw, cw, ct, wf, wg, part, core_in, sbuf, rbuf,
    load_sem, halo_send, halo_recv, core_send, core_recv, rs_send, rs_recv, ag_send, ag_recv, fw_send, fw_recv,
):
    me = lax.axis_index("space")
    core = lax.axis_index("dp")
    if reduce_here:
        fin = tiles_ref
    else:
        part = tiles_ref
    loads = [
        pltpu.make_async_copy(src, dst, load_sem.at[number])
        for number, (src, dst) in enumerate(
            [(f_hbm, f_ref), (c_hbm, c_ref), (nb_hbm, nb_ref), (w_hbm, w_ref)]
        )
    ]
    for load in loads:
        load.start()

    fx[...] = jnp.zeros_like(fx)
    fy[...] = jnp.zeros_like(fy)
    cx[...] = jnp.zeros_like(cx)
    cy[...] = jnp.zeros_like(cy)

    barrier = pltpu.get_barrier_semaphore()
    if reduce_here:
        for step in range(1, count):
            pl.semaphore_signal(
                barrier, inc=1, device_id={"space": (me + step) % count}, device_id_type=MESH
            )
        pl.semaphore_signal(barrier, inc=1, device_id={"dp": 1 - core}, device_id_type=MESH)
    else:
        for step in (1, 3, 4, 5):
            for other in (me + step, me - step):

                @pl.when(in_range(other, count))
                def _():
                    pl.semaphore_signal(
                        barrier, inc=1, device_id={"space": other}, device_id_type=MESH
                    )

    def halo(kind):
        x_ref, y_ref, ys_ref = ((fx, fy, fys), (cx, cy, cys))[kind]
        entries = []
        for side in range(2):
            dx = 2 * side - 1
            target = me - TILES_Y * dx
            face = EDGE - 1 if side == 0 else 0
            source = f_ref.at[0, :, face] if kind == 0 else cz.at[:, face]
            entries.append((
                receives(target, dx, 0, count, True),
                receives(me, dx, 0, count, True),
                source, x_ref.at[side], target,
            ))
        for side, column in DIAGONALS:
            dx, dy = column - 1, 2 * side - 1
            target = me - TILES_Y * dx - dy
            entries.append((
                receives(target, dx, dy, count, kind == 1),
                receives(me, dx, dy, count, kind == 1),
                ys_ref.at[side], y_ref.at[side, column], target,
            ))
        out = []
        for number, (sent, arrives, source, target_ref, target) in enumerate(entries):
            out.append((sent, arrives, pltpu.make_async_remote_copy(
                src_ref=source, dst_ref=target_ref,
                send_sem=halo_send.at[kind * 8 + number],
                recv_sem=halo_recv.at[kind * 8 + number],
                device_id={"space": target}, device_id_type=MESH,
            )))
        return out

    def start_halo(copies):
        for sent, _, copy in copies:
            pl.when(sent)(copy.start)

    def wait_halo(copies):
        for _, arrives, copy in copies:
            pl.when(arrives)(copy.wait_recv)

    loads[0].wait()
    fys[0] = f_ref[0, 1].astype(jnp.float32)[:, EDGE - 1].astype(jnp.bfloat16)
    fys[1] = f_ref[0, 0].astype(jnp.float32)[:, 0].astype(jnp.bfloat16)

    if reduce_here:
        pl.semaphore_wait(barrier, count)
    else:
        for step in (1, 3, 4, 5):
            for other in (me + step, me - step):

                @pl.when(in_range(other, count))
                def _():
                    pl.semaphore_wait(barrier, 1)

    f_copies, c_copies = halo(0), halo(1)
    start_halo(f_copies)

    loads[1].wait()
    loads[2].wait()
    for brick in range(2):
        other = 1 - brick
        before = jnp.where(nb_ref[0, brick, 4] >= 0, 1.0, 0.0)
        after = jnp.where(nb_ref[0, brick, 5] >= 0, 1.0, 0.0)
        cz[brick, :, :, :ROWS] = c_ref[0, brick]
        low = low_lanes((EDGE, EDGE, PAIR))
        edge = jnp.where(
            low,
            c_ref[0, other, :, :, :PAIR].astype(jnp.float32) * after,
            c_ref[0, other, :, :, ROWS - PAIR :].astype(jnp.float32) * before,
        )
        cz[brick, :, :, ROWS:] = edge.astype(jnp.bfloat16)
    cys[0] = cz[1].astype(jnp.float32)[:, EDGE - 1].astype(jnp.bfloat16)
    cys[1] = cz[0].astype(jnp.float32)[:, 0].astype(jnp.bfloat16)
    start_halo(c_copies)

    loads[3].wait()
    blank = jnp.zeros((CH, CH), jnp.bfloat16)
    for a in range(3):
        for b in range(3):
            taps = [w_ref[a, b, d] for d in range(3)]
            for w, slot in enumerate((1, 2, 3, 0)):
                left = taps[w] if w < 3 else blank
                right = taps[w - 1] if w > 0 else blank
                block = jnp.concatenate([left, right], axis=1)
                row = (b * 4 + slot) * CH
                wf[row : row + CH, a * PAIR : (a + 1) * PAIR] = block
                cell, half = ((1, 0), (0, 1), (1, 1), (0, 0))[w]
                row = (2 - a) * PAIR + cell * CH
                lane = (2 - b) * 4 * CH + half * PAIR
                wg[row : row + CH, lane : lane + PAIR] = block

    pieces = []
    for k in range(PAIRS):
        lanes = slice(k * PAIR, (k + 1) * PAIR)
        pieces.append(
            jnp.stack([c_ref[0, b, :, :, lanes].astype(jnp.float32) for b in range(2)], axis=1)
        )
    turned = jnp.stack(pieces, axis=2).reshape(-1, PAIR).T
    step = 2 * PAIRS * EDGE
    for a in range(3):
        padded = [jnp.zeros((PAIR, a * step), jnp.float32)] if a > 0 else []
        padded.append(turned)
        if a < 2:
            padded.append(jnp.zeros((PAIR, (2 - a) * step), jnp.float32))
        ct[a * PAIR : (a + 1) * PAIR] = jnp.concatenate(padded, axis=1).astype(jnp.bfloat16)

    wait_halo(f_copies)

    def stack(values, x_ref, width):
        first = x_ref[0].astype(jnp.float32)[None, ..., :width]
        last = x_ref[1].astype(jnp.float32)[None, ..., :width]
        return jnp.concatenate([first, jnp.stack(values, axis=1), last], axis=0)

    center = stack([f_ref[0, b].astype(jnp.float32) for b in range(2)], fx, ROWS)
    row_low, row_high = outer_rows(center, fy, ROWS)

    def third_edge(values):
        pieces = []
        for brick in range(2):
            other = values[:, 1 - brick]
            before = jnp.where(nb_ref[0, brick, 4] >= 0, 1.0, 0.0)
            after = jnp.where(nb_ref[0, brick, 5] >= 0, 1.0, 0.0)
            low = low_lanes(other.shape[:-1] + (PAIR,))
            pieces.append(
                jnp.where(low, other[..., :PAIR] * after, other[..., ROWS - PAIR :] * before)
            )
        return jnp.stack(pieces, axis=1)

    build_features = window_builder(
        xw, center, third_edge(center), row_low, row_high, third_edge(row_low), third_edge(row_high)
    )

    low = low_lanes((CH, PAIR))
    core_copies = [
        pltpu.make_async_remote_copy(
            src_ref=part.at[pl.ds((1 - core) * OWNED + first, last - first)],
            dst_ref=core_in.at[pl.ds(first, last - first)],
            send_sem=core_send.at[batch], recv_sem=core_recv.at[batch],
            device_id={"dp": 1 - core}, device_id_type=MESH,
        )
        for batch, (first, last) in enumerate(BATCHES)
    ] if reduce_here else []

    def scatter_copy(tile):
        return pltpu.make_async_remote_copy(
            src_ref=sbuf.at[tile], dst_ref=rbuf.at[me],
            send_sem=rs_send.at[tile], recv_sem=rs_recv.at[me],
            device_id={"space": tile}, device_id_type=MESH,
        )

    def scatter(batch):
        core_copies[batch].wait_recv()
        for tile in range(*BATCHES[batch]):
            total = part[core * OWNED + tile] + core_in[tile]
            sbuf[tile] = total.astype(jnp.bfloat16)
            pl.when(me != tile)(scatter_copy(tile).start)

    first_taps = []
    for b in range(3):
        build_features(b)
        grad = jnp.dot(
            ct[...], xw[:, b * 4 * CH : (b + 1) * 4 * CH], preferred_element_type=jnp.float32
        )
        for a in range(3):
            cell0 = grad[a * PAIR : a * PAIR + CH]
            cell1 = grad[a * PAIR + CH : (a + 1) * PAIR]
            turned0 = pltpu.roll(cell1[:, :PAIR], CH, 1)
            turned1 = pltpu.roll(cell1[:, PAIR:], CH, 1)
            tap = b * 3 + a
            part[SPOT["late", tap]] = cell0[:, PAIR:] + jnp.where(low, turned1, turned0)
            first_taps.append(cell0[:, :PAIR] + turned1)
            if tap % 2 == 1 or tap == 8:
                pair = first_taps[tap - tap % 2 :] + [jnp.zeros((CH, PAIR), jnp.float32)]
                part[SPOT["early", tap // 2]] = jnp.where(low, pltpu.roll(pair[0], CH, 1), pair[1])
        if reduce_here:
            core_copies[b].start()
            if b > 0:
                scatter(b - 1)

    if reduce_here:
        scatter(2)

        @pl.when(me < OWNED)
        def _():
            rbuf[me] = sbuf[me]

    result = jnp.dot(xw[...], wf[...], preferred_element_type=jnp.float32)

    def put_response(brick, k, value):
        resp_ref[0, brick, :, :, k * PAIR : (k + 1) * PAIR] = value

    sum_taps(result, put_response)

    wait_halo(c_copies)
    wide = stack([cz[b].astype(jnp.float32) for b in range(2)], cx, WIDE)
    wide_low, wide_high = outer_rows(wide, cy, WIDE)
    build_cotangent = window_builder(
        cw, wide[..., :ROWS], wide[..., ROWS:], wide_low[..., :ROWS], wide_high[..., :ROWS],
        wide_low[..., ROWS:], wide_high[..., ROWS:],
    )
    for tap in range(3):
        build_cotangent(tap)

    if reduce_here:
        def gather_copy(step):
            target = (me + step) % count
            return pltpu.make_async_remote_copy(
                src_ref=fin.at[core * OWNED + me], dst_ref=fin.at[core * OWNED + me],
                send_sem=ag_send.at[step], recv_sem=ag_recv.at[me],
                device_id={"space": target}, device_id_type=MESH,
            )

        def forward_copy(tile):
            spot = fin.at[core * OWNED + tile]
            return pltpu.make_async_remote_copy(
                src_ref=spot, dst_ref=spot,
                send_sem=fw_send.at[tile], recv_sem=fw_recv.at[tile],
                device_id={"dp": 1 - core}, device_id_type=MESH,
            )

        @pl.when(me < OWNED)
        def _():
            total = jnp.zeros((CH, PAIR), jnp.float32)
            for source in range(count):

                @pl.when(me != source)
                def _():
                    pltpu.make_async_remote_copy(
                        src_ref=sbuf.at[0], dst_ref=rbuf.at[source],
                        send_sem=rs_send.at[0], recv_sem=rs_recv.at[source],
                        device_id={"space": source}, device_id_type=MESH,
                    ).wait_recv()

                total = total + rbuf[source].astype(jnp.float32)
            fin[core * OWNED + me] = turn(total).astype(jnp.bfloat16)
            for step in range(1, count):
                gather_copy(step).start()

    result = lax.dot_general(
        cw[...], wg[...], (((1,), (1,)), ((), ())), preferred_element_type=jnp.float32
    )

    def put_gradient(brick, k, value):
        fg_ref[0, brick, :, :, k * PAIR : (k + 1) * PAIR] = value

    sum_taps(result, put_gradient)

    if reduce_here:
        for tile in range(OWNED):

            @pl.when(me != tile)
            def _():
                spot = fin.at[core * OWNED + tile]
                pltpu.make_async_remote_copy(
                    src_ref=spot, dst_ref=spot,
                    send_sem=ag_send.at[0], recv_sem=ag_recv.at[tile],
                    device_id={"space": tile}, device_id_type=MESH,
                ).wait_recv()

            forward_copy(tile).start()

        for tile in range(OWNED):
            spot = fin.at[(1 - core) * OWNED + tile]
            pltpu.make_async_remote_copy(
                src_ref=spot, dst_ref=spot,
                send_sem=fw_send.at[tile], recv_sem=fw_recv.at[tile],
                device_id={"dp": 1 - core}, device_id_type=MESH,
            ).wait_recv()
        for tile in range(OWNED):
            forward_copy(tile).wait_send()

        @pl.when(me < OWNED)
        def _():
            for step in range(1, count):
                gather_copy(step).wait_send()
    else:
        for tile in range(TILES):
            part[tile] = turn(part[tile])
    if reduce_here:
        for copy in core_copies:
            copy.wait_send()
        for tile in range(OWNED):
            pl.when(me != tile)(scatter_copy(tile).wait_send)
    for sent, _, copy in f_copies + c_copies:
        pl.when(sent)(copy.wait_send)


def finish_body(scale, resp_ref, fg_ref, tiles_ref, resp_hbm, fg_hbm, kg_hbm, kg, sems):
    copies = [
        pltpu.make_async_copy(resp_ref, resp_hbm, sems.at[0]),
        pltpu.make_async_copy(fg_ref, fg_hbm, sems.at[1]),
    ]
    for copy in copies:
        copy.start()
    for a in range(3):
        for b in range(3):
            tap = b * 3 + a
            later = tiles_ref[SPOT["late", tap]].astype(jnp.float32) * scale
            first = tiles_ref[SPOT["early", tap // 2]].astype(jnp.float32) * scale
            kg[a, b, 0] = first[:, tap % 2 * CH : (tap % 2 + 1) * CH]
            kg[a, b, 1] = later[:, :CH]
            kg[a, b, 2] = later[:, CH:]
        copies.append(pltpu.make_async_copy(kg.at[a], kg_hbm.at[a], sems.at[2 + a]))
        copies[-1].start()
    for copy in copies:
        copy.wait()


def body(features, cotangent, kernel, neighbours):
    count = lax.axis_size("space")
    dp_count = lax.axis_size("dp")
    reduce_here = count == 8 and dp_count == 2
    cells = features.shape[0] * features.shape[1] * dp_count * count * EDGE**3
    scale = 1.0 / math.sqrt(cells)
    bf16, f32 = jnp.bfloat16, jnp.float32
    planes = 2 * (EDGE + 2)
    rows = PAIRS * planes * EDGE
    dma = pltpu.SemaphoreType.DMA
    vmem = pl.BlockSpec(memory_space=pltpu.VMEM)
    hbm = pl.BlockSpec(memory_space=pltpu.HBM)
    part_shape = (TILES, CH, PAIR)
    response, feature_grad, tiles = pl.pallas_call(
        functools.partial(kernel_body, count, reduce_here),
        out_shape=(
            pltpu.VMEM(features.shape, bf16),
            pltpu.VMEM(features.shape, bf16),
            pltpu.VMEM(part_shape, bf16 if reduce_here else f32),
        ),
        in_specs=[hbm] * 4,
        out_specs=(vmem, vmem, vmem),
        scratch_shapes=[
            pltpu.SMEM(neighbours.shape, jnp.int32),
            pltpu.VMEM(features.shape, bf16),
            pltpu.VMEM(features.shape, bf16),
            pltpu.VMEM(kernel.shape, bf16),
            pltpu.VMEM((2, 2, EDGE, ROWS), bf16),
            pltpu.VMEM((2, 3, EDGE, ROWS), bf16),
            pltpu.VMEM((2, 2, EDGE, WIDE), bf16),
            pltpu.VMEM((2, 3, EDGE, WIDE), bf16),
            pltpu.VMEM((2, EDGE, ROWS), bf16),
            pltpu.VMEM((2, EDGE, WIDE), bf16),
            pltpu.VMEM((2, EDGE, EDGE, WIDE), bf16),
            pltpu.VMEM((rows, 12 * CH), bf16),
            pltpu.VMEM((rows, 12 * CH), bf16),
            pltpu.VMEM((6 * CH, rows), bf16),
            pltpu.VMEM((12 * CH, 6 * CH), bf16),
            pltpu.VMEM((6 * CH, 12 * CH), bf16),
            pltpu.VMEM(part_shape, f32),
            pltpu.VMEM((OWNED, CH, PAIR), f32),
            pltpu.VMEM((8, CH, PAIR), bf16),
            pltpu.VMEM((8, CH, PAIR), bf16),
            dma((4,)), dma((16,)), dma((16,)), dma((3,)), dma((3,)), dma((8,)), dma((8,)),
            dma((8,)), dma((8,)), dma((8,)), dma((8,)),
        ],
        compiler_params=pltpu.CompilerParams(
            collective_id=0, has_side_effects=True, vmem_limit_bytes=40 * 1024 * 1024
        ),
        cost_estimate=pl.CostEstimate(flops=10**9, bytes_accessed=2 * 10**6, transcendentals=0),
    )(*(
        pltpu.with_memory_space_constraint(x, pltpu.HBM)
        for x in (neighbours, features, cotangent, kernel)
    ))
    if not reduce_here:
        tiles = lax.psum(tiles, ("space", "dp"))
    return pl.pallas_call(
        functools.partial(finish_body, scale),
        out_shape=(
            jax.ShapeDtypeStruct(features.shape, bf16),
            jax.ShapeDtypeStruct(features.shape, bf16),
            jax.ShapeDtypeStruct(kernel.shape, f32),
        ),
        in_specs=[vmem] * 3,
        out_specs=(hbm,) * 3,
        scratch_shapes=[pltpu.VMEM(kernel.shape, f32), dma((5,))],
        cost_estimate=pl.CostEstimate(flops=10**6, bytes_accessed=10**6, transcendentals=0),
    )(*(
        pltpu.with_memory_space_constraint(x, pltpu.VMEM)
        for x in (response, feature_grad, tiles)
    ))


def solution(mesh):
    in_specs = (
        P(("groups", "dp"), "space", None, None, None),
        P(("groups", "dp"), "space", None, None, None),
        P(),
        P(("groups", "dp"), "space", None),
    )
    out_specs = (
        P(("groups", "dp"), "space", None, None, None),
        P(("groups", "dp"), "space", None, None, None),
        P("groups", None, None, None, None),
    )
    return jax.shard_map(body, mesh=mesh, in_specs=in_specs, out_specs=out_specs, check_vma=False)
```

```python
import functools
import math

import jax
import jax.numpy as jnp
from jax import lax
from jax.experimental import pallas as pl
from jax.experimental.pallas import tpu as pltpu
from jax.sharding import PartitionSpec as P

TILES_Y = 4
EDGE = 8
CH = 64
PAIR = 2 * CH
PAIRS = EDGE // 2
ROWS = EDGE * CH
WIDE = ROWS + PAIR
SLOTS = 8
OWNERS = 4
FIRST_OWNER = 2
MESH = pl.DeviceIdType.MESH
BATCHES = ((0, 2), (2, 4), (4, 7))
OWNERS_READY = ((0,), (1,), (2, 3))
READY = (
    [("late", 0), ("late", 1), ("late", 2), ("early", 0)]
    + [("late", 3), ("late", 4), ("late", 5), ("early", 1)]
    + [("early", 2), ("late", 6), ("late", 7), ("late", 8), ("early", 3), ("early", 4)]
)
SPOT = {name: number % 2 * SLOTS + number // 2 for number, name in enumerate(READY)}
DIAGONALS = [(side, dx) for side in range(2) for dx in range(3)]


def low_lanes(shape):
    return lax.broadcasted_iota(jnp.int32, shape, len(shape) - 1) < CH


def in_range(tile, count):
    return (tile >= 0) & (tile < count)


def receives(tile, dx, dy, count, first_x):
    column = (tile + TILES_Y // 2) % TILES_Y + dy
    there = in_range(tile + TILES_Y * dx + dy, count) & (column >= 0) & (column < TILES_Y)
    between = tile + TILES_Y * dx if first_x else tile + dy
    return in_range(tile, count) & in_range(between, count) & there


def window_builder(out_ref, center, edge, halo_low, halo_high, edge_low, edge_high):
    def shifted(values, low_row, high_row, tap):
        if tap == 0:
            return jnp.concatenate([low_row, values[:, :, : EDGE - 1]], axis=2)
        if tap == 2:
            return jnp.concatenate([values[:, :, 1:], high_row], axis=2)
        return values

    def build(tap):
        moved = shifted(center, halo_low, halo_high, tap)
        outer = shifted(edge, edge_low, edge_high, tap)
        low = low_lanes(outer.shape)
        pairs = [moved[..., PAIR * k : PAIR * (k + 1)] for k in range(PAIRS)]
        around = []
        for k in range(PAIRS):
            after = pairs[k + 1] if k + 1 < PAIRS else outer
            before = pairs[k - 1] if k > 0 else outer
            around.append(jnp.where(low, after, before))
        for half, pieces in enumerate((around, pairs)):
            rows = jnp.stack(pieces, axis=2).reshape(-1, PAIR).astype(jnp.bfloat16)
            base = (2 * tap + half) * PAIR
            out_ref[:, base : base + PAIR] = rows

    return build


def outer_rows(center, y_ref, width):
    sides = []
    for side in range(2):
        below = y_ref[side, 0].astype(jnp.float32)[EDGE - 1 :, None, :width]
        level = y_ref[side, 1].astype(jnp.float32)[:, None, :width]
        above = y_ref[side, 2].astype(jnp.float32)[:1, None, :width]
        sides.append(jnp.concatenate([below, level, above], axis=0))
    low = jnp.stack([sides[0], center[:, 0, EDGE - 1 :]], axis=1)
    high = jnp.stack([center[:, 1, :1], sides[1]], axis=1)
    return low, high


def sum_taps(result, store):
    step = 2 * PAIRS * EDGE
    count = EDGE * step
    total = result[:count, :PAIR]
    for a in range(1, 3):
        total = total + result[a * step : a * step + count, a * PAIR : (a + 1) * PAIR]
    total = total.reshape(EDGE, 2, PAIRS, EDGE, PAIR).astype(jnp.bfloat16)
    for brick in range(2):
        for k in range(PAIRS):
            store(brick, k, total[:, brick, k])


def turn(tile):
    turned = tile.T
    return jnp.concatenate([turned[:CH], turned[CH:]], axis=1)


def kernel_body(
    count, reduce_here,
    nb_hbm, f_hbm, c_hbm, w_hbm,
    resp_ref, fg_ref, tiles_ref,
    nb_ref, f_ref, c_ref, w_ref,
    fx, fy, cx, cy, fys, cys, cz, xw, cw, ct, wf, wg, part, core_in, sbuf, rbuf,
    load_sem, halo_send, halo_recv, core_send, core_recv, rs_send, rs_recv, ag_send, ag_recv, fw_send, fw_recv,
):
    me = lax.axis_index("space")
    core = lax.axis_index("dp")
    if reduce_here:
        fin = tiles_ref
    else:
        part = tiles_ref
    loads = [
        pltpu.make_async_copy(src, dst, load_sem.at[number])
        for number, (src, dst) in enumerate(
            [(f_hbm, f_ref), (c_hbm, c_ref), (nb_hbm, nb_ref), (w_hbm, w_ref)]
        )
    ]
    for load in loads:
        load.start()

    fx[...] = jnp.zeros_like(fx)
    fy[...] = jnp.zeros_like(fy)
    cx[...] = jnp.zeros_like(cx)
    cy[...] = jnp.zeros_like(cy)

    barrier = pltpu.get_barrier_semaphore()
    if reduce_here:
        for step in range(1, count):
            pl.semaphore_signal(
                barrier, inc=1, device_id={"space": (me + step) % count}, device_id_type=MESH
            )
        pl.semaphore_signal(barrier, inc=1, device_id={"dp": 1 - core}, device_id_type=MESH)
    else:
        for step in (1, 3, 4, 5):
            for other in (me + step, me - step):

                @pl.when(in_range(other, count))
                def _():
                    pl.semaphore_signal(
                        barrier, inc=1, device_id={"space": other}, device_id_type=MESH
                    )

    def halo(kind):
        x_ref, y_ref, ys_ref = ((fx, fy, fys), (cx, cy, cys))[kind]
        entries = []
        for side in range(2):
            dx = 2 * side - 1
            target = me - TILES_Y * dx
            face = EDGE - 1 if side == 0 else 0
            source = f_ref.at[0, :, face] if kind == 0 else cz.at[:, face]
            entries.append((
                receives(target, dx, 0, count, True),
                receives(me, dx, 0, count, True),
                source, x_ref.at[side], target,
            ))
        for side, column in DIAGONALS:
            dx, dy = column - 1, 2 * side - 1
            target = me - TILES_Y * dx - dy
            entries.append((
                receives(target, dx, dy, count, kind == 1),
                receives(me, dx, dy, count, kind == 1),
                ys_ref.at[side], y_ref.at[side, column], target,
            ))
        out = []
        for number, (sent, arrives, source, target_ref, target) in enumerate(entries):
            out.append((sent, arrives, pltpu.make_async_remote_copy(
                src_ref=source, dst_ref=target_ref,
                send_sem=halo_send.at[kind * 8 + number],
                recv_sem=halo_recv.at[kind * 8 + number],
                device_id={"space": target}, device_id_type=MESH,
            )))
        return out

    def start_halo(copies):
        for sent, _, copy in copies:
            pl.when(sent)(copy.start)

    def wait_halo(copies):
        for _, arrives, copy in copies:
            pl.when(arrives)(copy.wait_recv)

    loads[0].wait()
    fys[0] = f_ref[0, 1].astype(jnp.float32)[:, EDGE - 1].astype(jnp.bfloat16)
    fys[1] = f_ref[0, 0].astype(jnp.float32)[:, 0].astype(jnp.bfloat16)

    if reduce_here:
        pl.semaphore_wait(barrier, count)
    else:
        for step in (1, 3, 4, 5):
            for other in (me + step, me - step):

                @pl.when(in_range(other, count))
                def _():
                    pl.semaphore_wait(barrier, 1)

    f_copies, c_copies = halo(0), halo(1)
    start_halo(f_copies)

    loads[1].wait()
    loads[2].wait()
    for brick in range(2):
        other = 1 - brick
        before = jnp.where(nb_ref[0, brick, 4] >= 0, 1.0, 0.0)
        after = jnp.where(nb_ref[0, brick, 5] >= 0, 1.0, 0.0)
        cz[brick, :, :, :ROWS] = c_ref[0, brick]
        low = low_lanes((EDGE, EDGE, PAIR))
        edge = jnp.where(
            low,
            c_ref[0, other, :, :, :PAIR].astype(jnp.float32) * after,
            c_ref[0, other, :, :, ROWS - PAIR :].astype(jnp.float32) * before,
        )
        cz[brick, :, :, ROWS:] = edge.astype(jnp.bfloat16)
    cys[0] = cz[1].astype(jnp.float32)[:, EDGE - 1].astype(jnp.bfloat16)
    cys[1] = cz[0].astype(jnp.float32)[:, 0].astype(jnp.bfloat16)

    loads[3].wait()
    blank = jnp.zeros((CH, CH), jnp.bfloat16)
    for a in range(3):
        for b in range(3):
            taps = [w_ref[a, b, d] for d in range(3)]
            for w, slot in enumerate((1, 2, 3, 0)):
                left = taps[w] if w < 3 else blank
                right = taps[w - 1] if w > 0 else blank
                block = jnp.concatenate([left, right], axis=1)
                row = (b * 4 + slot) * CH
                wf[row : row + CH, a * PAIR : (a + 1) * PAIR] = block
                cell, half = ((1, 0), (0, 1), (1, 1), (0, 0))[w]
                row = (2 - a) * PAIR + cell * CH
                lane = (2 - b) * 4 * CH + half * PAIR
                wg[row : row + CH, lane : lane + PAIR] = block

    pieces = []
    for k in range(PAIRS):
        lanes = slice(k * PAIR, (k + 1) * PAIR)
        pieces.append(
            jnp.stack([c_ref[0, b, :, :, lanes].astype(jnp.float32) for b in range(2)], axis=1)
        )
    turned = jnp.stack(pieces, axis=2).reshape(-1, PAIR).T
    step = 2 * PAIRS * EDGE
    for a in range(3):
        padded = [jnp.zeros((PAIR, a * step), jnp.float32)] if a > 0 else []
        padded.append(turned)
        if a < 2:
            padded.append(jnp.zeros((PAIR, (2 - a) * step), jnp.float32))
        ct[a * PAIR : (a + 1) * PAIR] = jnp.concatenate(padded, axis=1).astype(jnp.bfloat16)

    wait_halo(f_copies)

    def stack(values, x_ref, width):
        first = x_ref[0].astype(jnp.float32)[None, ..., :width]
        last = x_ref[1].astype(jnp.float32)[None, ..., :width]
        return jnp.concatenate([first, jnp.stack(values, axis=1), last], axis=0)

    center = stack([f_ref[0, b].astype(jnp.float32) for b in range(2)], fx, ROWS)
    row_low, row_high = outer_rows(center, fy, ROWS)

    def third_edge(values):
        pieces = []
        for brick in range(2):
            other = values[:, 1 - brick]
            before = jnp.where(nb_ref[0, brick, 4] >= 0, 1.0, 0.0)
            after = jnp.where(nb_ref[0, brick, 5] >= 0, 1.0, 0.0)
            low = low_lanes(other.shape[:-1] + (PAIR,))
            pieces.append(
                jnp.where(low, other[..., :PAIR] * after, other[..., ROWS - PAIR :] * before)
            )
        return jnp.stack(pieces, axis=1)

    build_features = window_builder(
        xw, center, third_edge(center), row_low, row_high, third_edge(row_low), third_edge(row_high)
    )

    low = low_lanes((CH, PAIR))
    core_copies = [
        pltpu.make_async_remote_copy(
            src_ref=part.at[pl.ds((1 - core) * SLOTS + first, last - first)],
            dst_ref=core_in.at[pl.ds(first, last - first)],
            send_sem=core_send.at[batch], recv_sem=core_recv.at[batch],
            device_id={"dp": 1 - core}, device_id_type=MESH,
        )
        for batch, (first, last) in enumerate(BATCHES)
    ] if reduce_here else []

    def scatter_copy(owner):
        return pltpu.make_async_remote_copy(
            src_ref=sbuf.at[pl.ds(2 * owner, 2)], dst_ref=rbuf.at[me],
            send_sem=rs_send.at[owner], recv_sem=rs_recv.at[me],
            device_id={"space": FIRST_OWNER + owner}, device_id_type=MESH,
        )

    def scatter(batch):
        core_copies[batch].wait_recv()
        for tile in range(*BATCHES[batch]):
            total = part[core * SLOTS + tile] + core_in[tile]
            sbuf[tile] = total.astype(jnp.bfloat16)
        for owner in OWNERS_READY[batch]:
            pl.when(me != FIRST_OWNER + owner)(scatter_copy(owner).start)

    if reduce_here:
        sbuf[SLOTS - 1] = jnp.zeros((CH, PAIR), jnp.bfloat16)
    else:
        for side in range(2):
            part[side * SLOTS + SLOTS - 1] = jnp.zeros((CH, PAIR), jnp.float32)

    first_taps = []
    for b in range(3):
        build_features(b)
        grad = jnp.dot(
            ct[...], xw[:, b * 4 * CH : (b + 1) * 4 * CH], preferred_element_type=jnp.float32
        )
        for a in range(3):
            cell0 = grad[a * PAIR : a * PAIR + CH]
            cell1 = grad[a * PAIR + CH : (a + 1) * PAIR]
            turned0 = pltpu.roll(cell1[:, :PAIR], CH, 1)
            turned1 = pltpu.roll(cell1[:, PAIR:], CH, 1)
            tap = b * 3 + a
            part[SPOT["late", tap]] = cell0[:, PAIR:] + jnp.where(low, turned1, turned0)
            first_taps.append(cell0[:, :PAIR] + turned1)
            if tap % 2 == 1 or tap == 8:
                pair = first_taps[tap - tap % 2 :] + [jnp.zeros((CH, PAIR), jnp.float32)]
                part[SPOT["early", tap // 2]] = jnp.where(low, pltpu.roll(pair[0], CH, 1), pair[1])
        if reduce_here:
            core_copies[b].start()
            if b > 0:
                scatter(b - 1)

    if reduce_here:
        scatter(2)
    start_halo(c_copies)

    result = jnp.dot(xw[...], wf[...], preferred_element_type=jnp.float32)

    def put_response(brick, k, value):
        resp_ref[0, brick, :, :, k * PAIR : (k + 1) * PAIR] = value

    sum_taps(result, put_response)

    if reduce_here:
        mine = me - FIRST_OWNER
        is_owner = (mine >= 0) & (mine < OWNERS)

        def gather_copy(step):
            spot = fin.at[pl.ds(core * SLOTS + 2 * mine, 2)]
            return pltpu.make_async_remote_copy(
                src_ref=spot, dst_ref=spot,
                send_sem=ag_send.at[step], recv_sem=ag_recv.at[mine],
                device_id={"space": (me + step) % count}, device_id_type=MESH,
            )

        def forward_copy(owner, from_core):
            spot = fin.at[pl.ds(from_core * SLOTS + 2 * owner, 2)]
            return pltpu.make_async_remote_copy(
                src_ref=spot, dst_ref=spot,
                send_sem=fw_send.at[owner], recv_sem=fw_recv.at[owner],
                device_id={"dp": 1 - core}, device_id_type=MESH,
            )

        @pl.when(is_owner)
        def _():
            total = sbuf[pl.ds(2 * mine, 2)].astype(jnp.float32)
            for step in range(1, count):
                source = (me + step) % count
                pltpu.make_async_remote_copy(
                    src_ref=sbuf.at[pl.ds(0, 2)], dst_ref=rbuf.at[source],
                    send_sem=rs_send.at[0], recv_sem=rs_recv.at[source],
                    device_id={"space": source}, device_id_type=MESH,
                ).wait_recv()
                total = total + rbuf[source].astype(jnp.float32)
            for half in range(2):
                fin[core * SLOTS + 2 * mine + half] = turn(total[half]).astype(jnp.bfloat16)
            for step in range(1, count):
                gather_copy(step).start()

    wait_halo(c_copies)
    wide = stack([cz[b].astype(jnp.float32) for b in range(2)], cx, WIDE)
    wide_low, wide_high = outer_rows(wide, cy, WIDE)
    build_cotangent = window_builder(
        cw, wide[..., :ROWS], wide[..., ROWS:], wide_low[..., :ROWS], wide_high[..., :ROWS],
        wide_low[..., ROWS:], wide_high[..., ROWS:],
    )
    for tap in range(3):
        build_cotangent(tap)

    result = lax.dot_general(
        cw[...], wg[...], (((1,), (1,)), ((), ())), preferred_element_type=jnp.float32
    )

    def put_gradient(brick, k, value):
        fg_ref[0, brick, :, :, k * PAIR : (k + 1) * PAIR] = value

    sum_taps(result, put_gradient)

    if reduce_here:
        for owner in range(OWNERS):

            @pl.when(me != FIRST_OWNER + owner)
            def _():
                spot = fin.at[pl.ds(core * SLOTS + 2 * owner, 2)]
                pltpu.make_async_remote_copy(
                    src_ref=spot, dst_ref=spot,
                    send_sem=ag_send.at[0], recv_sem=ag_recv.at[owner],
                    device_id={"space": FIRST_OWNER + owner}, device_id_type=MESH,
                ).wait_recv()

            forward_copy(owner, core).start()
        for owner in range(OWNERS):
            forward_copy(owner, 1 - core).wait_recv()
        for owner in range(OWNERS):
            forward_copy(owner, core).wait_send()
            pl.when(me != FIRST_OWNER + owner)(scatter_copy(owner).wait_send)
        for copy in core_copies:
            copy.wait_send()

        @pl.when(is_owner)
        def _():
            for step in range(1, count):
                gather_copy(step).wait_send()
    else:
        for name in READY:
            part[SPOT[name]] = turn(part[SPOT[name]])
    for sent, _, copy in f_copies + c_copies:
        pl.when(sent)(copy.wait_send)


def finish_body(scale, resp_ref, fg_ref, tiles_ref, resp_hbm, fg_hbm, kg_hbm, kg, sems):
    copies = [
        pltpu.make_async_copy(resp_ref, resp_hbm, sems.at[0]),
        pltpu.make_async_copy(fg_ref, fg_hbm, sems.at[1]),
    ]
    for copy in copies:
        copy.start()
    for a in range(3):
        for b in range(3):
            tap = b * 3 + a
            later = tiles_ref[SPOT["late", tap]].astype(jnp.float32) * scale
            first = tiles_ref[SPOT["early", tap // 2]].astype(jnp.float32) * scale
            kg[a, b, 0] = first[:, tap % 2 * CH : (tap % 2 + 1) * CH]
            kg[a, b, 1] = later[:, :CH]
            kg[a, b, 2] = later[:, CH:]
        copies.append(pltpu.make_async_copy(kg.at[a], kg_hbm.at[a], sems.at[2 + a]))
        copies[-1].start()
    for copy in copies:
        copy.wait()


def body(features, cotangent, kernel, neighbours):
    count = lax.axis_size("space")
    dp_count = lax.axis_size("dp")
    reduce_here = count == 8 and dp_count == 2
    cells = features.shape[0] * features.shape[1] * dp_count * count * EDGE**3
    scale = 1.0 / math.sqrt(cells)
    bf16, f32 = jnp.bfloat16, jnp.float32
    planes = 2 * (EDGE + 2)
    rows = PAIRS * planes * EDGE
    dma = pltpu.SemaphoreType.DMA
    vmem = pl.BlockSpec(memory_space=pltpu.VMEM)
    hbm = pl.BlockSpec(memory_space=pltpu.HBM)
    part_shape = (2 * SLOTS, CH, PAIR)
    response, feature_grad, tiles = pl.pallas_call(
        functools.partial(kernel_body, count, reduce_here),
        out_shape=(
            pltpu.VMEM(features.shape, bf16),
            pltpu.VMEM(features.shape, bf16),
            pltpu.VMEM(part_shape, bf16 if reduce_here else f32),
        ),
        in_specs=[hbm] * 4,
        out_specs=(vmem, vmem, vmem),
        scratch_shapes=[
            pltpu.SMEM(neighbours.shape, jnp.int32),
            pltpu.VMEM(features.shape, bf16),
            pltpu.VMEM(features.shape, bf16),
            pltpu.VMEM(kernel.shape, bf16),
            pltpu.VMEM((2, 2, EDGE, ROWS), bf16),
            pltpu.VMEM((2, 3, EDGE, ROWS), bf16),
            pltpu.VMEM((2, 2, EDGE, WIDE), bf16),
            pltpu.VMEM((2, 3, EDGE, WIDE), bf16),
            pltpu.VMEM((2, EDGE, ROWS), bf16),
            pltpu.VMEM((2, EDGE, WIDE), bf16),
            pltpu.VMEM((2, EDGE, EDGE, WIDE), bf16),
            pltpu.VMEM((rows, 12 * CH), bf16),
            pltpu.VMEM((rows, 12 * CH), bf16),
            pltpu.VMEM((6 * CH, rows), bf16),
            pltpu.VMEM((12 * CH, 6 * CH), bf16),
            pltpu.VMEM((6 * CH, 12 * CH), bf16),
            pltpu.VMEM(part_shape, f32),
            pltpu.VMEM((SLOTS, CH, PAIR), f32),
            pltpu.VMEM((SLOTS, CH, PAIR), bf16),
            pltpu.VMEM((8, 2, CH, PAIR), bf16),
            dma((4,)), dma((16,)), dma((16,)), dma((3,)), dma((3,)), dma((8,)), dma((8,)),
            dma((8,)), dma((8,)), dma((8,)), dma((8,)),
        ],
        compiler_params=pltpu.CompilerParams(
            collective_id=0, has_side_effects=True, vmem_limit_bytes=40 * 1024 * 1024
        ),
        cost_estimate=pl.CostEstimate(flops=10**9, bytes_accessed=2 * 10**6, transcendentals=0),
    )(*(
        pltpu.with_memory_space_constraint(x, pltpu.HBM)
        for x in (neighbours, features, cotangent, kernel)
    ))
    if not reduce_here:
        tiles = lax.psum(tiles, ("space", "dp"))
    return pl.pallas_call(
        functools.partial(finish_body, scale),
        out_shape=(
            jax.ShapeDtypeStruct(features.shape, bf16),
            jax.ShapeDtypeStruct(features.shape, bf16),
            jax.ShapeDtypeStruct(kernel.shape, f32),
        ),
        in_specs=[vmem] * 3,
        out_specs=(hbm,) * 3,
        scratch_shapes=[pltpu.VMEM(kernel.shape, f32), dma((5,))],
        cost_estimate=pl.CostEstimate(flops=10**6, bytes_accessed=10**6, transcendentals=0),
    )(*(
        pltpu.with_memory_space_constraint(x, pltpu.VMEM)
        for x in (response, feature_grad, tiles)
    ))


def solution(mesh):
    in_specs = (
        P(("groups", "dp"), "space", None, None, None),
        P(("groups", "dp"), "space", None, None, None),
        P(),
        P(("groups", "dp"), "space", None),
    )
    out_specs = (
        P(("groups", "dp"), "space", None, None, None),
        P(("groups", "dp"), "space", None, None, None),
        P("groups", None, None, None, None),
    )
    return jax.shard_map(body, mesh=mesh, in_specs=in_specs, out_specs=out_specs, check_vma=False)
```

```python
import functools
import math

import jax
import jax.numpy as jnp
from jax import lax
from jax.experimental import pallas as pl
from jax.experimental.pallas import tpu as pltpu
from jax.sharding import PartitionSpec as P

TILES_Y = 4
EDGE = 8
CH = 64
PAIR = 2 * CH
PAIRS = EDGE // 2
ROWS = EDGE * CH
WIDE = ROWS + PAIR
TILES = 14
OWNED = TILES // 2
MESH = pl.DeviceIdType.MESH
BATCHES = ((0, 2), (2, 4), (4, 7))
READY = (
    [("late", 0), ("late", 1), ("late", 2), ("early", 0)]
    + [("late", 3), ("late", 4), ("late", 5), ("early", 1)]
    + [("early", 2), ("late", 6), ("late", 7), ("late", 8), ("early", 3), ("early", 4)]
)
SPOT = {name: number % 2 * OWNED + number // 2 for number, name in enumerate(READY)}
DIAGONALS = [(side, dx) for side in range(2) for dx in range(3)]


def low_lanes(shape):
    return lax.broadcasted_iota(jnp.int32, shape, len(shape) - 1) < CH


def in_range(tile, count):
    return (tile >= 0) & (tile < count)


def receives(tile, dx, dy, count, first_x):
    column = (tile + TILES_Y // 2) % TILES_Y + dy
    there = in_range(tile + TILES_Y * dx + dy, count) & (column >= 0) & (column < TILES_Y)
    between = tile + TILES_Y * dx if first_x else tile + dy
    return in_range(tile, count) & in_range(between, count) & there


def window_builder(out_ref, center, edge, halo_low, halo_high, edge_low, edge_high):
    def shifted(values, low_row, high_row, tap):
        if tap == 0:
            return jnp.concatenate([low_row, values[:, :, : EDGE - 1]], axis=2)
        if tap == 2:
            return jnp.concatenate([values[:, :, 1:], high_row], axis=2)
        return values

    def build(tap):
        moved = shifted(center, halo_low, halo_high, tap)
        outer = shifted(edge, edge_low, edge_high, tap)
        low = low_lanes(outer.shape)
        pairs = [moved[..., PAIR * k : PAIR * (k + 1)] for k in range(PAIRS)]
        around = []
        for k in range(PAIRS):
            after = pairs[k + 1] if k + 1 < PAIRS else outer
            before = pairs[k - 1] if k > 0 else outer
            around.append(jnp.where(low, after, before))
        for half, pieces in enumerate((around, pairs)):
            rows = jnp.stack(pieces, axis=2).reshape(-1, PAIR).astype(jnp.bfloat16)
            base = (2 * tap + half) * PAIR
            out_ref[:, base : base + PAIR] = rows

    return build


def outer_rows(center, y_ref, width):
    sides = []
    for side in range(2):
        below = y_ref[side, 0].astype(jnp.float32)[EDGE - 1 :, None, :width]
        level = y_ref[side, 1].astype(jnp.float32)[:, None, :width]
        above = y_ref[side, 2].astype(jnp.float32)[:1, None, :width]
        sides.append(jnp.concatenate([below, level, above], axis=0))
    low = jnp.stack([sides[0], center[:, 0, EDGE - 1 :]], axis=1)
    high = jnp.stack([center[:, 1, :1], sides[1]], axis=1)
    return low, high


def sum_taps(result, store):
    step = 2 * PAIRS * EDGE
    count = EDGE * step
    total = result[:count, :PAIR]
    for a in range(1, 3):
        total = total + result[a * step : a * step + count, a * PAIR : (a + 1) * PAIR]
    total = total.reshape(EDGE, 2, PAIRS, EDGE, PAIR).astype(jnp.bfloat16)
    for brick in range(2):
        for k in range(PAIRS):
            store(brick, k, total[:, brick, k])


def turn(tile):
    turned = tile.T
    return jnp.concatenate([turned[:CH], turned[CH:]], axis=1)


def kernel_body(
    count, reduce_here,
    nb_hbm, f_hbm, c_hbm, w_hbm,
    resp_ref, fg_ref, tiles_ref,
    nb_ref, f_ref, c_ref, w_ref,
    fx, fy, cx, cy, fys, cys, cz, xw, cw, ct, wf, wg, part, core_in, sbuf, rbuf,
    load_sem, halo_send, halo_recv, core_send, core_recv, rs_send, rs_recv, ag_send, ag_recv, fw_send, fw_recv,
):
    me = lax.axis_index("space")
    core = lax.axis_index("dp")
    if reduce_here:
        fin = tiles_ref
    else:
        part = tiles_ref
    loads = [
        pltpu.make_async_copy(src, dst, load_sem.at[number])
        for number, (src, dst) in enumerate(
            [(f_hbm, f_ref), (c_hbm, c_ref), (nb_hbm, nb_ref), (w_hbm, w_ref)]
        )
    ]
    for load in loads:
        load.start()

    fx[...] = jnp.zeros_like(fx)
    fy[...] = jnp.zeros_like(fy)
    cx[...] = jnp.zeros_like(cx)
    cy[...] = jnp.zeros_like(cy)

    barrier = pltpu.get_barrier_semaphore()
    if reduce_here:
        for step in range(1, count):
            pl.semaphore_signal(
                barrier, inc=1, device_id={"space": (me + step) % count}, device_id_type=MESH
            )
        pl.semaphore_signal(barrier, inc=1, device_id={"dp": 1 - core}, device_id_type=MESH)
    else:
        for step in (1, 3, 4, 5):
            for other in (me + step, me - step):

                @pl.when(in_range(other, count))
                def _():
                    pl.semaphore_signal(
                        barrier, inc=1, device_id={"space": other}, device_id_type=MESH
                    )

    def halo(kind):
        x_ref, y_ref, ys_ref = ((fx, fy, fys), (cx, cy, cys))[kind]
        entries = []
        for side in range(2):
            dx = 2 * side - 1
            target = me - TILES_Y * dx
            face = EDGE - 1 if side == 0 else 0
            source = f_ref.at[0, :, face] if kind == 0 else cz.at[:, face]
            entries.append((
                receives(target, dx, 0, count, True),
                receives(me, dx, 0, count, True),
                source, x_ref.at[side], target,
            ))
        for side, column in DIAGONALS:
            dx, dy = column - 1, 2 * side - 1
            target = me - TILES_Y * dx - dy
            entries.append((
                receives(target, dx, dy, count, kind == 1),
                receives(me, dx, dy, count, kind == 1),
                ys_ref.at[side], y_ref.at[side, column], target,
            ))
        out = []
        for number, (sent, arrives, source, target_ref, target) in enumerate(entries):
            out.append((sent, arrives, pltpu.make_async_remote_copy(
                src_ref=source, dst_ref=target_ref,
                send_sem=halo_send.at[kind * 8 + number],
                recv_sem=halo_recv.at[kind * 8 + number],
                device_id={"space": target}, device_id_type=MESH,
            )))
        return out

    def start_halo(copies):
        for sent, _, copy in copies:
            pl.when(sent)(copy.start)

    def wait_halo(copies):
        for _, arrives, copy in copies:
            pl.when(arrives)(copy.wait_recv)

    loads[0].wait()
    fys[0] = f_ref[0, 1].astype(jnp.float32)[:, EDGE - 1].astype(jnp.bfloat16)
    fys[1] = f_ref[0, 0].astype(jnp.float32)[:, 0].astype(jnp.bfloat16)

    if reduce_here:
        pl.semaphore_wait(barrier, count)
    else:
        for step in (1, 3, 4, 5):
            for other in (me + step, me - step):

                @pl.when(in_range(other, count))
                def _():
                    pl.semaphore_wait(barrier, 1)

    f_copies, c_copies = halo(0), halo(1)
    start_halo(f_copies)

    loads[1].wait()
    loads[2].wait()
    for brick in range(2):
        other = 1 - brick
        before = jnp.where(nb_ref[0, brick, 4] >= 0, 1.0, 0.0)
        after = jnp.where(nb_ref[0, brick, 5] >= 0, 1.0, 0.0)
        cz[brick, :, :, :ROWS] = c_ref[0, brick]
        low = low_lanes((EDGE, EDGE, PAIR))
        edge = jnp.where(
            low,
            c_ref[0, other, :, :, :PAIR].astype(jnp.float32) * after,
            c_ref[0, other, :, :, ROWS - PAIR :].astype(jnp.float32) * before,
        )
        cz[brick, :, :, ROWS:] = edge.astype(jnp.bfloat16)
    cys[0] = cz[1].astype(jnp.float32)[:, EDGE - 1].astype(jnp.bfloat16)
    cys[1] = cz[0].astype(jnp.float32)[:, 0].astype(jnp.bfloat16)

    loads[3].wait()
    blank = jnp.zeros((CH, CH), jnp.bfloat16)
    for a in range(3):
        for b in range(3):
            taps = [w_ref[a, b, d] for d in range(3)]
            for w, slot in enumerate((1, 2, 3, 0)):
                left = taps[w] if w < 3 else blank
                right = taps[w - 1] if w > 0 else blank
                block = jnp.concatenate([left, right], axis=1)
                row = (b * 4 + slot) * CH
                wf[row : row + CH, a * PAIR : (a + 1) * PAIR] = block
                cell, half = ((1, 0), (0, 1), (1, 1), (0, 0))[w]
                row = (2 - a) * PAIR + cell * CH
                lane = (2 - b) * 4 * CH + half * PAIR
                wg[row : row + CH, lane : lane + PAIR] = block

    pieces = []
    for k in range(PAIRS):
        lanes = slice(k * PAIR, (k + 1) * PAIR)
        pieces.append(
            jnp.stack([c_ref[0, b, :, :, lanes].astype(jnp.float32) for b in range(2)], axis=1)
        )
    turned = jnp.stack(pieces, axis=2).reshape(-1, PAIR).T
    step = 2 * PAIRS * EDGE
    for a in range(3):
        padded = [jnp.zeros((PAIR, a * step), jnp.float32)] if a > 0 else []
        padded.append(turned)
        if a < 2:
            padded.append(jnp.zeros((PAIR, (2 - a) * step), jnp.float32))
        ct[a * PAIR : (a + 1) * PAIR] = jnp.concatenate(padded, axis=1).astype(jnp.bfloat16)

    wait_halo(f_copies)
    start_halo(c_copies)

    def stack(values, x_ref, width):
        first = x_ref[0].astype(jnp.float32)[None, ..., :width]
        last = x_ref[1].astype(jnp.float32)[None, ..., :width]
        return jnp.concatenate([first, jnp.stack(values, axis=1), last], axis=0)

    center = stack([f_ref[0, b].astype(jnp.float32) for b in range(2)], fx, ROWS)
    row_low, row_high = outer_rows(center, fy, ROWS)

    def third_edge(values):
        pieces = []
        for brick in range(2):
            other = values[:, 1 - brick]
            before = jnp.where(nb_ref[0, brick, 4] >= 0, 1.0, 0.0)
            after = jnp.where(nb_ref[0, brick, 5] >= 0, 1.0, 0.0)
            low = low_lanes(other.shape[:-1] + (PAIR,))
            pieces.append(
                jnp.where(low, other[..., :PAIR] * after, other[..., ROWS - PAIR :] * before)
            )
        return jnp.stack(pieces, axis=1)

    build_features = window_builder(
        xw, center, third_edge(center), row_low, row_high, third_edge(row_low), third_edge(row_high)
    )

    low = low_lanes((CH, PAIR))
    core_copies = [
        pltpu.make_async_remote_copy(
            src_ref=part.at[pl.ds((1 - core) * OWNED + first, last - first)],
            dst_ref=core_in.at[pl.ds(first, last - first)],
            send_sem=core_send.at[batch], recv_sem=core_recv.at[batch],
            device_id={"dp": 1 - core}, device_id_type=MESH,
        )
        for batch, (first, last) in enumerate(BATCHES)
    ] if reduce_here else []

    def scatter_copy(step):
        target = (me + step) % count
        return target, pltpu.make_async_remote_copy(
            src_ref=sbuf.at[target], dst_ref=rbuf.at[me],
            send_sem=rs_send.at[step], recv_sem=rs_recv.at[me],
            device_id={"space": target}, device_id_type=MESH,
        )

    def add_core(batch):
        core_copies[batch].wait_recv()
        for tile in range(*BATCHES[batch]):
            total = part[core * OWNED + tile] + core_in[tile]
            sbuf[tile] = total.astype(jnp.bfloat16)

    first_taps = []
    for b in range(3):
        build_features(b)
        grad = jnp.dot(
            ct[...], xw[:, b * 4 * CH : (b + 1) * 4 * CH], preferred_element_type=jnp.float32
        )
        for a in range(3):
            cell0 = grad[a * PAIR : a * PAIR + CH]
            cell1 = grad[a * PAIR + CH : (a + 1) * PAIR]
            turned0 = pltpu.roll(cell1[:, :PAIR], CH, 1)
            turned1 = pltpu.roll(cell1[:, PAIR:], CH, 1)
            tap = b * 3 + a
            part[SPOT["late", tap]] = cell0[:, PAIR:] + jnp.where(low, turned1, turned0)
            first_taps.append(cell0[:, :PAIR] + turned1)
            if tap % 2 == 1 or tap == 8:
                pair = first_taps[tap - tap % 2 :] + [jnp.zeros((CH, PAIR), jnp.float32)]
                part[SPOT["early", tap // 2]] = jnp.where(low, pltpu.roll(pair[0], CH, 1), pair[1])
        if reduce_here:
            core_copies[b].start()
            if b > 0:
                add_core(b - 1)

    if reduce_here:
        add_core(2)
        for step in range(1, count):
            target, copy = scatter_copy(step)
            pl.when(target < OWNED)(copy.start)

    result = jnp.dot(xw[...], wf[...], preferred_element_type=jnp.float32)

    def put_response(brick, k, value):
        resp_ref[0, brick, :, :, k * PAIR : (k + 1) * PAIR] = value

    sum_taps(result, put_response)

    wait_halo(c_copies)
    wide = stack([cz[b].astype(jnp.float32) for b in range(2)], cx, WIDE)
    wide_low, wide_high = outer_rows(wide, cy, WIDE)
    build_cotangent = window_builder(
        cw, wide[..., :ROWS], wide[..., ROWS:], wide_low[..., :ROWS], wide_high[..., :ROWS],
        wide_low[..., ROWS:], wide_high[..., ROWS:],
    )
    for tap in range(3):
        build_cotangent(tap)

    if reduce_here:
        def gather_copy(step):
            target = (me + step) % count
            return pltpu.make_async_remote_copy(
                src_ref=fin.at[core * OWNED + me], dst_ref=fin.at[core * OWNED + me],
                send_sem=ag_send.at[step], recv_sem=ag_recv.at[me],
                device_id={"space": target}, device_id_type=MESH,
            )

        def forward_copy(tile):
            spot = fin.at[core * OWNED + tile]
            return pltpu.make_async_remote_copy(
                src_ref=spot, dst_ref=spot,
                send_sem=fw_send.at[tile], recv_sem=fw_recv.at[tile],
                device_id={"dp": 1 - core}, device_id_type=MESH,
            )

        @pl.when(me < OWNED)
        def _():
            total = sbuf[me].astype(jnp.float32)
            for step in range(1, count):
                source = (me + step) % count
                pltpu.make_async_remote_copy(
                    src_ref=sbuf.at[0], dst_ref=rbuf.at[source],
                    send_sem=rs_send.at[0], recv_sem=rs_recv.at[source],
                    device_id={"space": source}, device_id_type=MESH,
                ).wait_recv()
                total = total + rbuf[source].astype(jnp.float32)
            fin[core * OWNED + me] = turn(total).astype(jnp.bfloat16)
            for step in range(1, count):
                gather_copy(step).start()

    result = lax.dot_general(
        cw[...], wg[...], (((1,), (1,)), ((), ())), preferred_element_type=jnp.float32
    )

    def put_gradient(brick, k, value):
        fg_ref[0, brick, :, :, k * PAIR : (k + 1) * PAIR] = value

    sum_taps(result, put_gradient)

    if reduce_here:
        for tile in range(OWNED):

            @pl.when(me != tile)
            def _():
                spot = fin.at[core * OWNED + tile]
                pltpu.make_async_remote_copy(
                    src_ref=spot, dst_ref=spot,
                    send_sem=ag_send.at[0], recv_sem=ag_recv.at[tile],
                    device_id={"space": tile}, device_id_type=MESH,
                ).wait_recv()

            forward_copy(tile).start()

        for tile in range(OWNED):
            spot = fin.at[(1 - core) * OWNED + tile]
            pltpu.make_async_remote_copy(
                src_ref=spot, dst_ref=spot,
                send_sem=fw_send.at[tile], recv_sem=fw_recv.at[tile],
                device_id={"dp": 1 - core}, device_id_type=MESH,
            ).wait_recv()
        for tile in range(OWNED):
            forward_copy(tile).wait_send()

        @pl.when(me < OWNED)
        def _():
            for step in range(1, count):
                gather_copy(step).wait_send()
    else:
        for tile in range(TILES):
            part[tile] = turn(part[tile])
    if reduce_here:
        for copy in core_copies:
            copy.wait_send()
        for step in range(1, count):
            target, copy = scatter_copy(step)
            pl.when(target < OWNED)(copy.wait_send)
    for sent, _, copy in f_copies + c_copies:
        pl.when(sent)(copy.wait_send)


def finish_body(scale, resp_ref, fg_ref, tiles_ref, resp_hbm, fg_hbm, kg_hbm, kg, sems):
    copies = [
        pltpu.make_async_copy(resp_ref, resp_hbm, sems.at[0]),
        pltpu.make_async_copy(fg_ref, fg_hbm, sems.at[1]),
    ]
    for copy in copies:
        copy.start()
    for a in range(3):
        for b in range(3):
            tap = b * 3 + a
            later = tiles_ref[SPOT["late", tap]].astype(jnp.float32) * scale
            first = tiles_ref[SPOT["early", tap // 2]].astype(jnp.float32) * scale
            kg[a, b, 0] = first[:, tap % 2 * CH : (tap % 2 + 1) * CH]
            kg[a, b, 1] = later[:, :CH]
            kg[a, b, 2] = later[:, CH:]
        copies.append(pltpu.make_async_copy(kg.at[a], kg_hbm.at[a], sems.at[2 + a]))
        copies[-1].start()
    for copy in copies:
        copy.wait()


def body(features, cotangent, kernel, neighbours):
    count = lax.axis_size("space")
    dp_count = lax.axis_size("dp")
    reduce_here = count == 8 and dp_count == 2
    cells = features.shape[0] * features.shape[1] * dp_count * count * EDGE**3
    scale = 1.0 / math.sqrt(cells)
    bf16, f32 = jnp.bfloat16, jnp.float32
    planes = 2 * (EDGE + 2)
    rows = PAIRS * planes * EDGE
    dma = pltpu.SemaphoreType.DMA
    vmem = pl.BlockSpec(memory_space=pltpu.VMEM)
    hbm = pl.BlockSpec(memory_space=pltpu.HBM)
    part_shape = (TILES, CH, PAIR)
    response, feature_grad, tiles = pl.pallas_call(
        functools.partial(kernel_body, count, reduce_here),
        out_shape=(
            pltpu.VMEM(features.shape, bf16),
            pltpu.VMEM(features.shape, bf16),
            pltpu.VMEM(part_shape, bf16 if reduce_here else f32),
        ),
        in_specs=[hbm] * 4,
        out_specs=(vmem, vmem, vmem),
        scratch_shapes=[
            pltpu.SMEM(neighbours.shape, jnp.int32),
            pltpu.VMEM(features.shape, bf16),
            pltpu.VMEM(features.shape, bf16),
            pltpu.VMEM(kernel.shape, bf16),
            pltpu.VMEM((2, 2, EDGE, ROWS), bf16),
            pltpu.VMEM((2, 3, EDGE, ROWS), bf16),
            pltpu.VMEM((2, 2, EDGE, WIDE), bf16),
            pltpu.VMEM((2, 3, EDGE, WIDE), bf16),
            pltpu.VMEM((2, EDGE, ROWS), bf16),
            pltpu.VMEM((2, EDGE, WIDE), bf16),
            pltpu.VMEM((2, EDGE, EDGE, WIDE), bf16),
            pltpu.VMEM((rows, 12 * CH), bf16),
            pltpu.VMEM((rows, 12 * CH), bf16),
            pltpu.VMEM((6 * CH, rows), bf16),
            pltpu.VMEM((12 * CH, 6 * CH), bf16),
            pltpu.VMEM((6 * CH, 12 * CH), bf16),
            pltpu.VMEM(part_shape, f32),
            pltpu.VMEM((OWNED, CH, PAIR), f32),
            pltpu.VMEM((8, CH, PAIR), bf16),
            pltpu.VMEM((8, CH, PAIR), bf16),
            dma((4,)), dma((16,)), dma((16,)), dma((3,)), dma((3,)), dma((8,)), dma((8,)),
            dma((8,)), dma((8,)), dma((8,)), dma((8,)),
        ],
        compiler_params=pltpu.CompilerParams(
            collective_id=0, has_side_effects=True, vmem_limit_bytes=40 * 1024 * 1024
        ),
        cost_estimate=pl.CostEstimate(flops=10**9, bytes_accessed=2 * 10**6, transcendentals=0),
    )(*(
        pltpu.with_memory_space_constraint(x, pltpu.HBM)
        for x in (neighbours, features, cotangent, kernel)
    ))
    if not reduce_here:
        tiles = lax.psum(tiles, ("space", "dp"))
    return pl.pallas_call(
        functools.partial(finish_body, scale),
        out_shape=(
            jax.ShapeDtypeStruct(features.shape, bf16),
            jax.ShapeDtypeStruct(features.shape, bf16),
            jax.ShapeDtypeStruct(kernel.shape, f32),
        ),
        in_specs=[vmem] * 3,
        out_specs=(hbm,) * 3,
        scratch_shapes=[pltpu.VMEM(kernel.shape, f32), dma((5,))],
        cost_estimate=pl.CostEstimate(flops=10**6, bytes_accessed=10**6, transcendentals=0),
    )(*(
        pltpu.with_memory_space_constraint(x, pltpu.VMEM)
        for x in (response, feature_grad, tiles)
    ))


def solution(mesh):
    in_specs = (
        P(("groups", "dp"), "space", None, None, None),
        P(("groups", "dp"), "space", None, None, None),
        P(),
        P(("groups", "dp"), "space", None),
    )
    out_specs = (
        P(("groups", "dp"), "space", None, None, None),
        P(("groups", "dp"), "space", None, None, None),
        P("groups", None, None, None, None),
    )
    return jax.shard_map(body, mesh=mesh, in_specs=in_specs, out_specs=out_specs, check_vma=False)
```

```python
import functools
import math

import jax
import jax.numpy as jnp
from jax import lax
from jax.experimental import pallas as pl
from jax.experimental.pallas import tpu as pltpu
from jax.sharding import PartitionSpec as P

TILES_Y = 4
EDGE = 8
CH = 64
PAIR = 2 * CH
PAIRS = EDGE // 2
ROWS = EDGE * CH
WIDE = ROWS + PAIR
TILES = 14
OWNED = TILES // 2
MESH = pl.DeviceIdType.MESH
BATCHES = ((0, 2), (2, 4), (4, 7))
READY = (
    [("late", 0), ("late", 1), ("late", 2), ("early", 0)]
    + [("late", 3), ("late", 4), ("late", 5), ("early", 1)]
    + [("early", 2), ("late", 6), ("late", 7), ("late", 8), ("early", 3), ("early", 4)]
)
SPOT = {name: number % 2 * OWNED + number // 2 for number, name in enumerate(READY)}
DIAGONALS = [(side, dx) for side in range(2) for dx in range(3)]


def low_lanes(shape):
    return lax.broadcasted_iota(jnp.int32, shape, len(shape) - 1) < CH


def in_range(tile, count):
    return (tile >= 0) & (tile < count)


def receives(tile, dx, dy, count, first_x):
    column = (tile + TILES_Y // 2) % TILES_Y + dy
    there = in_range(tile + TILES_Y * dx + dy, count) & (column >= 0) & (column < TILES_Y)
    between = tile + TILES_Y * dx if first_x else tile + dy
    return in_range(tile, count) & in_range(between, count) & there


def window_builder(out_ref, center, edge, halo_low, halo_high, edge_low, edge_high):
    def shifted(values, low_row, high_row, tap):
        if tap == 0:
            return jnp.concatenate([low_row, values[:, :, : EDGE - 1]], axis=2)
        if tap == 2:
            return jnp.concatenate([values[:, :, 1:], high_row], axis=2)
        return values

    def build(tap):
        moved = shifted(center, halo_low, halo_high, tap)
        outer = shifted(edge, edge_low, edge_high, tap)
        low = low_lanes(outer.shape)
        pairs = [moved[..., PAIR * k : PAIR * (k + 1)] for k in range(PAIRS)]
        around = []
        for k in range(PAIRS):
            after = pairs[k + 1] if k + 1 < PAIRS else outer
            before = pairs[k - 1] if k > 0 else outer
            around.append(jnp.where(low, after, before))
        for half, pieces in enumerate((around, pairs)):
            rows = jnp.stack(pieces, axis=2).reshape(-1, PAIR).astype(jnp.bfloat16)
            base = (2 * tap + half) * PAIR
            out_ref[:, base : base + PAIR] = rows

    return build


def outer_rows(center, y_ref, width):
    sides = []
    for side in range(2):
        below = y_ref[side, 0].astype(jnp.float32)[EDGE - 1 :, None, :width]
        level = y_ref[side, 1].astype(jnp.float32)[:, None, :width]
        above = y_ref[side, 2].astype(jnp.float32)[:1, None, :width]
        sides.append(jnp.concatenate([below, level, above], axis=0))
    low = jnp.stack([sides[0], center[:, 0, EDGE - 1 :]], axis=1)
    high = jnp.stack([center[:, 1, :1], sides[1]], axis=1)
    return low, high


def sum_taps(result, store):
    step = 2 * PAIRS * EDGE
    count = EDGE * step
    total = result[:count, :PAIR]
    for a in range(1, 3):
        total = total + result[a * step : a * step + count, a * PAIR : (a + 1) * PAIR]
    total = total.reshape(EDGE, 2, PAIRS, EDGE, PAIR).astype(jnp.bfloat16)
    for brick in range(2):
        for k in range(PAIRS):
            store(brick, k, total[:, brick, k])


def turn(tile):
    turned = tile.T
    return jnp.concatenate([turned[:CH], turned[CH:]], axis=1)


def kernel_body(
    count, reduce_here,
    nb_hbm, f_hbm, c_hbm, w_hbm,
    resp_ref, fg_ref, tiles_ref,
    nb_ref, f_ref, c_ref, w_ref,
    fx, fy, cx, cy, fys, cys, cz, xw, cw, ct, wf, wg, part, core_in, sbuf, rbuf,
    load_sem, halo_send, halo_recv, core_send, core_recv, rs_send, rs_recv, ag_send, ag_recv, fw_send, fw_recv,
):
    me = lax.axis_index("space")
    core = lax.axis_index("dp")
    if reduce_here:
        fin = tiles_ref
    else:
        part = tiles_ref
    loads = [
        pltpu.make_async_copy(src, dst, load_sem.at[number])
        for number, (src, dst) in enumerate(
            [(f_hbm, f_ref), (c_hbm, c_ref), (nb_hbm, nb_ref), (w_hbm, w_ref)]
        )
    ]
    for load in loads:
        load.start()

    fx[...] = jnp.zeros_like(fx)
    fy[...] = jnp.zeros_like(fy)
    cx[...] = jnp.zeros_like(cx)
    cy[...] = jnp.zeros_like(cy)

    barrier = pltpu.get_barrier_semaphore()
    if reduce_here:
        for step in range(1, count):
            pl.semaphore_signal(
                barrier, inc=1, device_id={"space": (me + step) % count}, device_id_type=MESH
            )
        pl.semaphore_signal(barrier, inc=1, device_id={"dp": 1 - core}, device_id_type=MESH)
    else:
        for step in (1, 3, 4, 5):
            for other in (me + step, me - step):

                @pl.when(in_range(other, count))
                def _():
                    pl.semaphore_signal(
                        barrier, inc=1, device_id={"space": other}, device_id_type=MESH
                    )

    def halo(kind):
        x_ref, y_ref, ys_ref = ((fx, fy, fys), (cx, cy, cys))[kind]
        entries = []
        for side in range(2):
            dx = 2 * side - 1
            target = me - TILES_Y * dx
            face = EDGE - 1 if side == 0 else 0
            source = f_ref.at[0, :, face] if kind == 0 else cz.at[:, face]
            entries.append((
                receives(target, dx, 0, count, True),
                receives(me, dx, 0, count, True),
                source, x_ref.at[side], target,
            ))
        for side, column in DIAGONALS:
            dx, dy = column - 1, 2 * side - 1
            target = me - TILES_Y * dx - dy
            entries.append((
                receives(target, dx, dy, count, kind == 1),
                receives(me, dx, dy, count, kind == 1),
                ys_ref.at[side], y_ref.at[side, column], target,
            ))
        out = []
        for number, (sent, arrives, source, target_ref, target) in enumerate(entries):
            out.append((sent, arrives, pltpu.make_async_remote_copy(
                src_ref=source, dst_ref=target_ref,
                send_sem=halo_send.at[kind * 8 + number],
                recv_sem=halo_recv.at[kind * 8 + number],
                device_id={"space": target}, device_id_type=MESH,
            )))
        return out

    def start_halo(copies):
        for sent, _, copy in copies:
            pl.when(sent)(copy.start)

    def wait_halo(copies):
        for _, arrives, copy in copies:
            pl.when(arrives)(copy.wait_recv)

    loads[0].wait()
    fys[0] = f_ref[0, 1].astype(jnp.float32)[:, EDGE - 1].astype(jnp.bfloat16)
    fys[1] = f_ref[0, 0].astype(jnp.float32)[:, 0].astype(jnp.bfloat16)

    if reduce_here:
        pl.semaphore_wait(barrier, count)
    else:
        for step in (1, 3, 4, 5):
            for other in (me + step, me - step):

                @pl.when(in_range(other, count))
                def _():
                    pl.semaphore_wait(barrier, 1)

    f_copies, c_copies = halo(0), halo(1)
    start_halo(f_copies)

    loads[1].wait()
    loads[2].wait()
    for brick in range(2):
        other = 1 - brick
        before = jnp.where(nb_ref[0, brick, 4] >= 0, 1.0, 0.0)
        after = jnp.where(nb_ref[0, brick, 5] >= 0, 1.0, 0.0)
        cz[brick, :, :, :ROWS] = c_ref[0, brick]
        low = low_lanes((EDGE, EDGE, PAIR))
        edge = jnp.where(
            low,
            c_ref[0, other, :, :, :PAIR].astype(jnp.float32) * after,
            c_ref[0, other, :, :, ROWS - PAIR :].astype(jnp.float32) * before,
        )
        cz[brick, :, :, ROWS:] = edge.astype(jnp.bfloat16)
    cys[0] = cz[1].astype(jnp.float32)[:, EDGE - 1].astype(jnp.bfloat16)
    cys[1] = cz[0].astype(jnp.float32)[:, 0].astype(jnp.bfloat16)

    loads[3].wait()
    blank = jnp.zeros((CH, CH), jnp.bfloat16)
    for a in range(3):
        for b in range(3):
            taps = [w_ref[a, b, d] for d in range(3)]
            for w, slot in enumerate((1, 2, 3, 0)):
                left = taps[w] if w < 3 else blank
                right = taps[w - 1] if w > 0 else blank
                block = jnp.concatenate([left, right], axis=1)
                row = (b * 4 + slot) * CH
                wf[row : row + CH, a * PAIR : (a + 1) * PAIR] = block
                cell, half = ((1, 0), (0, 1), (1, 1), (0, 0))[w]
                row = (2 - a) * PAIR + cell * CH
                lane = (2 - b) * 4 * CH + half * PAIR
                wg[row : row + CH, lane : lane + PAIR] = block

    pieces = []
    for k in range(PAIRS):
        lanes = slice(k * PAIR, (k + 1) * PAIR)
        pieces.append(
            jnp.stack([c_ref[0, b, :, :, lanes].astype(jnp.float32) for b in range(2)], axis=1)
        )
    turned = jnp.stack(pieces, axis=2).reshape(-1, PAIR).T
    step = 2 * PAIRS * EDGE
    for a in range(3):
        padded = [jnp.zeros((PAIR, a * step), jnp.float32)] if a > 0 else []
        padded.append(turned)
        if a < 2:
            padded.append(jnp.zeros((PAIR, (2 - a) * step), jnp.float32))
        ct[a * PAIR : (a + 1) * PAIR] = jnp.concatenate(padded, axis=1).astype(jnp.bfloat16)

    wait_halo(f_copies)
    start_halo(c_copies)

    def stack(values, x_ref, width):
        first = x_ref[0].astype(jnp.float32)[None, ..., :width]
        last = x_ref[1].astype(jnp.float32)[None, ..., :width]
        return jnp.concatenate([first, jnp.stack(values, axis=1), last], axis=0)

    center = stack([f_ref[0, b].astype(jnp.float32) for b in range(2)], fx, ROWS)
    row_low, row_high = outer_rows(center, fy, ROWS)

    def third_edge(values):
        pieces = []
        for brick in range(2):
            other = values[:, 1 - brick]
            before = jnp.where(nb_ref[0, brick, 4] >= 0, 1.0, 0.0)
            after = jnp.where(nb_ref[0, brick, 5] >= 0, 1.0, 0.0)
            low = low_lanes(other.shape[:-1] + (PAIR,))
            pieces.append(
                jnp.where(low, other[..., :PAIR] * after, other[..., ROWS - PAIR :] * before)
            )
        return jnp.stack(pieces, axis=1)

    build_features = window_builder(
        xw, center, third_edge(center), row_low, row_high, third_edge(row_low), third_edge(row_high)
    )

    low = low_lanes((CH, PAIR))
    core_copies = [
        pltpu.make_async_remote_copy(
            src_ref=part.at[pl.ds((1 - core) * OWNED + first, last - first)],
            dst_ref=core_in.at[pl.ds(first, last - first)],
            send_sem=core_send.at[batch], recv_sem=core_recv.at[batch],
            device_id={"dp": 1 - core}, device_id_type=MESH,
        )
        for batch, (first, last) in enumerate(BATCHES)
    ] if reduce_here else []

    def scatter_copy(step):
        target = (me + step) % count
        return target, pltpu.make_async_remote_copy(
            src_ref=sbuf.at[target], dst_ref=rbuf.at[me],
            send_sem=rs_send.at[step], recv_sem=rs_recv.at[me],
            device_id={"space": target}, device_id_type=MESH,
        )

    def add_core(batch):
        core_copies[batch].wait_recv()
        for tile in range(*BATCHES[batch]):
            total = part[core * OWNED + tile] + core_in[tile]
            sbuf[tile] = total.astype(jnp.bfloat16)

    first_taps = []
    for b in range(3):
        build_features(b)
        grad = jnp.dot(
            ct[...], xw[:, b * 4 * CH : (b + 1) * 4 * CH], preferred_element_type=jnp.float32
        )
        for a in range(3):
            cell0 = grad[a * PAIR : a * PAIR + CH]
            cell1 = grad[a * PAIR + CH : (a + 1) * PAIR]
            turned0 = pltpu.roll(cell1[:, :PAIR], CH, 1)
            turned1 = pltpu.roll(cell1[:, PAIR:], CH, 1)
            tap = b * 3 + a
            part[SPOT["late", tap]] = cell0[:, PAIR:] + jnp.where(low, turned1, turned0)
            first_taps.append(cell0[:, :PAIR] + turned1)
            if tap % 2 == 1 or tap == 8:
                pair = first_taps[tap - tap % 2 :] + [jnp.zeros((CH, PAIR), jnp.float32)]
                part[SPOT["early", tap // 2]] = jnp.where(low, pltpu.roll(pair[0], CH, 1), pair[1])
        if reduce_here:
            core_copies[b].start()
            if b > 0:
                add_core(b - 1)

    if reduce_here:
        add_core(2)
        for step in range(1, count):
            target, copy = scatter_copy(step)
            pl.when(target < OWNED)(copy.start)

    result = jnp.dot(xw[...], wf[...], preferred_element_type=jnp.float32)

    def put_response(brick, k, value):
        resp_ref[0, brick, :, :, k * PAIR : (k + 1) * PAIR] = value

    sum_taps(result, put_response)

    wait_halo(c_copies)
    wide = stack([cz[b].astype(jnp.float32) for b in range(2)], cx, WIDE)
    wide_low, wide_high = outer_rows(wide, cy, WIDE)
    build_cotangent = window_builder(
        cw, wide[..., :ROWS], wide[..., ROWS:], wide_low[..., :ROWS], wide_high[..., :ROWS],
        wide_low[..., ROWS:], wide_high[..., ROWS:],
    )
    for tap in range(3):
        build_cotangent(tap)

    result = lax.dot_general(
        cw[...], wg[...], (((1,), (1,)), ((), ())), preferred_element_type=jnp.float32
    )

    def put_gradient(brick, k, value):
        fg_ref[0, brick, :, :, k * PAIR : (k + 1) * PAIR] = value

    sum_taps(result, put_gradient)

    if reduce_here:
        def gather_copy(step):
            target = (me + step) % count
            return pltpu.make_async_remote_copy(
                src_ref=fin.at[core * OWNED + me], dst_ref=fin.at[core * OWNED + me],
                send_sem=ag_send.at[step], recv_sem=ag_recv.at[me],
                device_id={"space": target}, device_id_type=MESH,
            )

        def forward_copy(tile):
            spot = fin.at[core * OWNED + tile]
            return pltpu.make_async_remote_copy(
                src_ref=spot, dst_ref=spot,
                send_sem=fw_send.at[tile], recv_sem=fw_recv.at[tile],
                device_id={"dp": 1 - core}, device_id_type=MESH,
            )

        @pl.when(me < OWNED)
        def _():
            total = sbuf[me].astype(jnp.float32)
            for step in range(1, count):
                source = (me + step) % count
                pltpu.make_async_remote_copy(
                    src_ref=sbuf.at[0], dst_ref=rbuf.at[source],
                    send_sem=rs_send.at[0], recv_sem=rs_recv.at[source],
                    device_id={"space": source}, device_id_type=MESH,
                ).wait_recv()
                total = total + rbuf[source].astype(jnp.float32)
            fin[core * OWNED + me] = turn(total).astype(jnp.bfloat16)
            for step in range(1, count):
                gather_copy(step).start()


    if reduce_here:
        for tile in range(OWNED):

            @pl.when(me != tile)
            def _():
                spot = fin.at[core * OWNED + tile]
                pltpu.make_async_remote_copy(
                    src_ref=spot, dst_ref=spot,
                    send_sem=ag_send.at[0], recv_sem=ag_recv.at[tile],
                    device_id={"space": tile}, device_id_type=MESH,
                ).wait_recv()

            forward_copy(tile).start()

        for tile in range(OWNED):
            spot = fin.at[(1 - core) * OWNED + tile]
            pltpu.make_async_remote_copy(
                src_ref=spot, dst_ref=spot,
                send_sem=fw_send.at[tile], recv_sem=fw_recv.at[tile],
                device_id={"dp": 1 - core}, device_id_type=MESH,
            ).wait_recv()
        for tile in range(OWNED):
            forward_copy(tile).wait_send()

        @pl.when(me < OWNED)
        def _():
            for step in range(1, count):
                gather_copy(step).wait_send()
    else:
        for tile in range(TILES):
            part[tile] = turn(part[tile])
    if reduce_here:
        for copy in core_copies:
            copy.wait_send()
        for step in range(1, count):
            target, copy = scatter_copy(step)
            pl.when(target < OWNED)(copy.wait_send)
    for sent, _, copy in f_copies + c_copies:
        pl.when(sent)(copy.wait_send)


def finish_body(scale, resp_ref, fg_ref, tiles_ref, resp_hbm, fg_hbm, kg_hbm, kg, sems):
    copies = [
        pltpu.make_async_copy(resp_ref, resp_hbm, sems.at[0]),
        pltpu.make_async_copy(fg_ref, fg_hbm, sems.at[1]),
    ]
    for copy in copies:
        copy.start()
    for a in range(3):
        for b in range(3):
            tap = b * 3 + a
            later = tiles_ref[SPOT["late", tap]].astype(jnp.float32) * scale
            first = tiles_ref[SPOT["early", tap // 2]].astype(jnp.float32) * scale
            kg[a, b, 0] = first[:, tap % 2 * CH : (tap % 2 + 1) * CH]
            kg[a, b, 1] = later[:, :CH]
            kg[a, b, 2] = later[:, CH:]
        copies.append(pltpu.make_async_copy(kg.at[a], kg_hbm.at[a], sems.at[2 + a]))
        copies[-1].start()
    for copy in copies:
        copy.wait()


def body(features, cotangent, kernel, neighbours):
    count = lax.axis_size("space")
    dp_count = lax.axis_size("dp")
    reduce_here = count == 8 and dp_count == 2
    cells = features.shape[0] * features.shape[1] * dp_count * count * EDGE**3
    scale = 1.0 / math.sqrt(cells)
    bf16, f32 = jnp.bfloat16, jnp.float32
    planes = 2 * (EDGE + 2)
    rows = PAIRS * planes * EDGE
    dma = pltpu.SemaphoreType.DMA
    vmem = pl.BlockSpec(memory_space=pltpu.VMEM)
    hbm = pl.BlockSpec(memory_space=pltpu.HBM)
    part_shape = (TILES, CH, PAIR)
    response, feature_grad, tiles = pl.pallas_call(
        functools.partial(kernel_body, count, reduce_here),
        out_shape=(
            pltpu.VMEM(features.shape, bf16),
            pltpu.VMEM(features.shape, bf16),
            pltpu.VMEM(part_shape, bf16 if reduce_here else f32),
        ),
        in_specs=[hbm] * 4,
        out_specs=(vmem, vmem, vmem),
        scratch_shapes=[
            pltpu.SMEM(neighbours.shape, jnp.int32),
            pltpu.VMEM(features.shape, bf16),
            pltpu.VMEM(features.shape, bf16),
            pltpu.VMEM(kernel.shape, bf16),
            pltpu.VMEM((2, 2, EDGE, ROWS), bf16),
            pltpu.VMEM((2, 3, EDGE, ROWS), bf16),
            pltpu.VMEM((2, 2, EDGE, WIDE), bf16),
            pltpu.VMEM((2, 3, EDGE, WIDE), bf16),
            pltpu.VMEM((2, EDGE, ROWS), bf16),
            pltpu.VMEM((2, EDGE, WIDE), bf16),
            pltpu.VMEM((2, EDGE, EDGE, WIDE), bf16),
            pltpu.VMEM((rows, 12 * CH), bf16),
            pltpu.VMEM((rows, 12 * CH), bf16),
            pltpu.VMEM((6 * CH, rows), bf16),
            pltpu.VMEM((12 * CH, 6 * CH), bf16),
            pltpu.VMEM((6 * CH, 12 * CH), bf16),
            pltpu.VMEM(part_shape, f32),
            pltpu.VMEM((OWNED, CH, PAIR), f32),
            pltpu.VMEM((8, CH, PAIR), bf16),
            pltpu.VMEM((8, CH, PAIR), bf16),
            dma((4,)), dma((16,)), dma((16,)), dma((3,)), dma((3,)), dma((8,)), dma((8,)),
            dma((8,)), dma((8,)), dma((8,)), dma((8,)),
        ],
        compiler_params=pltpu.CompilerParams(
            collective_id=0, has_side_effects=True, vmem_limit_bytes=40 * 1024 * 1024
        ),
        cost_estimate=pl.CostEstimate(flops=10**9, bytes_accessed=2 * 10**6, transcendentals=0),
    )(*(
        pltpu.with_memory_space_constraint(x, pltpu.HBM)
        for x in (neighbours, features, cotangent, kernel)
    ))
    if not reduce_here:
        tiles = lax.psum(tiles, ("space", "dp"))
    return pl.pallas_call(
        functools.partial(finish_body, scale),
        out_shape=(
            jax.ShapeDtypeStruct(features.shape, bf16),
            jax.ShapeDtypeStruct(features.shape, bf16),
            jax.ShapeDtypeStruct(kernel.shape, f32),
        ),
        in_specs=[vmem] * 3,
        out_specs=(hbm,) * 3,
        scratch_shapes=[pltpu.VMEM(kernel.shape, f32), dma((5,))],
        cost_estimate=pl.CostEstimate(flops=10**6, bytes_accessed=10**6, transcendentals=0),
    )(*(
        pltpu.with_memory_space_constraint(x, pltpu.VMEM)
        for x in (response, feature_grad, tiles)
    ))


def solution(mesh):
    in_specs = (
        P(("groups", "dp"), "space", None, None, None),
        P(("groups", "dp"), "space", None, None, None),
        P(),
        P(("groups", "dp"), "space", None),
    )
    out_specs = (
        P(("groups", "dp"), "space", None, None, None),
        P(("groups", "dp"), "space", None, None, None),
        P("groups", None, None, None, None),
    )
    return jax.shard_map(body, mesh=mesh, in_specs=in_specs, out_specs=out_specs, check_vma=False)
```

```python
import functools
import math

import jax
import jax.numpy as jnp
from jax import lax
from jax.experimental import pallas as pl
from jax.experimental.pallas import tpu as pltpu
from jax.sharding import PartitionSpec as P

TILES_Y = 4
EDGE = 8
CH = 64
PAIR = 2 * CH
PAIRS = EDGE // 2
ROWS = EDGE * CH
WIDE = ROWS + PAIR
TILES = 14
OWNED = TILES // 2
MESH = pl.DeviceIdType.MESH
BATCHES = ((0, 2), (2, 4), (4, 7))
READY = (
    [("late", 0), ("late", 1), ("late", 2), ("early", 0)]
    + [("late", 3), ("late", 4), ("late", 5), ("early", 1)]
    + [("early", 2), ("late", 6), ("late", 7), ("late", 8), ("early", 3), ("early", 4)]
)
SPOT = {name: number % 2 * OWNED + number // 2 for number, name in enumerate(READY)}
DIAGONALS = [(side, dx) for side in range(2) for dx in range(3)]


def low_lanes(shape):
    return lax.broadcasted_iota(jnp.int32, shape, len(shape) - 1) < CH


def in_range(tile, count):
    return (tile >= 0) & (tile < count)


def receives(tile, dx, dy, count, first_x):
    column = (tile + TILES_Y // 2) % TILES_Y + dy
    there = in_range(tile + TILES_Y * dx + dy, count) & (column >= 0) & (column < TILES_Y)
    between = tile + TILES_Y * dx if first_x else tile + dy
    return in_range(tile, count) & in_range(between, count) & there


def window_builder(out_ref, center, edge, halo_low, halo_high, edge_low, edge_high):
    def shifted(values, low_row, high_row, tap):
        if tap == 0:
            return jnp.concatenate([low_row, values[:, :, : EDGE - 1]], axis=2)
        if tap == 2:
            return jnp.concatenate([values[:, :, 1:], high_row], axis=2)
        return values

    def build(tap):
        moved = shifted(center, halo_low, halo_high, tap)
        outer = shifted(edge, edge_low, edge_high, tap)
        low = low_lanes(outer.shape)
        pairs = [moved[..., PAIR * k : PAIR * (k + 1)] for k in range(PAIRS)]
        around = []
        for k in range(PAIRS):
            after = pairs[k + 1] if k + 1 < PAIRS else outer
            before = pairs[k - 1] if k > 0 else outer
            around.append(jnp.where(low, after, before))
        for half, pieces in enumerate((around, pairs)):
            rows = jnp.stack(pieces, axis=2).reshape(-1, PAIR).astype(jnp.bfloat16)
            base = (2 * tap + half) * PAIR
            out_ref[:, base : base + PAIR] = rows

    return build


def outer_rows(center, y_ref, width):
    sides = []
    for side in range(2):
        below = y_ref[side, 0].astype(jnp.float32)[EDGE - 1 :, None, :width]
        level = y_ref[side, 1].astype(jnp.float32)[:, None, :width]
        above = y_ref[side, 2].astype(jnp.float32)[:1, None, :width]
        sides.append(jnp.concatenate([below, level, above], axis=0))
    low = jnp.stack([sides[0], center[:, 0, EDGE - 1 :]], axis=1)
    high = jnp.stack([center[:, 1, :1], sides[1]], axis=1)
    return low, high


def sum_taps(result, store):
    step = 2 * PAIRS * EDGE
    count = EDGE * step
    total = result[:count, :PAIR]
    for a in range(1, 3):
        total = total + result[a * step : a * step + count, a * PAIR : (a + 1) * PAIR]
    total = total.reshape(EDGE, 2, PAIRS, EDGE, PAIR).astype(jnp.bfloat16)
    for brick in range(2):
        for k in range(PAIRS):
            store(brick, k, total[:, brick, k])


def turn(tile):
    turned = tile.T
    return jnp.concatenate([turned[:CH], turned[CH:]], axis=1)


def kernel_body(
    count, reduce_here,
    nb_hbm, f_hbm, c_hbm, w_hbm,
    resp_ref, fg_ref, tiles_ref,
    nb_ref, f_ref, c_ref, w_ref,
    fx, fy, cx, cy, fys, cys, cz, xw, cw, ct, wf, wg, part, core_in, sbuf, rbuf,
    load_sem, halo_send, halo_recv, core_send, core_recv, rs_send, rs_recv, ag_send, ag_recv, fw_send, fw_recv,
):
    me = lax.axis_index("space")
    core = lax.axis_index("dp")
    if reduce_here:
        fin = tiles_ref
    else:
        part = tiles_ref
    loads = [
        pltpu.make_async_copy(src, dst, load_sem.at[number])
        for number, (src, dst) in enumerate(
            [(f_hbm, f_ref), (c_hbm, c_ref), (nb_hbm, nb_ref), (w_hbm, w_ref)]
        )
    ]
    for load in loads:
        load.start()

    fx[...] = jnp.zeros_like(fx)
    fy[...] = jnp.zeros_like(fy)
    cx[...] = jnp.zeros_like(cx)
    cy[...] = jnp.zeros_like(cy)

    barrier = pltpu.get_barrier_semaphore()
    if reduce_here:
        for step in range(1, count):
            pl.semaphore_signal(
                barrier, inc=1, device_id={"space": (me + step) % count}, device_id_type=MESH
            )
        pl.semaphore_signal(barrier, inc=1, device_id={"dp": 1 - core}, device_id_type=MESH)
    else:
        for step in (1, 3, 4, 5):
            for other in (me + step, me - step):

                @pl.when(in_range(other, count))
                def _():
                    pl.semaphore_signal(
                        barrier, inc=1, device_id={"space": other}, device_id_type=MESH
                    )

    def halo(kind):
        x_ref, y_ref, ys_ref = ((fx, fy, fys), (cx, cy, cys))[kind]
        entries = []
        for side in range(2):
            dx = 2 * side - 1
            target = me - TILES_Y * dx
            face = EDGE - 1 if side == 0 else 0
            source = f_ref.at[0, :, face] if kind == 0 else cz.at[:, face]
            entries.append((
                receives(target, dx, 0, count, True),
                receives(me, dx, 0, count, True),
                source, x_ref.at[side], target,
            ))
        for side, column in DIAGONALS:
            dx, dy = column - 1, 2 * side - 1
            target = me - TILES_Y * dx - dy
            entries.append((
                receives(target, dx, dy, count, kind == 1),
                receives(me, dx, dy, count, kind == 1),
                ys_ref.at[side], y_ref.at[side, column], target,
            ))
        out = []
        for number, (sent, arrives, source, target_ref, target) in enumerate(entries):
            out.append((sent, arrives, pltpu.make_async_remote_copy(
                src_ref=source, dst_ref=target_ref,
                send_sem=halo_send.at[kind * 8 + number],
                recv_sem=halo_recv.at[kind * 8 + number],
                device_id={"space": target}, device_id_type=MESH,
            )))
        return out

    def start_halo(copies):
        for sent, _, copy in copies:
            pl.when(sent)(copy.start)

    def wait_halo(copies):
        for _, arrives, copy in copies:
            pl.when(arrives)(copy.wait_recv)

    loads[0].wait()
    fys[0] = f_ref[0, 1].astype(jnp.float32)[:, EDGE - 1].astype(jnp.bfloat16)
    fys[1] = f_ref[0, 0].astype(jnp.float32)[:, 0].astype(jnp.bfloat16)

    if reduce_here:
        pl.semaphore_wait(barrier, count)
    else:
        for step in (1, 3, 4, 5):
            for other in (me + step, me - step):

                @pl.when(in_range(other, count))
                def _():
                    pl.semaphore_wait(barrier, 1)

    f_copies, c_copies = halo(0), halo(1)
    start_halo(f_copies)

    loads[1].wait()
    loads[2].wait()
    for brick in range(2):
        other = 1 - brick
        before = jnp.where(nb_ref[0, brick, 4] >= 0, 1.0, 0.0)
        after = jnp.where(nb_ref[0, brick, 5] >= 0, 1.0, 0.0)
        cz[brick, :, :, :ROWS] = c_ref[0, brick]
        low = low_lanes((EDGE, EDGE, PAIR))
        edge = jnp.where(
            low,
            c_ref[0, other, :, :, :PAIR].astype(jnp.float32) * after,
            c_ref[0, other, :, :, ROWS - PAIR :].astype(jnp.float32) * before,
        )
        cz[brick, :, :, ROWS:] = edge.astype(jnp.bfloat16)
    cys[0] = cz[1].astype(jnp.float32)[:, EDGE - 1].astype(jnp.bfloat16)
    cys[1] = cz[0].astype(jnp.float32)[:, 0].astype(jnp.bfloat16)

    loads[3].wait()
    blank = jnp.zeros((CH, CH), jnp.bfloat16)
    for a in range(3):
        for b in range(3):
            taps = [w_ref[a, b, d] for d in range(3)]
            for w, slot in enumerate((1, 2, 3, 0)):
                left = taps[w] if w < 3 else blank
                right = taps[w - 1] if w > 0 else blank
                block = jnp.concatenate([left, right], axis=1)
                row = (b * 4 + slot) * CH
                wf[row : row + CH, a * PAIR : (a + 1) * PAIR] = block
                cell, half = ((1, 0), (0, 1), (1, 1), (0, 0))[w]
                row = (2 - a) * PAIR + cell * CH
                lane = (2 - b) * 4 * CH + half * PAIR
                wg[row : row + CH, lane : lane + PAIR] = block

    pieces = []
    for k in range(PAIRS):
        lanes = slice(k * PAIR, (k + 1) * PAIR)
        pieces.append(
            jnp.stack([c_ref[0, b, :, :, lanes].astype(jnp.float32) for b in range(2)], axis=1)
        )
    turned = jnp.stack(pieces, axis=2).reshape(-1, PAIR).T
    step = 2 * PAIRS * EDGE
    for a in range(3):
        padded = [jnp.zeros((PAIR, a * step), jnp.float32)] if a > 0 else []
        padded.append(turned)
        if a < 2:
            padded.append(jnp.zeros((PAIR, (2 - a) * step), jnp.float32))
        ct[a * PAIR : (a + 1) * PAIR] = jnp.concatenate(padded, axis=1).astype(jnp.bfloat16)

    wait_halo(f_copies)
    start_halo(c_copies)

    def stack(values, x_ref, width):
        first = x_ref[0].astype(jnp.float32)[None, ..., :width]
        last = x_ref[1].astype(jnp.float32)[None, ..., :width]
        return jnp.concatenate([first, jnp.stack(values, axis=1), last], axis=0)

    center = stack([f_ref[0, b].astype(jnp.float32) for b in range(2)], fx, ROWS)
    row_low, row_high = outer_rows(center, fy, ROWS)

    def third_edge(values):
        pieces = []
        for brick in range(2):
            other = values[:, 1 - brick]
            before = jnp.where(nb_ref[0, brick, 4] >= 0, 1.0, 0.0)
            after = jnp.where(nb_ref[0, brick, 5] >= 0, 1.0, 0.0)
            low = low_lanes(other.shape[:-1] + (PAIR,))
            pieces.append(
                jnp.where(low, other[..., :PAIR] * after, other[..., ROWS - PAIR :] * before)
            )
        return jnp.stack(pieces, axis=1)

    build_features = window_builder(
        xw, center, third_edge(center), row_low, row_high, third_edge(row_low), third_edge(row_high)
    )

    low = low_lanes((CH, PAIR))
    core_copies = [
        pltpu.make_async_remote_copy(
            src_ref=part.at[pl.ds((1 - core) * OWNED + first, last - first)],
            dst_ref=core_in.at[pl.ds(first, last - first)],
            send_sem=core_send.at[batch], recv_sem=core_recv.at[batch],
            device_id={"dp": 1 - core}, device_id_type=MESH,
        )
        for batch, (first, last) in enumerate(BATCHES)
    ] if reduce_here else []

    def scatter_copy(step):
        target = (me + step) % count
        return target, pltpu.make_async_remote_copy(
            src_ref=sbuf.at[target], dst_ref=rbuf.at[me],
            send_sem=rs_send.at[step], recv_sem=rs_recv.at[me],
            device_id={"space": target}, device_id_type=MESH,
        )

    def scatter(first, last):
        for step in range(1, count):
            target, copy = scatter_copy(step)
            pl.when((target >= first) & (target < last))(copy.start)

    def add_core(batch):
        core_copies[batch].wait_recv()
        for tile in range(*BATCHES[batch]):
            total = part[core * OWNED + tile] + core_in[tile]
            sbuf[tile] = total.astype(jnp.bfloat16)

    first_taps = []
    for b in range(3):
        build_features(b)
        grad = jnp.dot(
            ct[...], xw[:, b * 4 * CH : (b + 1) * 4 * CH], preferred_element_type=jnp.float32
        )
        for a in range(3):
            cell0 = grad[a * PAIR : a * PAIR + CH]
            cell1 = grad[a * PAIR + CH : (a + 1) * PAIR]
            turned0 = pltpu.roll(cell1[:, :PAIR], CH, 1)
            turned1 = pltpu.roll(cell1[:, PAIR:], CH, 1)
            tap = b * 3 + a
            part[SPOT["late", tap]] = cell0[:, PAIR:] + jnp.where(low, turned1, turned0)
            first_taps.append(cell0[:, :PAIR] + turned1)
            if tap % 2 == 1 or tap == 8:
                pair = first_taps[tap - tap % 2 :] + [jnp.zeros((CH, PAIR), jnp.float32)]
                part[SPOT["early", tap // 2]] = jnp.where(low, pltpu.roll(pair[0], CH, 1), pair[1])
        if reduce_here:
            core_copies[b].start()
            if b > 0:
                add_core(b - 1)
    if reduce_here:
        scatter(0, BATCHES[1][1])

    if reduce_here:
        add_core(2)
        scatter(BATCHES[1][1], OWNED)

    result = jnp.dot(xw[...], wf[...], preferred_element_type=jnp.float32)

    def put_response(brick, k, value):
        resp_ref[0, brick, :, :, k * PAIR : (k + 1) * PAIR] = value

    sum_taps(result, put_response)

    wait_halo(c_copies)
    wide = stack([cz[b].astype(jnp.float32) for b in range(2)], cx, WIDE)
    wide_low, wide_high = outer_rows(wide, cy, WIDE)
    build_cotangent = window_builder(
        cw, wide[..., :ROWS], wide[..., ROWS:], wide_low[..., :ROWS], wide_high[..., :ROWS],
        wide_low[..., ROWS:], wide_high[..., ROWS:],
    )
    for tap in range(3):
        build_cotangent(tap)

    result = lax.dot_general(
        cw[...], wg[...], (((1,), (1,)), ((), ())), preferred_element_type=jnp.float32
    )

    def put_gradient(brick, k, value):
        fg_ref[0, brick, :, :, k * PAIR : (k + 1) * PAIR] = value

    sum_taps(result, put_gradient)

    if reduce_here:
        def gather_copy(step):
            target = (me + step) % count
            return pltpu.make_async_remote_copy(
                src_ref=fin.at[core * OWNED + me], dst_ref=fin.at[core * OWNED + me],
                send_sem=ag_send.at[step], recv_sem=ag_recv.at[me],
                device_id={"space": target}, device_id_type=MESH,
            )

        def forward_copy(tile):
            spot = fin.at[core * OWNED + tile]
            return pltpu.make_async_remote_copy(
                src_ref=spot, dst_ref=spot,
                send_sem=fw_send.at[tile], recv_sem=fw_recv.at[tile],
                device_id={"dp": 1 - core}, device_id_type=MESH,
            )

        @pl.when(me < OWNED)
        def _():
            total = sbuf[me].astype(jnp.float32)
            for step in range(1, count):
                source = (me + step) % count
                pltpu.make_async_remote_copy(
                    src_ref=sbuf.at[0], dst_ref=rbuf.at[source],
                    send_sem=rs_send.at[0], recv_sem=rs_recv.at[source],
                    device_id={"space": source}, device_id_type=MESH,
                ).wait_recv()
                total = total + rbuf[source].astype(jnp.float32)
            fin[core * OWNED + me] = turn(total).astype(jnp.bfloat16)
            for step in range(1, count):
                gather_copy(step).start()


    if reduce_here:
        for tile in range(OWNED):

            @pl.when(me != tile)
            def _():
                spot = fin.at[core * OWNED + tile]
                pltpu.make_async_remote_copy(
                    src_ref=spot, dst_ref=spot,
                    send_sem=ag_send.at[0], recv_sem=ag_recv.at[tile],
                    device_id={"space": tile}, device_id_type=MESH,
                ).wait_recv()

            forward_copy(tile).start()

        for tile in range(OWNED):
            spot = fin.at[(1 - core) * OWNED + tile]
            pltpu.make_async_remote_copy(
                src_ref=spot, dst_ref=spot,
                send_sem=fw_send.at[tile], recv_sem=fw_recv.at[tile],
                device_id={"dp": 1 - core}, device_id_type=MESH,
            ).wait_recv()
        for tile in range(OWNED):
            forward_copy(tile).wait_send()

        @pl.when(me < OWNED)
        def _():
            for step in range(1, count):
                gather_copy(step).wait_send()
    else:
        for tile in range(TILES):
            part[tile] = turn(part[tile])
    if reduce_here:
        for copy in core_copies:
            copy.wait_send()
        for step in range(1, count):
            target, copy = scatter_copy(step)
            pl.when(target < OWNED)(copy.wait_send)
    for sent, _, copy in f_copies + c_copies:
        pl.when(sent)(copy.wait_send)


def finish_body(scale, resp_ref, fg_ref, tiles_ref, resp_hbm, fg_hbm, kg_hbm, kg, sems):
    copies = [
        pltpu.make_async_copy(resp_ref, resp_hbm, sems.at[0]),
        pltpu.make_async_copy(fg_ref, fg_hbm, sems.at[1]),
    ]
    for copy in copies:
        copy.start()
    for a in range(3):
        for b in range(3):
            tap = b * 3 + a
            later = tiles_ref[SPOT["late", tap]].astype(jnp.float32) * scale
            first = tiles_ref[SPOT["early", tap // 2]].astype(jnp.float32) * scale
            kg[a, b, 0] = first[:, tap % 2 * CH : (tap % 2 + 1) * CH]
            kg[a, b, 1] = later[:, :CH]
            kg[a, b, 2] = later[:, CH:]
        copies.append(pltpu.make_async_copy(kg.at[a], kg_hbm.at[a], sems.at[2 + a]))
        copies[-1].start()
    for copy in copies:
        copy.wait()


def body(features, cotangent, kernel, neighbours):
    count = lax.axis_size("space")
    dp_count = lax.axis_size("dp")
    reduce_here = count == 8 and dp_count == 2
    cells = features.shape[0] * features.shape[1] * dp_count * count * EDGE**3
    scale = 1.0 / math.sqrt(cells)
    bf16, f32 = jnp.bfloat16, jnp.float32
    planes = 2 * (EDGE + 2)
    rows = PAIRS * planes * EDGE
    dma = pltpu.SemaphoreType.DMA
    vmem = pl.BlockSpec(memory_space=pltpu.VMEM)
    hbm = pl.BlockSpec(memory_space=pltpu.HBM)
    part_shape = (TILES, CH, PAIR)
    response, feature_grad, tiles = pl.pallas_call(
        functools.partial(kernel_body, count, reduce_here),
        out_shape=(
            pltpu.VMEM(features.shape, bf16),
            pltpu.VMEM(features.shape, bf16),
            pltpu.VMEM(part_shape, bf16 if reduce_here else f32),
        ),
        in_specs=[hbm] * 4,
        out_specs=(vmem, vmem, vmem),
        scratch_shapes=[
            pltpu.SMEM(neighbours.shape, jnp.int32),
            pltpu.VMEM(features.shape, bf16),
            pltpu.VMEM(features.shape, bf16),
            pltpu.VMEM(kernel.shape, bf16),
            pltpu.VMEM((2, 2, EDGE, ROWS), bf16),
            pltpu.VMEM((2, 3, EDGE, ROWS), bf16),
            pltpu.VMEM((2, 2, EDGE, WIDE), bf16),
            pltpu.VMEM((2, 3, EDGE, WIDE), bf16),
            pltpu.VMEM((2, EDGE, ROWS), bf16),
            pltpu.VMEM((2, EDGE, WIDE), bf16),
            pltpu.VMEM((2, EDGE, EDGE, WIDE), bf16),
            pltpu.VMEM((rows, 12 * CH), bf16),
            pltpu.VMEM((rows, 12 * CH), bf16),
            pltpu.VMEM((6 * CH, rows), bf16),
            pltpu.VMEM((12 * CH, 6 * CH), bf16),
            pltpu.VMEM((6 * CH, 12 * CH), bf16),
            pltpu.VMEM(part_shape, f32),
            pltpu.VMEM((OWNED, CH, PAIR), f32),
            pltpu.VMEM((8, CH, PAIR), bf16),
            pltpu.VMEM((8, CH, PAIR), bf16),
            dma((4,)), dma((16,)), dma((16,)), dma((3,)), dma((3,)), dma((8,)), dma((8,)),
            dma((8,)), dma((8,)), dma((8,)), dma((8,)),
        ],
        compiler_params=pltpu.CompilerParams(
            collective_id=0, has_side_effects=True, vmem_limit_bytes=40 * 1024 * 1024
        ),
        cost_estimate=pl.CostEstimate(flops=10**9, bytes_accessed=2 * 10**6, transcendentals=0),
    )(*(
        pltpu.with_memory_space_constraint(x, pltpu.HBM)
        for x in (neighbours, features, cotangent, kernel)
    ))
    if not reduce_here:
        tiles = lax.psum(tiles, ("space", "dp"))
    return pl.pallas_call(
        functools.partial(finish_body, scale),
        out_shape=(
            jax.ShapeDtypeStruct(features.shape, bf16),
            jax.ShapeDtypeStruct(features.shape, bf16),
            jax.ShapeDtypeStruct(kernel.shape, f32),
        ),
        in_specs=[vmem] * 3,
        out_specs=(hbm,) * 3,
        scratch_shapes=[pltpu.VMEM(kernel.shape, f32), dma((5,))],
        cost_estimate=pl.CostEstimate(flops=10**6, bytes_accessed=10**6, transcendentals=0),
    )(*(
        pltpu.with_memory_space_constraint(x, pltpu.VMEM)
        for x in (response, feature_grad, tiles)
    ))


def solution(mesh):
    in_specs = (
        P(("groups", "dp"), "space", None, None, None),
        P(("groups", "dp"), "space", None, None, None),
        P(),
        P(("groups", "dp"), "space", None),
    )
    out_specs = (
        P(("groups", "dp"), "space", None, None, None),
        P(("groups", "dp"), "space", None, None, None),
        P("groups", None, None, None, None),
    )
    return jax.shard_map(body, mesh=mesh, in_specs=in_specs, out_specs=out_specs, check_vma=False)
```
